256 devices in a mesh: src: 16 (over z, core), win: 4 (over y), ccd: 4 (over x).
Axes of the slice: x: 4, y: 4, z: 8, core: 2. Of those that a mesh axis runs over, the one named last changes fastest.
Arguments:
- block_bin: int32 [32768], P(('src', 'win', 'ccd')), may hold values from 0 to 7999, as said below
- block_rows: int32 [32768], P(('src', 'win', 'ccd')), may hold values from 16 to 128
- row_source: int32 [32768, 128], P(('src', 'win', 'ccd')), may hold values from 0 to 4095
- obs_resid: float32 [32768, 128], P(('src', 'win', 'ccd')), may hold values from -6 to 6
- obs_phase: float32 [32768, 128], P(('src', 'win', 'ccd')), may hold values from 0 to 1
- att_partial: float32 [32768, 4, 128], P(('src', 'win', 'ccd')), may hold values from -6 to 6
- src_partial: float32 [32768, 5, 128], P(('src', 'win', 'ccd')), may hold values from -6 to 6
Outputs:
- attitude_delta: float32 [64, 4, 128], P(('src', 'win'))
- source_delta: float32 [5, 262144], P(None, ('src', 'win'))
The draws below stay inside these ranges and needn't reach their ends.
Inputs may be any that keep to these rules, and one draw needn't show every extreme that they name: Of the 128 blocks of one device, at most 4 fall in one window (block_bin // 125); in every draw some window receives exactly 4 blocks from every device, and every window receives blocks from some device.
All inputs are finite; a program needn't handle non-finite values.
Results may differ from the reference program's by a relative error of at most 0.029.
Values sent between devices are 32-bit elements; how exact they have to be, the bound alone decides.
No kernel may reach another device: no remote copies, remote signals or barrier semaphores. Data moves between devices by JAX's collectives and lax.ppermute only.
A program may use at most 64 MiB of HBM per device.

```python
import jax
import jax.numpy as jnp
from jax import lax

KNOTS_W = 128
NBLK = 128
SRC_DEV = 4096
BLOCK_LEN = 128
ITERS = 8
WINDOWS = 64
CAP = 4
BINS_W = 125
BLOCKS = 32768
N_SRC = 16
N_WIN = 4
N_CCD = 4
DEVICES = 256


def draw_block_bin(key, part):
    slot_total = WINDOWS * CAP
    key_dense, key_busy, key_order, key_local = jax.random.split(key, 4)
    density = jax.random.randint(key_dense, (WINDOWS,), 0, 4)
    busiest = jax.random.randint(key_busy, (), 0, WINDOWS)
    slot_window = jnp.arange(slot_total, dtype=jnp.int32) // CAP
    device_window = jnp.arange(DEVICES, dtype=jnp.int32) % WINDOWS
    priority = jax.random.randint(key_order, (DEVICES, slot_total), 0, 1 << 14)
    priority = priority + density[slot_window][None, :] * (1 << 12)
    priority = priority + jnp.where(slot_window == busiest, 1 << 17, 0)[None, :]
    priority = priority + jnp.where(slot_window[None, :] == device_window[:, None], 1 << 16, 0)
    scores = priority * slot_total + jnp.arange(slot_total, dtype=jnp.int32)[None, :]
    ordered = jnp.argsort(-scores, axis=1, stable=True)
    chosen = ordered[:, :NBLK]
    window_of = chosen // CAP
    local_bin = jax.random.randint(key_local, (DEVICES, NBLK), 0, BINS_W)
    return (window_of * BINS_W + local_bin).reshape(-1).astype(jnp.int32)


def touch_ends(values, key, smallest, top_value):
    shape = values.shape
    place = [jax.random.randint(jax.random.fold_in(key, axis), (), 0, shape[axis]) for axis in range(len(shape))]
    values = values.at[tuple(place)].set(smallest)
    longest = shape.index(max(shape))
    place[longest] = (place[longest] + 1) % shape[longest]
    return values.at[tuple(place)].set(top_value)


def shard_levels(key, shape, cuts, least, largest):
    def one(axis_at, blocks):
        heights = jax.random.uniform(jax.random.fold_in(jax.random.fold_in(key, 6), axis_at), (blocks,), jnp.float32, least / len(cuts), largest / len(cuts))
        return jnp.repeat(jnp.exp(heights), shape[axis_at] // blocks).reshape((-1,) + (1,) * (len(shape) - axis_at - 1))

    loudness = one(*cuts[0])
    for cut in cuts[1:]:
        loudness = loudness * one(*cut)
    return loudness


def gaussian(key, dims, deviation, reach, shards=(), kind=jnp.bfloat16):
    factor_of = shard_levels(key, dims, shards, -0.22, 0.18) if shards else 1.0
    drawn = jax.random.normal(key, dims, jnp.float32) * deviation * factor_of
    return jnp.minimum(jnp.maximum(drawn, -reach), reach).astype(kind)


def setup_inputs(seed: int = 0) -> dict:
    keys = jax.random.split(jax.random.key(seed), 8)
    block_bin = draw_block_bin(jax.random.fold_in(keys[7], 71), 0)
    block_rows = touch_ends(jax.random.randint(keys[1], (BLOCKS,), 16, BLOCK_LEN + 1), jax.random.fold_in(keys[1], 1), 16, BLOCK_LEN).astype(jnp.int32)
    row_source = touch_ends(jax.random.randint(keys[2], (BLOCKS, BLOCK_LEN), 0, SRC_DEV), jax.random.fold_in(keys[2], 1), 0, SRC_DEV - 1).astype(jnp.int32)
    obs_resid = gaussian(keys[3], (BLOCKS, BLOCK_LEN), 1.0, 6.0, ((0, 256),), jnp.float32)
    obs_phase = jnp.clip(1.0 * jax.random.uniform(keys[4], (BLOCKS, BLOCK_LEN), jnp.float32) ** shard_levels(keys[4], (BLOCKS, BLOCK_LEN), ((0, 256),), -0.2, 0.2), 0.0, 1.0)
    att_partial = gaussian(keys[5], (BLOCKS, 4, BLOCK_LEN), 1.0, 6.0, ((0, 256),), jnp.float32)
    src_partial = gaussian(keys[6], (BLOCKS, 5, BLOCK_LEN), 1.0, 6.0, ((0, 256),), jnp.float32)
    return dict(block_bin=block_bin, block_rows=block_rows, row_source=row_source, obs_resid=obs_resid, obs_phase=obs_phase, att_partial=att_partial, src_partial=src_partial)


KNOT_PRIOR = 1.0
SOURCE_PRIOR = 1.0
PRECISE = lax.Precision.HIGHEST
PAIR_LIST = [(first, second) for first in range(5) for second in range(first, 5)]

def spline_basis(phase_values):
    square = phase_values * phase_values
    third_power = square * phase_values
    remain = 1.0 - phase_values
    return jnp.stack([remain * remain * remain / 6.0, (3.0 * third_power - 6.0 * square + 4.0) / 6.0, (-3.0 * third_power + 3.0 * square + 3.0 * phase_values + 1.0) / 6.0, third_power / 6.0], axis=-2)

def design_rows(phase_values, partial_values):
    spline = spline_basis(phase_values)
    new_shape = spline.shape[:-2] + (16, spline.shape[-1])
    return (spline[..., :, None, :] * partial_values[..., None, :, :]).reshape(new_shape)

def block_normals(design, resid_values):
    grams = jnp.einsum('...ar,...br->...ab', design, design, precision=PRECISE)
    right_side = jnp.einsum('...ar,...r->...a', design, resid_values, precision=PRECISE)
    return (grams.reshape(grams.shape[:-2] + (256,)), right_side)

def spread_knots(values_in):
    summed = None
    for offset in range(4):
        piece_part = values_in[..., 4 * offset:4 * offset + 4, :]
        widths = [(0, 0)] * (piece_part.ndim - 1) + [(offset, 3 - offset)]
        padded = jnp.pad(piece_part, widths)
        summed = padded if summed is None else summed + padded
    return summed

def apply_normal(gram_bins, vector):
    bin_count = gram_bins.shape[-1]
    gathered = jnp.concatenate([vector[..., :, offset:offset + bin_count] for offset in range(4)], axis=-2)
    blocks = gram_bins.reshape(gram_bins.shape[:-2] + (16, 16, bin_count))
    product = lax.optimization_barrier(jnp.sum(blocks * gathered[..., None, :, :], axis=-2))
    return KNOT_PRIOR * vector + spread_knots(product)

def solve_window(gram_bins, right_bins):
    right_side = spread_knots(right_bins)
    estimate = jnp.zeros_like(right_side)
    residual = right_side
    direction = right_side
    norm_now = lax.optimization_barrier(jnp.sum(residual * residual, axis=(-2, -1), keepdims=True))
    for iteration in range(ITERS):
        applied = apply_normal(gram_bins, direction)
        step_size = norm_now / lax.optimization_barrier(jnp.sum(direction * applied, axis=(-2, -1), keepdims=True))
        estimate = estimate + step_size * direction
        residual = residual - step_size * applied
        norm_next = lax.optimization_barrier(jnp.sum(residual * residual, axis=(-2, -1), keepdims=True))
        direction = residual + norm_next / norm_now * direction
        norm_now = norm_next
    return estimate

def pick_knots(chosen, local_bin):
    knot_index = local_bin[:, None] + jnp.arange(4, dtype=jnp.int32)[None, :]
    knot_index = jnp.broadcast_to(knot_index[:, None, :], (local_bin.shape[0], 4, 4))
    picked = jnp.take_along_axis(chosen, knot_index, axis=2)
    return jnp.transpose(picked, (0, 2, 1)).reshape(local_bin.shape[0], 16)

def source_terms(gain_masked, corrected):
    columns = [gain_masked[:, pair[0]] * gain_masked[:, pair[1]] for pair in PAIR_LIST]
    columns = columns + [gain_masked[:, param] * corrected for param in range(5)]
    return jnp.stack(columns, axis=-1).reshape(-1, 20)

def solve_five(matrix, right_side):
    entries = {}
    for position, pair in enumerate(PAIR_LIST):
        diagonal_add = SOURCE_PRIOR if pair[0] == pair[1] else 0.0
        entries[pair] = matrix[position] + diagonal_add
    lower_part = {}
    for column in range(5):
        pivot_value = entries[column, column]
        for earlier in range(column):
            pivot_value = pivot_value - lower_part[column, earlier] * lower_part[column, earlier]
        lower_part[column, column] = jnp.sqrt(pivot_value)
        for row_at in range(column + 1, 5):
            running = entries[column, row_at]
            for earlier in range(column):
                running = running - lower_part[row_at, earlier] * lower_part[column, earlier]
            lower_part[row_at, column] = running / lower_part[column, column]
    forward = []
    for row_at in range(5):
        running = right_side[row_at]
        for earlier in range(row_at):
            running = running - lower_part[row_at, earlier] * forward[earlier]
        forward.append(running / lower_part[row_at, row_at])
    backward = [None] * 5
    for row_at in reversed(range(5)):
        running = forward[row_at]
        for later in range(row_at + 1, 5):
            running = running - lower_part[later, row_at] * backward[later]
        backward[row_at] = running / lower_part[row_at, row_at]
    return jnp.stack(backward, axis=0)

def reference(block_bin, block_rows, row_source, obs_resid, obs_phase, att_partial, src_partial):
    device_count = N_SRC * N_WIN * N_CCD
    per_device = block_bin.shape[0] // device_count
    row_width = obs_resid.shape[1]
    bins_window = KNOTS_W - 3
    windows_all = N_SRC * N_WIN
    all_bins = windows_all * bins_window

    def reshaped(values_in):
        return values_in.reshape((device_count, per_device) + values_in.shape[1:])
    stacked = (reshaped(block_bin), reshaped(block_rows), reshaped(row_source), reshaped(obs_resid), reshaped(obs_phase), reshaped(att_partial), reshaped(src_partial))
    position = lax.broadcasted_iota(jnp.int32, (per_device, row_width), 1)

    def first_pass(totals, inputs):
        bins_here, counts_here, source_here, resid_here, phase_here, partial_here, gain_here = inputs
        mask_here = (position < counts_here[:, None]).astype(jnp.float32)
        design = design_rows(phase_here, partial_here * mask_here[:, None, :])
        grams, right_side = block_normals(design, resid_here * mask_here)
        gram_sum = totals[0] + jax.ops.segment_sum(grams, bins_here, num_segments=all_bins)
        right_sum = totals[1] + jax.ops.segment_sum(right_side, bins_here, num_segments=all_bins)
        return ((gram_sum, right_sum), None)
    initial = (jnp.zeros((all_bins, 256), jnp.float32), jnp.zeros((all_bins, 16), jnp.float32))
    (gram_sum, right_sum), unused = lax.scan(first_pass, initial, stacked)
    gram_bins = jnp.transpose(gram_sum.reshape(windows_all, bins_window, 256), (0, 2, 1))
    right_bins = jnp.transpose(right_sum.reshape(windows_all, bins_window, 16), (0, 2, 1))
    attitude = solve_window(gram_bins, right_bins)

    def second_pass(totals, inputs):
        device_id, bins_here, counts_here, source_here, resid_here, phase_here, partial_here, gain_here = inputs
        mask_here = (position < counts_here[:, None]).astype(jnp.float32)
        design = design_rows(phase_here, partial_here * mask_here[:, None, :])
        window_here = bins_here // bins_window
        knots = pick_knots(attitude[window_here], bins_here % bins_window)
        correction = lax.optimization_barrier(jnp.sum(design * knots[:, :, None], axis=1))
        corrected = (resid_here - correction) * mask_here
        terms = source_terms(gain_here * mask_here[:, None, :], corrected)
        source_ids = device_id // N_CCD * SRC_DEV + source_here
        return (totals + jax.ops.segment_sum(terms, source_ids.reshape(-1), num_segments=windows_all * SRC_DEV), None)
    device_ids = jnp.arange(device_count, dtype=jnp.int32)
    summed, unused_two = lax.scan(second_pass, jnp.zeros((windows_all * SRC_DEV, 20), jnp.float32), (device_ids,) + stacked)
    source_delta = solve_five(summed[:, :15].T, summed[:, 15:].T)
    return (attitude, source_delta)
```

```python
import functools
import math

import jax
import jax.numpy as jnp
import numpy as np
from jax import lax
from jax.experimental import pallas as pl
from jax.experimental.pallas import tpu as pltpu
from jax.sharding import PartitionSpec as P

KNOTS_W = 128
BINS_W = 125
NBLK = 128
ROWS = 128
WINDOWS = 64
CAP = 4
SLOTS = WINDOWS * CAP
SRC_DEV = 4096
ITERS = 8
N_CCD = 4
HIGH = 16
LOW = 256
STEP_BLOCKS = 16

KNOT_PRIOR = 1.0
SOURCE_PRIOR = 1.0
PAIR_LIST = [(first, second) for first in range(5) for second in range(first, 5)]
ATT_PAIRS = [(first, second) for first in range(4) for second in range(first, 4)]
RHS_AT = 70
BIN_AT = 86
FEATS = 88

F32 = jnp.float32
BF16 = jnp.bfloat16
NT = (((1,), (1,)), ((), ()))
NN = (((1,), (0,)), ((), ()))

SPLINE = np.array([[1, 0, 0, 0], [4, 12, 6, 1], [1, 6, 12, 4], [0, 0, 0, 1]], np.float64) / 6.0


def knot_matrix():
    pair_at = {}
    for at, (first, second) in enumerate(ATT_PAIRS):
        pair_at[first, second] = pair_at[second, first] = at
    table = np.zeros((120, 4 * FEATS), np.float64)
    for d in range(-3, 4):
        for p in range(4):
            for q in range(4):
                row = ((d + 3) * 4 + p) * 4 + q
                for l in range(4):
                    j = l - d
                    if 0 <= j < 4:
                        for m, value in enumerate(np.convolve(SPLINE[j], SPLINE[l])):
                            table[row, l * FEATS + m * 10 + pair_at[q, p]] += value
    for q in range(4):
        for j in range(4):
            table[112 + q, j * FEATS + RHS_AT + 4 * j + q] = 1.0
            table[116 + q, j * FEATS + RHS_AT + 4 * j + q] = 1.0
    return table.astype(np.float32)


def split_parts(values, count):
    parts = []
    for at in range(count):
        part = values.astype(BF16)
        parts.append(part)
        if at + 1 < count:
            values = values - part.astype(F32)
    return parts


def exact_dot(values, ones, dims, swap=False):
    total = None
    for part in split_parts(values, 3):
        pair = (ones, part) if swap else (part, ones)
        piece = lax.dot_general(*pair, dims, preferred_element_type=F32)
        total = piece if total is None else total + piece
    return total


def indicator(condition):
    return jnp.where(condition, 1.0, 0.0).astype(BF16)


def iota(shape, axis):
    return lax.broadcasted_iota(jnp.int32, shape, axis)


def iota_f(shape, axis):
    return iota(shape, axis).astype(F32)


def normals_kernel(bin_ref, rows_ref, resid_ref, phase_ref, att_ref, send_ref, obs_ref, slot_ref, pay_ref):
    square = (NBLK, NBLK)
    bins = bin_ref[...].astype(F32)
    window = jnp.floor((bins + 0.5) * (1.0 / BINS_W))
    local_bin = bins - BINS_W * window
    mask = iota(square, 0) < rows_ref[...]
    u = phase_ref[...].T
    resid = jnp.where(mask, resid_ref[...].T, 0.0)
    att = [jnp.where(mask, att_ref[pl.ds(q, NBLK, stride=4), :].T, 0.0) for q in range(4)]
    obs_ref[0:128, :] = u
    obs_ref[128:256, :] = resid
    for q in range(4):
        obs_ref[256 + 128 * q : 384 + 128 * q, :] = att[q]
    v = 1.0 - u
    u2, v2 = u * u, v * v
    u3, v3 = u2 * u, v2 * v
    cubes = [v3, u * v2, u2 * v, u3]
    powers = [v3 * v3, u * v2 * v3, u2 * v2 * v2, u3 * v3, u2 * u2 * v2, u3 * u2 * v, u3 * u3]
    for at, (first, second) in enumerate(ATT_PAIRS):
        product = att[first] * att[second]
        for m in range(7):
            row = m * 10 + at
            pay_ref[row : row + 1, :] = jnp.sum(powers[m] * product, axis=0, keepdims=True)
    for q in range(4):
        product = att[q] * resid
        sums = [jnp.sum(cubes[i] * product, axis=0, keepdims=True) for i in range(4)]
        for j in range(4):
            total = None
            for i in range(4):
                if SPLINE[j, i] != 0.0:
                    piece = float(SPLINE[j, i]) * sums[i]
                    total = piece if total is None else total + piece
            row = RHS_AT + 4 * j + q
            pay_ref[row : row + 1, :] = total
    pay_ref[BIN_AT : BIN_AT + 1, :] = local_bin
    pay_ref[BIN_AT + 1 :, :] = jnp.zeros((NBLK - BIN_AT - 1, NBLK), F32)
    window_column = jnp.broadcast_to(window, square).T
    earlier = jnp.where(window_column == window, 1.0, 0.0) * jnp.where(iota(square, 0) < iota(square, 1), 1.0, 0.0)
    rank = jnp.sum(earlier, axis=0, keepdims=True)
    slot_ref[...] = jnp.concatenate([window, rank, jnp.zeros((6, NBLK), F32)], axis=0)
    place = indicator(iota_f((SLOTS, NBLK), 0) == CAP * window + rank)
    send_ref[...] = exact_dot(pay_ref[...], place, NT, swap=True)


def bins_kernel(got_ref, out_ref):
    got = got_ref[...].T
    place = indicator(iota_f((KNOTS_W, SLOTS), 0) == got[BIN_AT : BIN_AT + 1, :])
    out_ref[...] = exact_dot(got[:FEATS], place, NT)


def attitude_kernel(own_ref, one_ref, two_ref, three_ref, got_ref, table_ref, att_ref, reply_ref):
    total = (own_ref[...] + two_ref[...]) + (one_ref[...] + three_ref[...])
    moved = jnp.concatenate([total] + [pltpu.roll(total, l, 1) for l in range(1, 4)], axis=0)
    band = lax.dot_general(table_ref[...], moved, NN, precision=lax.Precision.HIGHEST, preferred_element_type=F32)
    groups = [band[8 * at : 8 * at + 8] for at in range(14)]
    lower_half = iota((8, KNOTS_W), 0) < 4

    def doubled(values):
        return values + pltpu.roll(values, 4, 0)

    def norm(values):
        return jnp.sum(jnp.sum(values, axis=1, keepdims=True), axis=0, keepdims=True)

    def apply(vector):
        spread = [
            jnp.where(lower_half, vector[2 * at : 2 * at + 1, :], vector[2 * at + 1 : 2 * at + 2, :]) for at in range(2)
        ]
        result = None
        for d in range(-3, 4):
            piece = groups[2 * (d + 3)] * spread[0] + groups[2 * (d + 3) + 1] * spread[1]
            if d:
                piece = pltpu.roll(piece, -d % KNOTS_W, 1)
            result = piece if result is None else result + piece
        return KNOT_PRIOR * vector + doubled(result)

    residual = band[112:120]
    direction = residual
    estimate = jnp.zeros_like(residual)
    norm_now = norm(residual * residual)
    for _ in range(ITERS):
        applied = apply(direction)
        step_size = norm_now / norm(direction * applied)
        estimate = estimate + step_size * direction
        residual = residual - step_size * applied
        norm_next = norm(residual * residual)
        direction = residual + norm_next / norm_now * direction
        norm_now = norm_next
    att_ref[0] = estimate[:4]
    moved = jnp.concatenate([estimate[:4]] + [pltpu.roll(estimate, KNOTS_W - j, 1)[:4] for j in range(1, 4)], axis=0)
    column = jnp.concatenate(
        [got_ref[pl.ds(s, WINDOWS, stride=CAP), :][:, BIN_AT : BIN_AT + 1] for s in range(CAP)], axis=0
    )
    place = indicator(iota_f((SLOTS, KNOTS_W), 1) == column)
    knots = exact_dot(moved, place, NT, swap=True)
    reply_ref[...] = jnp.zeros((WINDOWS, 128), F32)
    for s in range(CAP):
        reply_ref[:, 16 * s : 16 * s + 16] = knots[WINDOWS * s : WINDOWS * s + WINDOWS]


def source_sums(count, terms_ref, high_ref, low_ref, a_ref, b_ref, acc_ref):
    high_at = iota_f((HIGH, ROWS), 0)
    low_at = iota_f((LOW, ROWS), 0).astype(BF16)
    acc_ref[...] = jnp.zeros(acc_ref.shape, F32)

    def step(at, carry):
        for inner in range(STEP_BLOCKS):
            block = at * STEP_BLOCKS + inner
            lanes = slice(inner * ROWS, inner * ROWS + ROWS)
            here = high_at == high_ref[pl.ds(block, 1), :]
            low = jnp.broadcast_to(low_ref[pl.ds(block, 1), :], (HIGH, ROWS)).astype(BF16)
            low = jnp.concatenate([low] * (LOW // HIGH), axis=0)
            b_ref[:, lanes] = jnp.where(low_at == low, jnp.ones((), BF16), jnp.zeros((), BF16))
            for c in range(2 * count):
                term = jnp.where(here, terms_ref[pl.ds(c * NBLK + block, 1), :], 0.0)
                a_ref[c * HIGH : (c + 1) * HIGH, lanes] = term.astype(BF16)
        acc_ref[...] += lax.dot_general(a_ref[...], b_ref[...], NT, preferred_element_type=F32)
        return carry

    lax.fori_loop(0, NBLK // STEP_BLOCKS, step, 0)


def put_terms(terms_ref, c, values):
    large = values.astype(BF16).astype(F32)
    terms_ref[2 * c * NBLK : (2 * c + 1) * NBLK, :] = large
    terms_ref[(2 * c + 1) * NBLK : (2 * c + 2) * NBLK, :] = values - large


def put_sources(source_ref, high_ref, low_ref):
    source = source_ref[...]
    high = source >> 8
    high_ref[...] = high.astype(F32)
    low_ref[...] = (source - (high << 8)).astype(F32)


def source_normals_kernel(rows_ref, source_ref, gain_ref, out_ref, terms_ref, high_ref, low_ref, a_ref, b_ref, acc_ref):
    square = (NBLK, ROWS)
    used = jnp.broadcast_to(rows_ref[...].astype(F32), square).T
    mask = iota_f(square, 1) < used
    put_sources(source_ref, high_ref, low_ref)
    gains = [jnp.where(mask, gain_ref[NBLK * p : NBLK * p + NBLK, :], 0.0) for p in range(5)]
    for at, (first, second) in enumerate(PAIR_LIST):
        put_terms(terms_ref, at, gains[first] * gains[second])
    source_sums(15, terms_ref, high_ref, low_ref, a_ref, b_ref, acc_ref)
    for c in range(15):
        out_ref[HIGH * c : HIGH * c + HIGH, :] = (
            acc_ref[2 * c * HIGH : (2 * c + 1) * HIGH, :] + acc_ref[(2 * c + 1) * HIGH : (2 * c + 2) * HIGH, :]
        )


def source_right_kernel(
    reply_ref, slot_ref, obs_ref, source_ref, gain_ref, out_ref, terms_ref, high_ref, low_ref, a_ref, b_ref, acc_ref
):
    put_sources(source_ref, high_ref, low_ref)
    place = indicator(iota_f((WINDOWS, NBLK), 0) == slot_ref[0:1, :])
    rank = slot_ref[1:2, :]
    spread = exact_dot(reply_ref[...].T, place, NN)
    knots = None
    for s in range(CAP):
        piece = jnp.where(rank == float(s), spread[16 * s : 16 * s + 16, :], 0.0)
        knots = piece if knots is None else knots + piece
    u = obs_ref[0:128, :]
    att = [obs_ref[256 + 128 * q : 384 + 128 * q, :] for q in range(4)]
    v = 1.0 - u
    u2, v2 = u * u, v * v
    cubes = [v2 * v, u * v2, u2 * v, u2 * u]
    values = obs_ref[128:256, :]
    for j in range(4):
        spline = None
        for i in range(4):
            if SPLINE[j, i] != 0.0:
                piece = float(SPLINE[j, i]) * cubes[i]
                spline = piece if spline is None else spline + piece
        inner = None
        for q in range(4):
            piece = att[q] * knots[4 * j + q : 4 * j + q + 1, :]
            inner = piece if inner is None else inner + piece
        values = values - spline * inner
    values = values.T
    for p in range(5):
        put_terms(terms_ref, p, gain_ref[NBLK * p : NBLK * p + NBLK, :] * values)
    source_sums(5, terms_ref, high_ref, low_ref, a_ref, b_ref, acc_ref)
    for c in range(5):
        out_ref[HIGH * c : HIGH * c + HIGH, :] = (
            acc_ref[2 * c * HIGH : (2 * c + 1) * HIGH, :] + acc_ref[(2 * c + 1) * HIGH : (2 * c + 2) * HIGH, :]
        )


def factor_kernel(own_ref, one_ref, two_ref, three_ref, out_ref):
    entries = {}
    for at, pair in enumerate(PAIR_LIST):
        rows = slice(HIGH * at, HIGH * at + HIGH)
        total = (own_ref[rows, :] + two_ref[rows, :]) + (one_ref[rows, :] + three_ref[rows, :])
        entries[pair] = total + SOURCE_PRIOR if pair[0] == pair[1] else total
    lower = {}
    for column in range(5):
        pivot = entries[column, column]
        for before in range(column):
            pivot = pivot - lower[column, before] * lower[column, before]
        inverse = 1.0 / jnp.sqrt(pivot)
        lower[column, column] = inverse
        for row in range(column + 1, 5):
            running = entries[column, row]
            for before in range(column):
                running = running - lower[row, before] * lower[column, before]
            lower[row, column] = running * inverse
    for at, (first, second) in enumerate(PAIR_LIST):
        out_ref[HIGH * at : HIGH * at + HIGH, :] = lower[second, first]


def solve_kernel(factor_ref, own_ref, one_ref, two_ref, three_ref, out_ref):
    lower = {}
    for at, (first, second) in enumerate(PAIR_LIST):
        lower[second, first] = factor_ref[HIGH * at : HIGH * at + HIGH, :]
    values = []
    for row in range(5):
        rows = slice(HIGH * row, HIGH * row + HIGH)
        running = (own_ref[rows, :] + two_ref[rows, :]) + (one_ref[rows, :] + three_ref[rows, :])
        for before in range(row):
            running = running - lower[row, before] * values[before]
        values.append(running * lower[row, row])
    for row in reversed(range(5)):
        running = values[row]
        for later in range(row + 1, 5):
            running = running - lower[later, row] * values[later]
        values[row] = running * lower[row, row]
    for row in range(5):
        for high in range(HIGH):
            out_ref[row : row + 1, LOW * high : LOW * high + LOW] = values[row][high : high + 1, :]


def f32(*shape):
    return jax.ShapeDtypeStruct(shape, F32)


def kernel_call(body, name, outs, *args, scratch=(), flops=1_000_000):
    size = sum(math.prod(a.shape) * 4 for a in args)
    return pl.pallas_call(
        body,
        out_shape=outs,
        scratch_shapes=list(scratch),
        compiler_params=pltpu.CompilerParams(vmem_limit_bytes=32 * 1024 * 1024),
        cost_estimate=pl.CostEstimate(flops=flops, bytes_accessed=size, transcendentals=0),
        name=name,
    )(*args)


def segment_scratch(count):
    return (
        pltpu.VMEM((2 * count * NBLK, ROWS), F32),
        pltpu.VMEM((NBLK, ROWS), F32),
        pltpu.VMEM((NBLK, ROWS), F32),
        pltpu.VMEM((2 * count * HIGH, STEP_BLOCKS * ROWS), BF16),
        pltpu.VMEM((LOW, STEP_BLOCKS * ROWS), BF16),
        pltpu.VMEM((2 * count * HIGH, LOW), F32),
    )


def from_others(values):
    return [
        lax.ppermute(values, "ccd", [(at, (at + shift) % N_CCD) for at in range(N_CCD)]) for shift in range(1, N_CCD)
    ]


def to_windows(values):
    return lax.all_to_all(values, ("src", "win"), split_axis=0, concat_axis=0, tiled=True)


def local(block_bin, block_rows, row_source, obs_resid, obs_phase, att_partial, src_partial):
    bins = block_bin.reshape(1, NBLK)
    rows = block_rows.reshape(1, NBLK)
    gains = jnp.transpose(src_partial, (1, 0, 2)).reshape(5 * NBLK, ROWS)
    send, obs, slots = kernel_call(
        normals_kernel,
        "normals",
        (f32(SLOTS, 128), f32(6 * ROWS, NBLK), f32(8, NBLK)),
        bins,
        rows,
        obs_resid,
        obs_phase,
        att_partial.reshape(4 * NBLK, ROWS),
        scratch=(pltpu.VMEM((NBLK, NBLK), F32),),
    )
    got = to_windows(send.reshape(WINDOWS, CAP, 128)).reshape(SLOTS, 128)
    normal = kernel_call(
        source_normals_kernel,
        "source_normals",
        f32(15 * HIGH, LOW),
        rows,
        row_source,
        gains,
        scratch=segment_scratch(15),
        flops=2 * 480 * 256 * 16384,
    )
    moments = kernel_call(bins_kernel, "bins", f32(FEATS, KNOTS_W), got)
    attitude, reply = kernel_call(
        attitude_kernel,
        "attitude",
        (f32(1, 4, KNOTS_W), f32(WINDOWS, 128)),
        moments,
        *from_others(moments),
        got,
        jnp.asarray(knot_matrix()),
    )
    knots = to_windows(reply)
    factors = kernel_call(factor_kernel, "factors", f32(15 * HIGH, LOW), normal, *from_others(normal))
    right = kernel_call(
        source_right_kernel,
        "source_right",
        f32(5 * HIGH, LOW),
        knots,
        slots,
        obs,
        row_source,
        gains,
        scratch=segment_scratch(5),
        flops=2 * 160 * 256 * 16384,
    )
    source_delta = kernel_call(solve_kernel, "solve", f32(5, SRC_DEV), factors, right, *from_others(right))
    return attitude, source_delta


def solution(mesh):
    return jax.shard_map(
        local,
        mesh=mesh,
        in_specs=(
            P(("src", "win", "ccd")),
            P(("src", "win", "ccd")),
            P(("src", "win", "ccd"), None),
            P(("src", "win", "ccd"), None),
            P(("src", "win", "ccd"), None),
            P(("src", "win", "ccd"), None, None),
            P(("src", "win", "ccd"), None, None),
        ),
        out_specs=(P(("src", "win"), None, None), P(None, ("src", "win"))),
        check_vma=False,
    )
```

```python
import functools
import math

import jax
import jax.numpy as jnp
import numpy as np
from jax import lax
from jax.experimental import pallas as pl
from jax.experimental.pallas import tpu as pltpu
from jax.sharding import PartitionSpec as P

KNOTS_W = 128
BINS_W = 125
NBLK = 128
ROWS = 128
WINDOWS = 64
CAP = 4
SLOTS = WINDOWS * CAP
SRC_DEV = 4096
ITERS = 8
N_CCD = 4
HIGH = 16
LOW = 256
STEP_BLOCKS = 16
STEPS = NBLK // STEP_BLOCKS

KNOT_PRIOR = 1.0
SOURCE_PRIOR = 1.0
PAIR_LIST = [(first, second) for first in range(5) for second in range(first, 5)]
ATT_PAIRS = [(first, second) for first in range(4) for second in range(first, 4)]
RHS_AT = 70
BIN_AT = 86
FEATS = 88

F32 = jnp.float32
BF16 = jnp.bfloat16
NT = (((1,), (1,)), ((), ()))
NN = (((1,), (0,)), ((), ()))

SPLINE = np.array([[1, 0, 0, 0], [4, 12, 6, 1], [1, 6, 12, 4], [0, 0, 0, 1]], np.float64) / 6.0


def knot_matrix():
    pair_at = {}
    for at, (first, second) in enumerate(ATT_PAIRS):
        pair_at[first, second] = pair_at[second, first] = at
    table = np.zeros((120, 4 * FEATS), np.float64)
    for d in range(-3, 4):
        for p in range(4):
            for q in range(4):
                row = ((d + 3) * 4 + p) * 4 + q
                for l in range(4):
                    j = l - d
                    if 0 <= j < 4:
                        for m, value in enumerate(np.convolve(SPLINE[j], SPLINE[l])):
                            table[row, l * FEATS + m * 10 + pair_at[q, p]] += value
    for q in range(4):
        for j in range(4):
            table[112 + q, j * FEATS + RHS_AT + 4 * j + q] = 1.0
            table[116 + q, j * FEATS + RHS_AT + 4 * j + q] = 1.0
    return table.astype(np.float32)


def split_parts(values, count):
    parts = []
    for at in range(count):
        part = values.astype(BF16)
        parts.append(part)
        if at + 1 < count:
            values = values - part.astype(F32)
    return parts


def exact_dot(values, ones, dims, swap=False):
    total = None
    for part in split_parts(values, 3):
        pair = (ones, part) if swap else (part, ones)
        piece = lax.dot_general(*pair, dims, preferred_element_type=F32)
        total = piece if total is None else total + piece
    return total


def indicator(condition):
    return jnp.where(condition, 1.0, 0.0).astype(BF16)


def iota(shape, axis):
    return lax.broadcasted_iota(jnp.int32, shape, axis)


def iota_f(shape, axis):
    return iota(shape, axis).astype(F32)


def normals_kernel(*refs):
    given, (send_ref, obs_ref, slot_ref), here, (pay_ref, done_ref) = refs[:5], refs[5:8], refs[8:13], refs[13:]
    copies = [pltpu.make_async_copy(given[at], here[at], done_ref.at[at]) for at in range(5)]
    for copy in copies:
        copy.start()
    for copy in copies:
        copy.wait()
    bin_ref, rows_ref, resid_ref, phase_ref, att_ref = here
    square = (NBLK, NBLK)
    bins = bin_ref[...].astype(F32)
    window = jnp.floor((bins + 0.5) * (1.0 / BINS_W))
    local_bin = bins - BINS_W * window
    mask = iota(square, 0) < rows_ref[...]
    u = phase_ref[...].T
    resid = jnp.where(mask, resid_ref[...].T, 0.0)
    att = [jnp.where(mask, att_ref[pl.ds(q, NBLK, stride=4), :].T, 0.0) for q in range(4)]
    obs_ref[0:128, :] = u
    obs_ref[128:256, :] = resid
    for q in range(4):
        obs_ref[256 + 128 * q : 384 + 128 * q, :] = att[q]
    v = 1.0 - u
    u2, v2 = u * u, v * v
    u3, v3 = u2 * u, v2 * v
    cubes = [v3, u * v2, u2 * v, u3]
    powers = [v3 * v3, u * v2 * v3, u2 * v2 * v2, u3 * v3, u2 * u2 * v2, u3 * u2 * v, u3 * u3]
    for at, (first, second) in enumerate(ATT_PAIRS):
        product = att[first] * att[second]
        for m in range(7):
            row = m * 10 + at
            pay_ref[row : row + 1, :] = jnp.sum(powers[m] * product, axis=0, keepdims=True)
    for q in range(4):
        product = att[q] * resid
        sums = [jnp.sum(cubes[i] * product, axis=0, keepdims=True) for i in range(4)]
        for j in range(4):
            total = None
            for i in range(4):
                if SPLINE[j, i] != 0.0:
                    piece = float(SPLINE[j, i]) * sums[i]
                    total = piece if total is None else total + piece
            row = RHS_AT + 4 * j + q
            pay_ref[row : row + 1, :] = total
    pay_ref[BIN_AT : BIN_AT + 1, :] = local_bin
    pay_ref[BIN_AT + 1 :, :] = jnp.zeros((NBLK - BIN_AT - 1, NBLK), F32)
    window_column = jnp.broadcast_to(window, square).T
    earlier = jnp.where(window_column == window, 1.0, 0.0) * jnp.where(iota(square, 0) < iota(square, 1), 1.0, 0.0)
    rank = jnp.sum(earlier, axis=0, keepdims=True)
    slot_ref[...] = jnp.concatenate([window, rank, jnp.zeros((6, NBLK), F32)], axis=0)
    place = indicator(iota_f((SLOTS, NBLK), 0) == CAP * window + rank)
    send_ref[...] = exact_dot(pay_ref[...], place, NT, swap=True)


def bins_kernel(got_ref, out_ref):
    got = got_ref[...].T
    place = indicator(iota_f((KNOTS_W, SLOTS), 0) == got[BIN_AT : BIN_AT + 1, :])
    out_ref[...] = exact_dot(got[:FEATS], place, NT)


def attitude_kernel(own_ref, one_ref, two_ref, three_ref, got_ref, table_ref, att_ref, reply_ref):
    total = (own_ref[...] + two_ref[...]) + (one_ref[...] + three_ref[...])
    moved = jnp.concatenate([total] + [pltpu.roll(total, l, 1) for l in range(1, 4)], axis=0)
    band = lax.dot_general(table_ref[...], moved, NN, precision=lax.Precision.HIGHEST, preferred_element_type=F32)
    groups = [band[8 * at : 8 * at + 8] for at in range(14)]
    lower_half = iota((8, KNOTS_W), 0) < 4

    def doubled(values):
        return values + pltpu.roll(values, 4, 0)

    def norm(values):
        return jnp.sum(jnp.sum(values, axis=1, keepdims=True), axis=0, keepdims=True)

    def apply(vector):
        spread = [
            jnp.where(lower_half, vector[2 * at : 2 * at + 1, :], vector[2 * at + 1 : 2 * at + 2, :]) for at in range(2)
        ]
        result = None
        for d in range(-3, 4):
            piece = groups[2 * (d + 3)] * spread[0] + groups[2 * (d + 3) + 1] * spread[1]
            if d:
                piece = pltpu.roll(piece, -d % KNOTS_W, 1)
            result = piece if result is None else result + piece
        return KNOT_PRIOR * vector + doubled(result)

    residual = band[112:120]
    direction = residual
    estimate = jnp.zeros_like(residual)
    norm_now = norm(residual * residual)
    for _ in range(ITERS):
        applied = apply(direction)
        step_size = norm_now / norm(direction * applied)
        estimate = estimate + step_size * direction
        residual = residual - step_size * applied
        norm_next = norm(residual * residual)
        direction = residual + norm_next / norm_now * direction
        norm_now = norm_next
    att_ref[0] = estimate[:4]
    moved = jnp.concatenate([estimate[:4]] + [pltpu.roll(estimate, KNOTS_W - j, 1)[:4] for j in range(1, 4)], axis=0)
    column = jnp.concatenate(
        [got_ref[pl.ds(s, WINDOWS, stride=CAP), :][:, BIN_AT : BIN_AT + 1] for s in range(CAP)], axis=0
    )
    place = indicator(iota_f((SLOTS, KNOTS_W), 1) == column)
    knots = exact_dot(moved, place, NT, swap=True)
    reply_ref[...] = jnp.zeros((WINDOWS, 128), F32)
    for s in range(CAP):
        reply_ref[:, 16 * s : 16 * s + 16] = knots[WINDOWS * s : WINDOWS * s + WINDOWS]


def source_sums(count, terms_ref, high_ref, low_ref, out_ref, acc_ref, *buffers):
    high_at = iota_f((HIGH, ROWS), 0)
    low_at = iota_f((LOW, ROWS), 0).astype(BF16)
    one, zero = jnp.ones((), BF16), jnp.zeros((), BF16)

    def build(at, slot):
        a_ref, b_ref = buffers[slot], buffers[2 + slot]
        for inner in range(STEP_BLOCKS):
            block = at * STEP_BLOCKS + inner
            lanes = slice(inner * ROWS, inner * ROWS + ROWS)
            here = high_at == high_ref[pl.ds(block, 1), :]
            low = jnp.broadcast_to(low_ref[pl.ds(block, 1), :], (HIGH, ROWS)).astype(BF16)
            low = jnp.concatenate([low] * (LOW // HIGH), axis=0)
            b_ref[:, lanes] = jnp.where(low_at == low, one, zero)
            for c in range(2 * count):
                term = jnp.where(here, terms_ref[pl.ds(c * NBLK + block, 1), :], 0.0)
                a_ref[c * HIGH : (c + 1) * HIGH, lanes] = term.astype(BF16)

    def multiply(slot):
        acc_ref[...] += lax.dot_general(buffers[2 + slot][...], buffers[slot][...], NT, preferred_element_type=F32)

    def step(pair, carry):
        multiply(0)
        build(2 * pair + 1, 1)
        multiply(1)
        build(2 * pair + 2, 0)
        return carry

    acc_ref[...] = jnp.zeros(acc_ref.shape, F32)
    build(0, 0)
    lax.fori_loop(0, STEPS // 2 - 1, step, 0)
    multiply(0)
    build(STEPS - 1, 1)
    multiply(1)
    sums = acc_ref[...].T
    for c in range(count):
        at = 2 * c * HIGH
        out_ref[HIGH * c : HIGH * c + HIGH, :] = sums[at : at + HIGH] + sums[at + HIGH : at + 2 * HIGH]


def put_terms(terms_ref, c, values):
    large = values.astype(BF16).astype(F32)
    terms_ref[2 * c * NBLK : (2 * c + 1) * NBLK, :] = large
    terms_ref[(2 * c + 1) * NBLK : (2 * c + 2) * NBLK, :] = values - large


def put_sources(source_ref, high_ref, low_ref):
    source = source_ref[...]
    high = source >> 8
    high_ref[...] = high.astype(F32)
    low_ref[...] = (source - (high << 8)).astype(F32)


def source_normals_kernel(rows_ref, source_ref, gain_ref, out_ref, terms_ref, high_ref, low_ref, *work):
    square = (NBLK, ROWS)
    used = jnp.broadcast_to(rows_ref[...].astype(F32), square).T
    mask = iota_f(square, 1) < used
    put_sources(source_ref, high_ref, low_ref)
    gains = [jnp.where(mask, gain_ref[NBLK * p : NBLK * p + NBLK, :], 0.0) for p in range(5)]
    for at, (first, second) in enumerate(PAIR_LIST):
        put_terms(terms_ref, at, gains[first] * gains[second])
    source_sums(15, terms_ref, high_ref, low_ref, out_ref, *work)


def source_right_kernel(
    reply_ref, slot_ref, obs_ref, source_ref, gain_ref, out_ref, terms_ref, high_ref, low_ref, *work
):
    put_sources(source_ref, high_ref, low_ref)
    place = indicator(iota_f((WINDOWS, NBLK), 0) == slot_ref[0:1, :])
    rank = slot_ref[1:2, :]
    spread = exact_dot(reply_ref[...].T, place, NN)
    knots = None
    for s in range(CAP):
        piece = jnp.where(rank == float(s), spread[16 * s : 16 * s + 16, :], 0.0)
        knots = piece if knots is None else knots + piece
    u = obs_ref[0:128, :]
    att = [obs_ref[256 + 128 * q : 384 + 128 * q, :] for q in range(4)]
    v = 1.0 - u
    u2, v2 = u * u, v * v
    cubes = [v2 * v, u * v2, u2 * v, u2 * u]
    values = obs_ref[128:256, :]
    for j in range(4):
        spline = None
        for i in range(4):
            if SPLINE[j, i] != 0.0:
                piece = float(SPLINE[j, i]) * cubes[i]
                spline = piece if spline is None else spline + piece
        inner = None
        for q in range(4):
            piece = att[q] * knots[4 * j + q : 4 * j + q + 1, :]
            inner = piece if inner is None else inner + piece
        values = values - spline * inner
    values = values.T
    for p in range(5):
        put_terms(terms_ref, p, gain_ref[NBLK * p : NBLK * p + NBLK, :] * values)
    source_sums(5, terms_ref, high_ref, low_ref, out_ref, *work)


def factor_kernel(own_ref, one_ref, two_ref, three_ref, out_ref):
    entries = {}
    for at, pair in enumerate(PAIR_LIST):
        rows = slice(HIGH * at, HIGH * at + HIGH)
        total = (own_ref[rows, :] + two_ref[rows, :]) + (one_ref[rows, :] + three_ref[rows, :])
        entries[pair] = total + SOURCE_PRIOR if pair[0] == pair[1] else total
    lower = {}
    for column in range(5):
        pivot = entries[column, column]
        for before in range(column):
            pivot = pivot - lower[column, before] * lower[column, before]
        inverse = 1.0 / jnp.sqrt(pivot)
        lower[column, column] = inverse
        for row in range(column + 1, 5):
            running = entries[column, row]
            for before in range(column):
                running = running - lower[row, before] * lower[column, before]
            lower[row, column] = running * inverse
    for at, (first, second) in enumerate(PAIR_LIST):
        out_ref[HIGH * at : HIGH * at + HIGH, :] = lower[second, first]


def solve_kernel(factor_ref, own_ref, one_ref, two_ref, three_ref, out_ref):
    lower = {}
    for at, (first, second) in enumerate(PAIR_LIST):
        lower[second, first] = factor_ref[HIGH * at : HIGH * at + HIGH, :]
    values = []
    for row in range(5):
        rows = slice(HIGH * row, HIGH * row + HIGH)
        running = (own_ref[rows, :] + two_ref[rows, :]) + (one_ref[rows, :] + three_ref[rows, :])
        for before in range(row):
            running = running - lower[row, before] * values[before]
        values.append(running * lower[row, row])
    for row in reversed(range(5)):
        running = values[row]
        for later in range(row + 1, 5):
            running = running - lower[later, row] * values[later]
        values[row] = running * lower[row, row]
    for row in range(5):
        for high in range(HIGH):
            out_ref[row : row + 1, LOW * high : LOW * high + LOW] = values[row][high : high + 1, :]


def f32(*shape):
    return jax.ShapeDtypeStruct(shape, F32)


def kernel_call(body, name, outs, *args, scratch=(), flops=1_000_000, in_specs=None, grant=32):
    size = sum(math.prod(a.shape) * 4 for a in args)
    return pl.pallas_call(
        body,
        out_shape=outs,
        in_specs=in_specs or [pl.BlockSpec(memory_space=pltpu.MemorySpace.VMEM)] * len(args),
        scratch_shapes=list(scratch),
        compiler_params=pltpu.CompilerParams(vmem_limit_bytes=grant * 1024 * 1024),
        cost_estimate=pl.CostEstimate(flops=flops, bytes_accessed=size, transcendentals=0),
        name=name,
    )(*args)


def segment_scratch(count):
    return (
        pltpu.VMEM((2 * count * NBLK, ROWS), F32),
        pltpu.VMEM((NBLK, ROWS), F32),
        pltpu.VMEM((NBLK, ROWS), F32),
        pltpu.VMEM((LOW, 2 * count * HIGH), F32),
        pltpu.VMEM((2 * count * HIGH, STEP_BLOCKS * ROWS), BF16),
        pltpu.VMEM((2 * count * HIGH, STEP_BLOCKS * ROWS), BF16),
        pltpu.VMEM((LOW, STEP_BLOCKS * ROWS), BF16),
        pltpu.VMEM((LOW, STEP_BLOCKS * ROWS), BF16),
    )


def from_others(values):
    return [
        lax.ppermute(values, "ccd", [(at, (at + shift) % N_CCD) for at in range(N_CCD)]) for shift in range(1, N_CCD)
    ]


def to_windows(values):
    return lax.all_to_all(values, ("src", "win"), split_axis=0, concat_axis=0, tiled=True)


def local(block_bin, block_rows, row_source, obs_resid, obs_phase, att_partial, src_partial):
    bins = block_bin.reshape(1, NBLK)
    rows = block_rows.reshape(1, NBLK)
    gains = jnp.transpose(src_partial, (1, 0, 2)).reshape(5 * NBLK, ROWS)
    send, obs, slots = kernel_call(
        normals_kernel,
        "normals",
        (f32(SLOTS, 128), f32(6 * ROWS, NBLK), f32(8, NBLK)),
        bins,
        rows,
        obs_resid,
        obs_phase,
        att_partial.reshape(4 * NBLK, ROWS),
        scratch=(
            pltpu.VMEM((1, NBLK), jnp.int32),
            pltpu.VMEM((1, NBLK), jnp.int32),
            pltpu.VMEM((NBLK, ROWS), F32),
            pltpu.VMEM((NBLK, ROWS), F32),
            pltpu.VMEM((4 * NBLK, ROWS), F32),
            pltpu.VMEM((NBLK, NBLK), F32),
            pltpu.SemaphoreType.DMA((5,)),
        ),
        in_specs=[pl.BlockSpec(memory_space=pl.ANY)] * 5,
        grant=56,
    )
    got = to_windows(send.reshape(WINDOWS, CAP, 128)).reshape(SLOTS, 128)
    normal = kernel_call(
        source_normals_kernel,
        "source_normals",
        f32(15 * HIGH, LOW),
        rows,
        row_source,
        gains,
        scratch=segment_scratch(15),
        flops=2 * 480 * 256 * 16384,
    )
    moments = kernel_call(bins_kernel, "bins", f32(FEATS, KNOTS_W), got)
    attitude, reply = kernel_call(
        attitude_kernel,
        "attitude",
        (f32(1, 4, KNOTS_W), f32(WINDOWS, 128)),
        moments,
        *from_others(moments),
        got,
        jnp.asarray(knot_matrix()),
    )
    knots = to_windows(reply)
    factors = kernel_call(factor_kernel, "factors", f32(15 * HIGH, LOW), normal, *from_others(normal))
    right = kernel_call(
        source_right_kernel,
        "source_right",
        f32(5 * HIGH, LOW),
        knots,
        slots,
        obs,
        row_source,
        gains,
        scratch=segment_scratch(5),
        flops=2 * 160 * 256 * 16384,
    )
    source_delta = kernel_call(solve_kernel, "solve", f32(5, SRC_DEV), factors, right, *from_others(right))
    return attitude, source_delta


def solution(mesh):
    return jax.shard_map(
        local,
        mesh=mesh,
        in_specs=(
            P(("src", "win", "ccd")),
            P(("src", "win", "ccd")),
            P(("src", "win", "ccd"), None),
            P(("src", "win", "ccd"), None),
            P(("src", "win", "ccd"), None),
            P(("src", "win", "ccd"), None, None),
            P(("src", "win", "ccd"), None, None),
        ),
        out_specs=(P(("src", "win"), None, None), P(None, ("src", "win"))),
        check_vma=False,
    )
```

```python
import math

import jax
import jax.numpy as jnp
import ml_dtypes
import numpy as np
from jax import lax
from jax.experimental import pallas as pl
from jax.experimental.pallas import tpu as pltpu
from jax.sharding import PartitionSpec as P

KNOTS_W = 128
BINS_W = 125
NBLK = 128
ROWS = 128
WINDOWS = 64
CAP = 4
SLOTS = WINDOWS * CAP
SRC_DEV = 4096
ITERS = 8
N_CCD = 4
HIGH = 16
LOW = 256
STEP_BLOCKS = 16
EARLY = 5
STEPS = NBLK // STEP_BLOCKS

KNOT_PRIOR = 1.0
SOURCE_PRIOR = 1.0
PAIR_LIST = [(first, second) for first in range(5) for second in range(first, 5)]
ATT_PAIRS = [(first, second) for first in range(4) for second in range(first, 4)]
RHS_AT = 70
BIN_AT = 86
FEATS = 88

F32 = jnp.float32
BF16 = jnp.bfloat16
NT = (((1,), (1,)), ((), ()))
NN = (((1,), (0,)), ((), ()))

PIECES = np.array([[1, 0, 0, 0], [4, 12, 6, 1], [1, 6, 12, 4], [0, 0, 0, 1]], np.int64)
SPLINE = PIECES / 6.0


def knot_matrix():
    pair_at = {}
    for at, (first, second) in enumerate(ATT_PAIRS):
        pair_at[first, second] = pair_at[second, first] = at
    table = np.zeros((120, 4 * FEATS), np.float64)
    for d in range(-3, 4):
        for p in range(4):
            for q in range(4):
                row = ((d + 3) * 4 + p) * 4 + q
                for l in range(4):
                    j = l - d
                    if 0 <= j < 4:
                        for m, value in enumerate(np.convolve(PIECES[j], PIECES[l])):
                            table[row, l * FEATS + m * 10 + pair_at[q, p]] += value
    for q in range(4):
        for j in range(4):
            table[112 + q, j * FEATS + RHS_AT + 4 * j + q] = 36.0
            table[116 + q, j * FEATS + RHS_AT + 4 * j + q] = 36.0
    return table.astype(ml_dtypes.bfloat16)


def split_parts(values, count):
    parts = []
    for at in range(count):
        part = values.astype(BF16)
        parts.append(part)
        if at + 1 < count:
            values = values - part.astype(F32)
    return parts


def exact_dot(values, ones, dims, swap=False):
    total = None
    for part in split_parts(values, 3):
        pair = (ones, part) if swap else (part, ones)
        piece = lax.dot_general(*pair, dims, preferred_element_type=F32)
        total = piece if total is None else total + piece
    return total


def indicator(condition):
    return jnp.where(condition, 1.0, 0.0).astype(BF16)


def iota(shape, axis):
    return lax.broadcasted_iota(jnp.int32, shape, axis)


def iota_f(shape, axis):
    return iota(shape, axis).astype(F32)


def normals_kernel(*refs):
    given, (send_ref, obs_ref, slot_ref, marked_ref), here = refs[:6], refs[6:10], refs[10:16]
    pay_ref, done_ref = refs[16:]
    bin_ref, rows_ref, phase_ref, att_ref, resid_ref, source_ref = here
    copies = [pltpu.make_async_copy(given[at], here[at], done_ref.at[at]) for at in range(6)]
    for copy in copies:
        copy.start()
    square = (NBLK, NBLK)
    copies[0].wait()
    bins = bin_ref[...].astype(F32)
    window = jnp.floor((bins + 0.5) * (1.0 / BINS_W))
    local_bin = bins - BINS_W * window
    window_column = jnp.broadcast_to(window, square).T
    earlier = jnp.where(window_column == window, 1.0, 0.0) * jnp.where(iota(square, 0) < iota(square, 1), 1.0, 0.0)
    rank = jnp.sum(earlier, axis=0, keepdims=True)
    slot_ref[...] = jnp.concatenate([window, rank, jnp.zeros((6, NBLK), F32)], axis=0)
    place = indicator(iota_f((SLOTS, NBLK), 0) == CAP * window + rank)
    copies[1].wait()
    mask = iota(square, 0) < rows_ref[...]
    used = jnp.broadcast_to(rows_ref[...].astype(F32), square).T
    for copy in copies[2:]:
        copy.wait()
    marked_ref[...] = jnp.where(iota_f(square, 1) < used, source_ref[...], -LOW)
    u = phase_ref[...].T
    resid = jnp.where(mask, resid_ref[...].T, 0.0)
    att = [jnp.where(mask, att_ref[pl.ds(q, NBLK, stride=4), :].T, 0.0) for q in range(4)]
    obs_ref[0:128, :] = u
    obs_ref[128:256, :] = resid
    for q in range(4):
        obs_ref[256 + 128 * q : 384 + 128 * q, :] = att[q]
    v = 1.0 - u
    u2, v2 = u * u, v * v
    u3, v3 = u2 * u, v2 * v
    cubes = [v3, u * v2, u2 * v, u3]
    powers = [v3 * v3, u * v2 * v3, u2 * v2 * v2, u3 * v3, u2 * u2 * v2, u3 * u2 * v, u3 * u3]
    for at, (first, second) in enumerate(ATT_PAIRS):
        product = att[first] * att[second]
        for m in range(7):
            row = m * 10 + at
            pay_ref[row : row + 1, :] = jnp.sum(powers[m] * product, axis=0, keepdims=True)
    for q in range(4):
        product = att[q] * resid
        sums = [jnp.sum(cubes[i] * product, axis=0, keepdims=True) for i in range(4)]
        for j in range(4):
            total = None
            for i in range(4):
                if SPLINE[j, i] != 0.0:
                    piece = float(SPLINE[j, i]) * sums[i]
                    total = piece if total is None else total + piece
            row = RHS_AT + 4 * j + q
            pay_ref[row : row + 1, :] = total
    pay_ref[BIN_AT : BIN_AT + 1, :] = local_bin
    pay_ref[BIN_AT + 1 :, :] = jnp.zeros((NBLK - BIN_AT - 1, NBLK), F32)
    send_ref[...] = exact_dot(pay_ref[...], place, NT, swap=True)


def bins_kernel(got_ref, out_ref):
    got = got_ref[...].T
    place = indicator(iota_f((KNOTS_W, SLOTS), 0) == got[BIN_AT : BIN_AT + 1, :])
    out_ref[...] = exact_dot(got[:FEATS], place, NT)


def attitude_kernel(own_ref, one_ref, two_ref, three_ref, got_ref, table_ref, *rest):
    att_ref, reply_ref = rest[1:3]
    total = ((own_ref[...] + two_ref[...]) + (one_ref[...] + three_ref[...])) * (1.0 / 36.0)
    moved = jnp.concatenate([total] + [pltpu.roll(total, l, 1) for l in range(1, 4)], axis=0)
    band = exact_dot(moved, table_ref[...], NN, swap=True)
    groups = [band[8 * at : 8 * at + 8] for at in range(14)]
    lower_half = iota((8, KNOTS_W), 0) < 4

    def doubled(values):
        return values + pltpu.roll(values, 4, 0)

    def norm(values):
        return jnp.sum(jnp.sum(values, axis=1, keepdims=True), axis=0, keepdims=True)

    def apply(vector):
        spread = [
            jnp.where(lower_half, vector[2 * at : 2 * at + 1, :], vector[2 * at + 1 : 2 * at + 2, :]) for at in range(2)
        ]
        pieces = []
        for d in range(-3, 4):
            piece = groups[2 * (d + 3)] * spread[0] + groups[2 * (d + 3) + 1] * spread[1]
            pieces.append(pltpu.roll(piece, -d % KNOTS_W, 1) if d else piece)
        outer = (pieces[0] + pieces[1]) + (pieces[2] + pieces[4])
        return KNOT_PRIOR * vector + doubled(outer + ((pieces[5] + pieces[6]) + pieces[3]))

    residual = band[112:120]
    direction = residual
    estimate = jnp.zeros_like(residual)
    for iteration in range(ITERS):
        applied = apply(direction)
        norm_now = norm(residual * residual)
        inverse = 1.0 / norm(direction * applied)
        across = norm(residual * applied)
        applied_norm = norm(applied * applied)
        step_size = norm_now * inverse
        estimate = estimate + step_size * direction
        residual = residual - step_size * applied
        if iteration + 1 < ITERS:
            ratio = 1.0 - 2.0 * (across * inverse) + step_size * (applied_norm * inverse)
            direction = residual + ratio * direction
    att_ref[0] = estimate[:4]
    moved = jnp.concatenate([estimate[:4]] + [pltpu.roll(estimate, KNOTS_W - j, 1)[:4] for j in range(1, 4)], axis=0)
    column = jnp.concatenate(
        [got_ref[pl.ds(s, WINDOWS, stride=CAP), :][:, BIN_AT : BIN_AT + 1] for s in range(CAP)], axis=0
    )
    place = indicator(iota_f((SLOTS, KNOTS_W), 1) == column)
    knots = exact_dot(moved, place, NT, swap=True)
    reply_ref[...] = jnp.zeros((WINDOWS, 128), F32)
    for s in range(CAP):
        reply_ref[:, 16 * s : 16 * s + 16] = knots[WINDOWS * s : WINDOWS * s + WINDOWS]


def source_sums(count, terms_ref, high_ref, low_ref, out_ref, acc_ref, *buffers):
    high_at = iota_f((HIGH, ROWS), 0)
    low_at = iota_f((LOW, ROWS), 0).astype(BF16)
    one, zero = jnp.ones((), BF16), jnp.zeros((), BF16)

    def build(at, slot):
        a_ref, b_ref = buffers[slot], buffers[2 + slot]
        for inner in range(STEP_BLOCKS):
            block = at * STEP_BLOCKS + inner
            lanes = slice(inner * ROWS, inner * ROWS + ROWS)
            here = high_at == high_ref[pl.ds(block, 1), :]
            low = jnp.broadcast_to(low_ref[pl.ds(block, 1), :], (HIGH, ROWS)).astype(BF16)
            low = jnp.concatenate([low] * (LOW // HIGH), axis=0)
            b_ref[:, lanes] = jnp.where(low_at == low, one, zero)
            for c in range(2 * count):
                term = jnp.where(here, terms_ref[pl.ds(c * NBLK + block, 1), :], 0.0)
                a_ref[c * HIGH : (c + 1) * HIGH, lanes] = term.astype(BF16)

    def multiply(slot):
        acc_ref[...] += lax.dot_general(buffers[2 + slot][...], buffers[slot][...], NT, preferred_element_type=F32)

    def step(pair, carry):
        multiply(0)
        build(2 * pair + 1, 1)
        multiply(1)
        build(2 * pair + 2, 0)
        return carry

    acc_ref[...] = jnp.zeros(acc_ref.shape, F32)
    build(0, 0)
    lax.fori_loop(0, STEPS // 2 - 1, step, 0)
    multiply(0)
    build(STEPS - 1, 1)
    multiply(1)
    sums = acc_ref[...].T
    for c in range(count):
        at = 2 * c * HIGH
        out_ref[HIGH * c : HIGH * c + HIGH, :] = sums[at : at + HIGH] + sums[at + HIGH : at + 2 * HIGH]


def put_terms(terms_ref, c, values):
    large = values.astype(BF16).astype(F32)
    terms_ref[2 * c * NBLK : (2 * c + 1) * NBLK, :] = large
    terms_ref[(2 * c + 1) * NBLK : (2 * c + 2) * NBLK, :] = values - large


def put_sources(marked_ref, high_ref, low_ref):
    source = marked_ref[...]
    high = source >> 8
    high_ref[...] = high.astype(F32)
    low_ref[...] = (source - (high << 8)).astype(F32)


def put_pairs(gain_ref, terms_ref, pairs):
    gains = [gain_ref[NBLK * p : NBLK * p + NBLK, :] for p in range(5)]
    for at, (first, second) in enumerate(pairs):
        put_terms(terms_ref, at, gains[first] * gains[second])


def early_normals_kernel(marked_ref, gain_ref, out_ref, terms_ref, high_ref, low_ref, *work):
    put_sources(marked_ref, high_ref, low_ref)
    put_pairs(gain_ref, terms_ref, PAIR_LIST[:EARLY])
    source_sums(EARLY, terms_ref, high_ref, low_ref, out_ref, *work)


def rest_normals_kernel(marked_ref, gain_ref, early_ref, after_ref, out_ref, done_ref, terms_ref, high_ref, low_ref, *work):
    copy = pltpu.make_async_copy(early_ref, out_ref.at[: HIGH * EARLY], done_ref)
    copy.start()
    put_sources(marked_ref, high_ref, low_ref)
    put_pairs(gain_ref, terms_ref, PAIR_LIST[EARLY:])
    source_sums(15 - EARLY, terms_ref, high_ref, low_ref, out_ref.at[HIGH * EARLY :], *work)
    copy.wait()


def source_right_kernel(
    reply_ref, slot_ref, obs_ref, marked_ref, gain_ref, out_ref, terms_ref, high_ref, low_ref, *work
):
    put_sources(marked_ref, high_ref, low_ref)
    place = indicator(iota_f((WINDOWS, NBLK), 0) == slot_ref[0:1, :])
    rank = slot_ref[1:2, :]
    spread = exact_dot(reply_ref[...].T, place, NN)
    knots = None
    for s in range(CAP):
        piece = jnp.where(rank == float(s), spread[16 * s : 16 * s + 16, :], 0.0)
        knots = piece if knots is None else knots + piece
    u = obs_ref[0:128, :]
    att = [obs_ref[256 + 128 * q : 384 + 128 * q, :] for q in range(4)]
    v = 1.0 - u
    u2, v2 = u * u, v * v
    cubes = [v2 * v, u * v2, u2 * v, u2 * u]
    values = obs_ref[128:256, :]
    for j in range(4):
        spline = None
        for i in range(4):
            if SPLINE[j, i] != 0.0:
                piece = float(SPLINE[j, i]) * cubes[i]
                spline = piece if spline is None else spline + piece
        inner = None
        for q in range(4):
            piece = att[q] * knots[4 * j + q : 4 * j + q + 1, :]
            inner = piece if inner is None else inner + piece
        values = values - spline * inner
    values = values.T
    for p in range(5):
        put_terms(terms_ref, p, gain_ref[NBLK * p : NBLK * p + NBLK, :] * values)
    source_sums(5, terms_ref, high_ref, low_ref, out_ref, *work)


def factor_kernel(own_ref, one_ref, two_ref, three_ref, out_ref):
    entries = {}
    for at, pair in enumerate(PAIR_LIST):
        rows = slice(HIGH * at, HIGH * at + HIGH)
        total = (own_ref[rows, :] + two_ref[rows, :]) + (one_ref[rows, :] + three_ref[rows, :])
        entries[pair] = total + SOURCE_PRIOR if pair[0] == pair[1] else total
    lower = {}
    for column in range(5):
        pivot = entries[column, column]
        for before in range(column):
            pivot = pivot - lower[column, before] * lower[column, before]
        inverse = 1.0 / jnp.sqrt(pivot)
        lower[column, column] = inverse
        for row in range(column + 1, 5):
            running = entries[column, row]
            for before in range(column):
                running = running - lower[row, before] * lower[column, before]
            lower[row, column] = running * inverse
    for at, (first, second) in enumerate(PAIR_LIST):
        out_ref[HIGH * at : HIGH * at + HIGH, :] = lower[second, first]


def solve_kernel(factor_ref, own_ref, one_ref, two_ref, three_ref, out_ref):
    lower = {}
    for at, (first, second) in enumerate(PAIR_LIST):
        lower[second, first] = factor_ref[HIGH * at : HIGH * at + HIGH, :]
    values = []
    for row in range(5):
        rows = slice(HIGH * row, HIGH * row + HIGH)
        running = (own_ref[rows, :] + two_ref[rows, :]) + (one_ref[rows, :] + three_ref[rows, :])
        for before in range(row):
            running = running - lower[row, before] * values[before]
        values.append(running * lower[row, row])
    for row in reversed(range(5)):
        running = values[row]
        for later in range(row + 1, 5):
            running = running - lower[later, row] * values[later]
        values[row] = running * lower[row, row]
    for row in range(5):
        for high in range(HIGH):
            out_ref[row : row + 1, LOW * high : LOW * high + LOW] = values[row][high : high + 1, :]


def f32(*shape):
    return jax.ShapeDtypeStruct(shape, F32)


def kernel_call(body, name, outs, *args, scratch=(), flops=1_000_000, far=(), grant=32, passed=None):
    passed = passed or {}
    place = [pl.ANY if at in far else pltpu.MemorySpace.VMEM for at in range(len(args))]
    out_place = [pl.ANY if at in passed.values() else pltpu.MemorySpace.VMEM for at in range(len(jax.tree.leaves(outs)))]
    out_specs = [pl.BlockSpec(memory_space=at) for at in out_place]
    size = sum(math.prod(a.shape) * 4 for a in args)
    return pl.pallas_call(
        body,
        out_shape=outs,
        in_specs=[pl.BlockSpec(memory_space=at) for at in place],
        out_specs=tuple(out_specs) if isinstance(outs, tuple) else out_specs[0],
        input_output_aliases=passed,
        scratch_shapes=list(scratch),
        compiler_params=pltpu.CompilerParams(vmem_limit_bytes=grant * 1024 * 1024),
        cost_estimate=pl.CostEstimate(flops=flops, bytes_accessed=size, transcendentals=0),
        name=name,
    )(*args)


def segment_scratch(count):
    return (
        pltpu.VMEM((2 * count * NBLK, ROWS), F32),
        pltpu.VMEM((NBLK, ROWS), F32),
        pltpu.VMEM((NBLK, ROWS), F32),
        pltpu.VMEM((LOW, 2 * count * HIGH), F32),
        pltpu.VMEM((2 * count * HIGH, STEP_BLOCKS * ROWS), BF16),
        pltpu.VMEM((2 * count * HIGH, STEP_BLOCKS * ROWS), BF16),
        pltpu.VMEM((LOW, STEP_BLOCKS * ROWS), BF16),
        pltpu.VMEM((LOW, STEP_BLOCKS * ROWS), BF16),
    )


def from_others(values):
    return [
        lax.ppermute(values, "ccd", [(at, (at + shift) % N_CCD) for at in range(N_CCD)]) for shift in range(1, N_CCD)
    ]


def to_windows(values):
    return lax.all_to_all(values, ("src", "win"), split_axis=0, concat_axis=0, tiled=True)


def local(block_bin, block_rows, row_source, obs_resid, obs_phase, att_partial, src_partial):
    bins = block_bin.reshape(1, NBLK)
    rows = block_rows.reshape(1, NBLK)
    gains = jnp.transpose(src_partial, (1, 0, 2)).reshape(5 * NBLK, ROWS)
    send, obs, slots, marked = kernel_call(
        normals_kernel,
        "normals",
        (f32(SLOTS, 128), f32(6 * ROWS, NBLK), f32(8, NBLK), jax.ShapeDtypeStruct((NBLK, ROWS), jnp.int32)),
        bins,
        rows,
        obs_phase,
        att_partial.reshape(4 * NBLK, ROWS),
        obs_resid,
        row_source,
        scratch=(
            pltpu.VMEM((1, NBLK), jnp.int32),
            pltpu.VMEM((1, NBLK), jnp.int32),
            pltpu.VMEM((NBLK, ROWS), F32),
            pltpu.VMEM((4 * NBLK, ROWS), F32),
            pltpu.VMEM((NBLK, ROWS), F32),
            pltpu.VMEM((NBLK, ROWS), jnp.int32),
            pltpu.VMEM((NBLK, NBLK), F32),
            pltpu.SemaphoreType.DMA((6,)),
        ),
        far=range(6),
        grant=56,
    )
    got = to_windows(send.reshape(WINDOWS, CAP, 128)).reshape(SLOTS, 128)
    early = kernel_call(
        early_normals_kernel,
        "early_normals",
        f32(EARLY * HIGH, LOW),
        marked,
        gains,
        scratch=segment_scratch(EARLY),
        flops=2 * 32 * EARLY * 256 * 16384,
    )
    moments = kernel_call(bins_kernel, "bins", f32(FEATS, KNOTS_W), got)
    normal = kernel_call(
        rest_normals_kernel,
        "rest_normals",
        f32(15 * HIGH, LOW),
        marked,
        gains,
        early,
        moments,
        scratch=(pltpu.SemaphoreType.DMA, *segment_scratch(15 - EARLY)),
        flops=2 * 32 * (15 - EARLY) * 256 * 16384,
        far=(2, 3),
    )
    attitude, reply, normal = kernel_call(
        attitude_kernel,
        "attitude",
        (f32(1, 4, KNOTS_W), f32(WINDOWS, 128), f32(15 * HIGH, LOW)),
        moments,
        *from_others(moments),
        got,
        jnp.asarray(knot_matrix()),
        normal,
        far=(6,),
        passed={6: 2},
    )
    knots = to_windows(reply)
    factors = kernel_call(factor_kernel, "factors", f32(15 * HIGH, LOW), normal, *from_others(normal))
    right = kernel_call(
        source_right_kernel,
        "source_right",
        f32(5 * HIGH, LOW),
        knots,
        slots,
        obs,
        marked,
        gains,
        scratch=segment_scratch(5),
        flops=2 * 160 * 256 * 16384,
    )
    source_delta = kernel_call(solve_kernel, "solve", f32(5, SRC_DEV), factors, right, *from_others(right))
    return attitude, source_delta


def solution(mesh):
    return jax.shard_map(
        local,
        mesh=mesh,
        in_specs=(
            P(("src", "win", "ccd")),
            P(("src", "win", "ccd")),
            P(("src", "win", "ccd"), None),
            P(("src", "win", "ccd"), None),
            P(("src", "win", "ccd"), None),
            P(("src", "win", "ccd"), None, None),
            P(("src", "win", "ccd"), None, None),
        ),
        out_specs=(P(("src", "win"), None, None), P(None, ("src", "win"))),
        check_vma=False,
    )
```

```python
import math

import jax
import jax.numpy as jnp
import ml_dtypes
import numpy as np
from jax import lax
from jax.experimental import pallas as pl
from jax.experimental.pallas import tpu as pltpu
from jax.sharding import PartitionSpec as P

KNOTS_W = 128
BINS_W = 125
NBLK = 128
ROWS = 128
WINDOWS = 64
CAP = 4
SLOTS = WINDOWS * CAP
SRC_DEV = 4096
ITERS = 8
N_CCD = 4
HIGH = 16
LOW = 256
STEP_BLOCKS = 16
STEPS = NBLK // STEP_BLOCKS

KNOT_PRIOR = 1.0
SOURCE_PRIOR = 1.0
PAIR_LIST = [(first, second) for first in range(5) for second in range(first, 5)]
ATT_PAIRS = [(first, second) for first in range(4) for second in range(first, 4)]
RHS_AT = 70
BIN_AT = 86
FEATS = 88

F32 = jnp.float32
BF16 = jnp.bfloat16
NT = (((1,), (1,)), ((), ()))
NN = (((1,), (0,)), ((), ()))

PIECES = np.array([[1, 0, 0, 0], [4, 12, 6, 1], [1, 6, 12, 4], [0, 0, 0, 1]], np.int64)
SPLINE = PIECES / 6.0


def knot_matrix():
    pair_at = {}
    for at, (first, second) in enumerate(ATT_PAIRS):
        pair_at[first, second] = pair_at[second, first] = at
    table = np.zeros((120, 4 * FEATS), np.float64)
    for d in range(-3, 4):
        for p in range(4):
            for q in range(4):
                row = ((d + 3) * 4 + p) * 4 + q
                for l in range(4):
                    j = l - d
                    if 0 <= j < 4:
                        for m, value in enumerate(np.convolve(PIECES[j], PIECES[l])):
                            table[row, l * FEATS + m * 10 + pair_at[q, p]] += value
    for q in range(4):
        for j in range(4):
            table[112 + q, j * FEATS + RHS_AT + 4 * j + q] = 36.0
            table[116 + q, j * FEATS + RHS_AT + 4 * j + q] = 36.0
    return table.astype(ml_dtypes.bfloat16)


def split_parts(values, count):
    parts = []
    for at in range(count):
        part = values.astype(BF16)
        parts.append(part)
        if at + 1 < count:
            values = values - part.astype(F32)
    return parts


def exact_dot(values, ones, dims, swap=False):
    total = None
    for part in split_parts(values, 3):
        pair = (ones, part) if swap else (part, ones)
        piece = lax.dot_general(*pair, dims, preferred_element_type=F32)
        total = piece if total is None else total + piece
    return total


def indicator(condition):
    return jnp.where(condition, 1.0, 0.0).astype(BF16)


def iota(shape, axis):
    return lax.broadcasted_iota(jnp.int32, shape, axis)


def iota_f(shape, axis):
    return iota(shape, axis).astype(F32)


def normals_kernel(*refs):
    given, (send_ref, obs_ref, slot_ref, marked_ref), here = refs[:6], refs[6:10], refs[10:16]
    pay_ref, done_ref = refs[16:]
    bin_ref, rows_ref, phase_ref, att_ref, resid_ref, source_ref = here
    copies = [pltpu.make_async_copy(given[at], here[at], done_ref.at[at]) for at in range(6)]
    for copy in copies:
        copy.start()
    square = (NBLK, NBLK)
    copies[0].wait()
    bins = bin_ref[...].astype(F32)
    window = jnp.floor((bins + 0.5) * (1.0 / BINS_W))
    local_bin = bins - BINS_W * window
    window_column = jnp.broadcast_to(window, square).T
    earlier = jnp.where(window_column == window, 1.0, 0.0) * jnp.where(iota(square, 0) < iota(square, 1), 1.0, 0.0)
    rank = jnp.sum(earlier, axis=0, keepdims=True)
    slot_ref[...] = jnp.concatenate([window, rank, jnp.zeros((6, NBLK), F32)], axis=0)
    place = indicator(iota_f((SLOTS, NBLK), 0) == CAP * window + rank)
    copies[1].wait()
    mask = iota(square, 0) < rows_ref[...]
    used = jnp.broadcast_to(rows_ref[...].astype(F32), square).T
    for copy in copies[2:]:
        copy.wait()
    marked_ref[...] = jnp.where(iota_f(square, 1) < used, source_ref[...], -LOW)
    u = phase_ref[...].T
    resid = jnp.where(mask, resid_ref[...].T, 0.0)
    att = [jnp.where(mask, att_ref[pl.ds(q, NBLK, stride=4), :].T, 0.0) for q in range(4)]
    obs_ref[0:128, :] = u
    obs_ref[128:256, :] = resid
    for q in range(4):
        obs_ref[256 + 128 * q : 384 + 128 * q, :] = att[q]
    v = 1.0 - u
    u2, v2 = u * u, v * v
    u3, v3 = u2 * u, v2 * v
    cubes = [v3, u * v2, u2 * v, u3]
    powers = [v3 * v3, u * v2 * v3, u2 * v2 * v2, u3 * v3, u2 * u2 * v2, u3 * u2 * v, u3 * u3]
    for at, (first, second) in enumerate(ATT_PAIRS):
        product = att[first] * att[second]
        for m in range(7):
            row = m * 10 + at
            pay_ref[row : row + 1, :] = jnp.sum(powers[m] * product, axis=0, keepdims=True)
    for q in range(4):
        product = att[q] * resid
        sums = [jnp.sum(cubes[i] * product, axis=0, keepdims=True) for i in range(4)]
        for j in range(4):
            total = None
            for i in range(4):
                if SPLINE[j, i] != 0.0:
                    piece = float(SPLINE[j, i]) * sums[i]
                    total = piece if total is None else total + piece
            row = RHS_AT + 4 * j + q
            pay_ref[row : row + 1, :] = total
    pay_ref[BIN_AT : BIN_AT + 1, :] = local_bin
    pay_ref[BIN_AT + 1 :, :] = jnp.zeros((NBLK - BIN_AT - 1, NBLK), F32)
    send_ref[...] = exact_dot(pay_ref[...], place, NT, swap=True)


def bins_kernel(got_ref, after_ref, out_ref):
    del after_ref
    got = got_ref[...].T
    place = indicator(iota_f((KNOTS_W, SLOTS), 0) == got[BIN_AT : BIN_AT + 1, :])
    out_ref[...] = exact_dot(got[:FEATS], place, NT)


def attitude_kernel(own_ref, one_ref, two_ref, three_ref, got_ref, table_ref, att_ref, reply_ref):
    total = ((own_ref[...] + two_ref[...]) + (one_ref[...] + three_ref[...])) * (1.0 / 36.0)
    moved = jnp.concatenate([total] + [pltpu.roll(total, l, 1) for l in range(1, 4)], axis=0)
    band = exact_dot(moved, table_ref[...], NN, swap=True)
    groups = [band[8 * at : 8 * at + 8] for at in range(14)]
    lower_half = iota((8, KNOTS_W), 0) < 4

    def doubled(values):
        return values + pltpu.roll(values, 4, 0)

    def norm(values):
        return jnp.sum(jnp.sum(values, axis=1, keepdims=True), axis=0, keepdims=True)

    def apply(vector):
        spread = [
            jnp.where(lower_half, vector[2 * at : 2 * at + 1, :], vector[2 * at + 1 : 2 * at + 2, :]) for at in range(2)
        ]
        pieces = []
        for d in range(-3, 4):
            piece = groups[2 * (d + 3)] * spread[0] + groups[2 * (d + 3) + 1] * spread[1]
            pieces.append(pltpu.roll(piece, -d % KNOTS_W, 1) if d else piece)
        outer = (pieces[0] + pieces[1]) + (pieces[2] + pieces[4])
        return KNOT_PRIOR * vector + doubled(outer + ((pieces[5] + pieces[6]) + pieces[3]))

    residual = band[112:120]
    direction = residual
    estimate = jnp.zeros_like(residual)
    for iteration in range(ITERS):
        applied = apply(direction)
        norm_now = norm(residual * residual)
        inverse = 1.0 / norm(direction * applied)
        across = norm(residual * applied)
        applied_norm = norm(applied * applied)
        step_size = norm_now * inverse
        estimate = estimate + step_size * direction
        residual = residual - step_size * applied
        if iteration + 1 < ITERS:
            ratio = 1.0 - 2.0 * (across * inverse) + step_size * (applied_norm * inverse)
            direction = residual + ratio * direction
    att_ref[0] = estimate[:4]
    moved = jnp.concatenate([estimate[:4]] + [pltpu.roll(estimate, KNOTS_W - j, 1)[:4] for j in range(1, 4)], axis=0)
    column = jnp.concatenate(
        [got_ref[pl.ds(s, WINDOWS, stride=CAP), :][:, BIN_AT : BIN_AT + 1] for s in range(CAP)], axis=0
    )
    place = indicator(iota_f((SLOTS, KNOTS_W), 1) == column)
    knots = exact_dot(moved, place, NT, swap=True)
    reply_ref[...] = jnp.zeros((WINDOWS, 128), F32)
    for s in range(CAP):
        reply_ref[:, 16 * s : 16 * s + 16] = knots[WINDOWS * s : WINDOWS * s + WINDOWS]


def source_sums(count, terms_ref, high_ref, low_ref, out_ref, acc_ref, *buffers):
    high_at = iota_f((HIGH, ROWS), 0)
    low_at = iota_f((LOW, ROWS), 0).astype(BF16)
    one, zero = jnp.ones((), BF16), jnp.zeros((), BF16)

    def build(at, slot):
        a_ref, b_ref = buffers[slot], buffers[2 + slot]
        for inner in range(STEP_BLOCKS):
            block = at * STEP_BLOCKS + inner
            lanes = slice(inner * ROWS, inner * ROWS + ROWS)
            here = high_at == high_ref[pl.ds(block, 1), :]
            low = jnp.broadcast_to(low_ref[pl.ds(block, 1), :], (HIGH, ROWS)).astype(BF16)
            low = jnp.concatenate([low] * (LOW // HIGH), axis=0)
            b_ref[:, lanes] = jnp.where(low_at == low, one, zero)
            for c in range(2 * count):
                term = jnp.where(here, terms_ref[pl.ds(c * NBLK + block, 1), :], 0.0)
                a_ref[c * HIGH : (c + 1) * HIGH, lanes] = term.astype(BF16)

    def multiply(slot):
        acc_ref[...] += lax.dot_general(buffers[2 + slot][...], buffers[slot][...], NT, preferred_element_type=F32)

    def step(pair, carry):
        multiply(0)
        build(2 * pair + 1, 1)
        multiply(1)
        build(2 * pair + 2, 0)
        return carry

    acc_ref[...] = jnp.zeros(acc_ref.shape, F32)
    build(0, 0)
    lax.fori_loop(0, STEPS // 2 - 1, step, 0)
    multiply(0)
    build(STEPS - 1, 1)
    multiply(1)
    sums = acc_ref[...].T
    for c in range(count):
        at = 2 * c * HIGH
        out_ref[HIGH * c : HIGH * c + HIGH, :] = sums[at : at + HIGH] + sums[at + HIGH : at + 2 * HIGH]


def put_terms(terms_ref, c, values):
    large = values.astype(BF16).astype(F32)
    terms_ref[2 * c * NBLK : (2 * c + 1) * NBLK, :] = large
    terms_ref[(2 * c + 1) * NBLK : (2 * c + 2) * NBLK, :] = values - large


def put_sources(marked_ref, high_ref, low_ref):
    source = marked_ref[...]
    high = source >> 8
    high_ref[...] = high.astype(F32)
    low_ref[...] = (source - (high << 8)).astype(F32)


def source_normals_kernel(marked_ref, gain_ref, out_ref, terms_ref, high_ref, low_ref, *work):
    put_sources(marked_ref, high_ref, low_ref)
    gains = [gain_ref[NBLK * p : NBLK * p + NBLK, :] for p in range(5)]
    for at, (first, second) in enumerate(PAIR_LIST):
        put_terms(terms_ref, at, gains[first] * gains[second])
    source_sums(15, terms_ref, high_ref, low_ref, out_ref, *work)


def source_right_kernel(
    reply_ref, slot_ref, obs_ref, marked_ref, gain_ref, out_ref, terms_ref, high_ref, low_ref, *work
):
    put_sources(marked_ref, high_ref, low_ref)
    place = indicator(iota_f((WINDOWS, NBLK), 0) == slot_ref[0:1, :])
    rank = slot_ref[1:2, :]
    spread = exact_dot(reply_ref[...].T, place, NN)
    knots = None
    for s in range(CAP):
        piece = jnp.where(rank == float(s), spread[16 * s : 16 * s + 16, :], 0.0)
        knots = piece if knots is None else knots + piece
    u = obs_ref[0:128, :]
    att = [obs_ref[256 + 128 * q : 384 + 128 * q, :] for q in range(4)]
    v = 1.0 - u
    u2, v2 = u * u, v * v
    cubes = [v2 * v, u * v2, u2 * v, u2 * u]
    values = obs_ref[128:256, :]
    for j in range(4):
        spline = None
        for i in range(4):
            if SPLINE[j, i] != 0.0:
                piece = float(SPLINE[j, i]) * cubes[i]
                spline = piece if spline is None else spline + piece
        inner = None
        for q in range(4):
            piece = att[q] * knots[4 * j + q : 4 * j + q + 1, :]
            inner = piece if inner is None else inner + piece
        values = values - spline * inner
    values = values.T
    for p in range(5):
        put_terms(terms_ref, p, gain_ref[NBLK * p : NBLK * p + NBLK, :] * values)
    source_sums(5, terms_ref, high_ref, low_ref, out_ref, *work)


def factor_kernel(own_ref, one_ref, two_ref, three_ref, out_ref):
    entries = {}
    for at, pair in enumerate(PAIR_LIST):
        rows = slice(HIGH * at, HIGH * at + HIGH)
        total = (own_ref[rows, :] + two_ref[rows, :]) + (one_ref[rows, :] + three_ref[rows, :])
        entries[pair] = total + SOURCE_PRIOR if pair[0] == pair[1] else total
    lower = {}
    for column in range(5):
        pivot = entries[column, column]
        for before in range(column):
            pivot = pivot - lower[column, before] * lower[column, before]
        inverse = 1.0 / jnp.sqrt(pivot)
        lower[column, column] = inverse
        for row in range(column + 1, 5):
            running = entries[column, row]
            for before in range(column):
                running = running - lower[row, before] * lower[column, before]
            lower[row, column] = running * inverse
    for at, (first, second) in enumerate(PAIR_LIST):
        out_ref[HIGH * at : HIGH * at + HIGH, :] = lower[second, first]


def solve_kernel(factor_ref, own_ref, one_ref, two_ref, three_ref, out_ref):
    lower = {}
    for at, (first, second) in enumerate(PAIR_LIST):
        lower[second, first] = factor_ref[HIGH * at : HIGH * at + HIGH, :]
    values = []
    for row in range(5):
        rows = slice(HIGH * row, HIGH * row + HIGH)
        running = (own_ref[rows, :] + two_ref[rows, :]) + (one_ref[rows, :] + three_ref[rows, :])
        for before in range(row):
            running = running - lower[row, before] * values[before]
        values.append(running * lower[row, row])
    for row in reversed(range(5)):
        running = values[row]
        for later in range(row + 1, 5):
            running = running - lower[later, row] * values[later]
        values[row] = running * lower[row, row]
    for row in range(5):
        for high in range(HIGH):
            out_ref[row : row + 1, LOW * high : LOW * high + LOW] = values[row][high : high + 1, :]


def f32(*shape):
    return jax.ShapeDtypeStruct(shape, F32)


def kernel_call(body, name, outs, *args, scratch=(), flops=1_000_000, far=(), grant=32, passed=None):
    passed = passed or {}
    place = [pl.ANY if at in far else pltpu.MemorySpace.VMEM for at in range(len(args))]
    out_place = [pl.ANY if at in passed.values() else pltpu.MemorySpace.VMEM for at in range(len(jax.tree.leaves(outs)))]
    out_specs = [pl.BlockSpec(memory_space=at) for at in out_place]
    size = sum(math.prod(a.shape) * 4 for a in args)
    return pl.pallas_call(
        body,
        out_shape=outs,
        in_specs=[pl.BlockSpec(memory_space=at) for at in place],
        out_specs=tuple(out_specs) if isinstance(outs, tuple) else out_specs[0],
        input_output_aliases=passed,
        scratch_shapes=list(scratch),
        compiler_params=pltpu.CompilerParams(vmem_limit_bytes=grant * 1024 * 1024),
        cost_estimate=pl.CostEstimate(flops=flops, bytes_accessed=size, transcendentals=0),
        name=name,
    )(*args)


def segment_scratch(count):
    return (
        pltpu.VMEM((2 * count * NBLK, ROWS), F32),
        pltpu.VMEM((NBLK, ROWS), F32),
        pltpu.VMEM((NBLK, ROWS), F32),
        pltpu.VMEM((LOW, 2 * count * HIGH), F32),
        pltpu.VMEM((2 * count * HIGH, STEP_BLOCKS * ROWS), BF16),
        pltpu.VMEM((2 * count * HIGH, STEP_BLOCKS * ROWS), BF16),
        pltpu.VMEM((LOW, STEP_BLOCKS * ROWS), BF16),
        pltpu.VMEM((LOW, STEP_BLOCKS * ROWS), BF16),
    )


def from_others(values):
    return [
        lax.ppermute(values, "ccd", [(at, (at + shift) % N_CCD) for at in range(N_CCD)]) for shift in range(1, N_CCD)
    ]


def to_windows(values):
    return lax.all_to_all(values, ("src", "win"), split_axis=0, concat_axis=0, tiled=True)


def local(block_bin, block_rows, row_source, obs_resid, obs_phase, att_partial, src_partial):
    bins = block_bin.reshape(1, NBLK)
    rows = block_rows.reshape(1, NBLK)
    gains = jnp.transpose(src_partial, (1, 0, 2)).reshape(5 * NBLK, ROWS)
    send, obs, slots, marked = kernel_call(
        normals_kernel,
        "normals",
        (f32(SLOTS, 128), f32(6 * ROWS, NBLK), f32(8, NBLK), jax.ShapeDtypeStruct((NBLK, ROWS), jnp.int32)),
        bins,
        rows,
        obs_phase,
        att_partial.reshape(4 * NBLK, ROWS),
        obs_resid,
        row_source,
        scratch=(
            pltpu.VMEM((1, NBLK), jnp.int32),
            pltpu.VMEM((1, NBLK), jnp.int32),
            pltpu.VMEM((NBLK, ROWS), F32),
            pltpu.VMEM((4 * NBLK, ROWS), F32),
            pltpu.VMEM((NBLK, ROWS), F32),
            pltpu.VMEM((NBLK, ROWS), jnp.int32),
            pltpu.VMEM((NBLK, NBLK), F32),
            pltpu.SemaphoreType.DMA((6,)),
        ),
        far=range(6),
        grant=56,
    )
    got = to_windows(send.reshape(WINDOWS, CAP, 128)).reshape(SLOTS, 128)
    normal = kernel_call(
        source_normals_kernel,
        "source_normals",
        f32(15 * HIGH, LOW),
        marked,
        gains,
        scratch=segment_scratch(15),
        flops=2 * 480 * 256 * 16384,
    )
    moments = kernel_call(bins_kernel, "bins", f32(FEATS, KNOTS_W), got, normal, far=(1,))
    attitude, reply = kernel_call(
        attitude_kernel,
        "attitude",
        (f32(1, 4, KNOTS_W), f32(WINDOWS, 128)),
        moments,
        *from_others(moments),
        got,
        jnp.asarray(knot_matrix()),
    )
    knots = to_windows(reply)
    factors = kernel_call(factor_kernel, "factors", f32(15 * HIGH, LOW), normal, *from_others(normal))
    right = kernel_call(
        source_right_kernel,
        "source_right",
        f32(5 * HIGH, LOW),
        knots,
        slots,
        obs,
        marked,
        gains,
        scratch=segment_scratch(5),
        flops=2 * 160 * 256 * 16384,
    )
    source_delta = kernel_call(solve_kernel, "solve", f32(5, SRC_DEV), factors, right, *from_others(right))
    return attitude, source_delta


def solution(mesh):
    return jax.shard_map(
        local,
        mesh=mesh,
        in_specs=(
            P(("src", "win", "ccd")),
            P(("src", "win", "ccd")),
            P(("src", "win", "ccd"), None),
            P(("src", "win", "ccd"), None),
            P(("src", "win", "ccd"), None),
            P(("src", "win", "ccd"), None, None),
            P(("src", "win", "ccd"), None, None),
        ),
        out_specs=(P(("src", "win"), None, None), P(None, ("src", "win"))),
        check_vma=False,
    )
```

```python
import math

import jax
import jax.numpy as jnp
import ml_dtypes
import numpy as np
from jax import lax
from jax.experimental import pallas as pl
from jax.experimental.pallas import tpu as pltpu
from jax.sharding import PartitionSpec as P

KNOTS_W = 128
BINS_W = 125
NBLK = 128
ROWS = 128
WINDOWS = 64
CAP = 4
SLOTS = WINDOWS * CAP
SRC_DEV = 4096
ITERS = 8
N_CCD = 4
HIGH = 16
LOW = 256
STEP_BLOCKS = 16
STEPS = NBLK // STEP_BLOCKS

KNOT_PRIOR = 1.0
SOURCE_PRIOR = 1.0
PAIR_LIST = [(first, second) for first in range(5) for second in range(first, 5)]
ATT_PAIRS = [(first, second) for first in range(4) for second in range(first, 4)]
RHS_AT = 70
BIN_AT = 86
FEATS = 88

F32 = jnp.float32
BF16 = jnp.bfloat16
NT = (((1,), (1,)), ((), ()))
NN = (((1,), (0,)), ((), ()))

PIECES = np.array([[1, 0, 0, 0], [4, 12, 6, 1], [1, 6, 12, 4], [0, 0, 0, 1]], np.int64)
SPLINE = PIECES / 6.0


def knot_matrix():
    pair_at = {}
    for at, (first, second) in enumerate(ATT_PAIRS):
        pair_at[first, second] = pair_at[second, first] = at
    table = np.zeros((120, 4 * FEATS), np.float64)
    for d in range(-3, 4):
        for p in range(4):
            for q in range(4):
                row = ((d + 3) * 4 + p) * 4 + q
                for l in range(4):
                    j = l - d
                    if 0 <= j < 4:
                        for m, value in enumerate(np.convolve(PIECES[j], PIECES[l])):
                            table[row, l * FEATS + m * 10 + pair_at[q, p]] += value
    for q in range(4):
        for j in range(4):
            table[112 + q, j * FEATS + RHS_AT + 4 * j + q] = 36.0
            table[116 + q, j * FEATS + RHS_AT + 4 * j + q] = 36.0
    return table.astype(ml_dtypes.bfloat16)


def split_parts(values, count):
    parts = []
    for at in range(count):
        part = values.astype(BF16)
        parts.append(part)
        if at + 1 < count:
            values = values - part.astype(F32)
    return parts


def exact_dot(values, ones, dims, swap=False):
    total = None
    for part in split_parts(values, 3):
        pair = (ones, part) if swap else (part, ones)
        piece = lax.dot_general(*pair, dims, preferred_element_type=F32)
        total = piece if total is None else total + piece
    return total


def indicator(condition):
    return jnp.where(condition, 1.0, 0.0).astype(BF16)


def iota(shape, axis):
    return lax.broadcasted_iota(jnp.int32, shape, axis)


def iota_f(shape, axis):
    return iota(shape, axis).astype(F32)


def normals_kernel(*refs):
    given, (send_ref, obs_ref, slot_ref, marked_ref), here = refs[:6], refs[6:10], refs[10:16]
    pay_ref, done_ref = refs[16:]
    bin_ref, rows_ref, phase_ref, att_ref, resid_ref, source_ref = here
    copies = [pltpu.make_async_copy(given[at], here[at], done_ref.at[at]) for at in range(6)]
    for copy in copies:
        copy.start()
    square = (NBLK, NBLK)
    copies[0].wait()
    bins = bin_ref[...].astype(F32)
    window = jnp.floor((bins + 0.5) * (1.0 / BINS_W))
    local_bin = bins - BINS_W * window
    window_column = jnp.broadcast_to(window, square).T
    earlier = jnp.where(window_column == window, 1.0, 0.0) * jnp.where(iota(square, 0) < iota(square, 1), 1.0, 0.0)
    rank = jnp.sum(earlier, axis=0, keepdims=True)
    slot_ref[...] = jnp.concatenate([window, rank, jnp.zeros((6, NBLK), F32)], axis=0)
    place = indicator(iota_f((SLOTS, NBLK), 0) == CAP * window + rank)
    copies[1].wait()
    mask = iota(square, 0) < rows_ref[...]
    used = jnp.broadcast_to(rows_ref[...].astype(F32), square).T
    for copy in copies[2:]:
        copy.wait()
    marked_ref[...] = jnp.where(iota_f(square, 1) < used, source_ref[...], -LOW)
    u = phase_ref[...].T
    resid = jnp.where(mask, resid_ref[...].T, 0.0)
    att = [jnp.where(mask, att_ref[pl.ds(q, NBLK, stride=4), :].T, 0.0) for q in range(4)]
    obs_ref[0:128, :] = u
    obs_ref[128:256, :] = resid
    for q in range(4):
        obs_ref[256 + 128 * q : 384 + 128 * q, :] = att[q]
    v = 1.0 - u
    u2, v2 = u * u, v * v
    u3, v3 = u2 * u, v2 * v
    cubes = [v3, u * v2, u2 * v, u3]
    powers = [v3 * v3, u * v2 * v3, u2 * v2 * v2, u3 * v3, u2 * u2 * v2, u3 * u2 * v, u3 * u3]
    for at, (first, second) in enumerate(ATT_PAIRS):
        product = att[first] * att[second]
        for m in range(7):
            row = m * 10 + at
            pay_ref[row : row + 1, :] = jnp.sum(powers[m] * product, axis=0, keepdims=True)
    for q in range(4):
        product = att[q] * resid
        sums = [jnp.sum(cubes[i] * product, axis=0, keepdims=True) for i in range(4)]
        for j in range(4):
            total = None
            for i in range(4):
                if SPLINE[j, i] != 0.0:
                    piece = float(SPLINE[j, i]) * sums[i]
                    total = piece if total is None else total + piece
            row = RHS_AT + 4 * j + q
            pay_ref[row : row + 1, :] = total
    pay_ref[BIN_AT : BIN_AT + 1, :] = local_bin
    pay_ref[BIN_AT + 1 :, :] = jnp.zeros((NBLK - BIN_AT - 1, NBLK), F32)
    send_ref[...] = exact_dot(pay_ref[...], place, NT, swap=True)


def bins_kernel(got_ref, after_ref, out_ref):
    del after_ref
    got = got_ref[...].T
    place = indicator(iota_f((KNOTS_W, SLOTS), 0) == got[BIN_AT : BIN_AT + 1, :])
    moments = exact_dot(got[:FEATS], place, NT)
    for at in range(N_CCD):
        out_ref[at] = moments


def attitude_kernel(parts_ref, got_ref, table_ref, att_ref, reply_ref):
    total = ((parts_ref[0] + parts_ref[1]) + (parts_ref[2] + parts_ref[3])) * (1.0 / 36.0)
    moved = jnp.concatenate([total] + [pltpu.roll(total, l, 1) for l in range(1, 4)], axis=0)
    band = exact_dot(moved, table_ref[...], NN, swap=True)
    groups = [band[8 * at : 8 * at + 8] for at in range(14)]
    lower_half = iota((8, KNOTS_W), 0) < 4

    def doubled(values):
        return values + pltpu.roll(values, 4, 0)

    def norm(values):
        return jnp.sum(jnp.sum(values, axis=1, keepdims=True), axis=0, keepdims=True)

    def apply(vector):
        spread = [
            jnp.where(lower_half, vector[2 * at : 2 * at + 1, :], vector[2 * at + 1 : 2 * at + 2, :]) for at in range(2)
        ]
        pieces = []
        for d in range(-3, 4):
            piece = groups[2 * (d + 3)] * spread[0] + groups[2 * (d + 3) + 1] * spread[1]
            pieces.append(pltpu.roll(piece, -d % KNOTS_W, 1) if d else piece)
        outer = (pieces[0] + pieces[1]) + (pieces[2] + pieces[4])
        return KNOT_PRIOR * vector + doubled(outer + ((pieces[5] + pieces[6]) + pieces[3]))

    residual = band[112:120]
    direction = residual
    estimate = jnp.zeros_like(residual)
    for iteration in range(ITERS):
        applied = apply(direction)
        norm_now = norm(residual * residual)
        inverse = 1.0 / norm(direction * applied)
        across = norm(residual * applied)
        applied_norm = norm(applied * applied)
        step_size = norm_now * inverse
        estimate = estimate + step_size * direction
        residual = residual - step_size * applied
        if iteration + 1 < ITERS:
            ratio = 1.0 - 2.0 * (across * inverse) + step_size * (applied_norm * inverse)
            direction = residual + ratio * direction
    att_ref[0] = estimate[:4]
    moved = jnp.concatenate([estimate[:4]] + [pltpu.roll(estimate, KNOTS_W - j, 1)[:4] for j in range(1, 4)], axis=0)
    column = jnp.concatenate(
        [got_ref[pl.ds(s, WINDOWS, stride=CAP), :][:, BIN_AT : BIN_AT + 1] for s in range(CAP)], axis=0
    )
    place = indicator(iota_f((SLOTS, KNOTS_W), 1) == column)
    knots = exact_dot(moved, place, NT, swap=True)
    reply_ref[...] = jnp.zeros((WINDOWS, 128), F32)
    for s in range(CAP):
        reply_ref[:, 16 * s : 16 * s + 16] = knots[WINDOWS * s : WINDOWS * s + WINDOWS]


def source_sums(count, terms_ref, high_ref, low_ref, out_ref, acc_ref, *buffers):
    high_at = iota_f((HIGH, ROWS), 0)
    low_at = iota_f((LOW, ROWS), 0).astype(BF16)
    one, zero = jnp.ones((), BF16), jnp.zeros((), BF16)

    def build(at, slot):
        a_ref, b_ref = buffers[slot], buffers[2 + slot]
        for inner in range(STEP_BLOCKS):
            block = at * STEP_BLOCKS + inner
            lanes = slice(inner * ROWS, inner * ROWS + ROWS)
            here = high_at == high_ref[pl.ds(block, 1), :]
            low = jnp.broadcast_to(low_ref[pl.ds(block, 1), :], (HIGH, ROWS)).astype(BF16)
            low = jnp.concatenate([low] * (LOW // HIGH), axis=0)
            b_ref[:, lanes] = jnp.where(low_at == low, one, zero)
            for c in range(2 * count):
                term = jnp.where(here, terms_ref[pl.ds(c * NBLK + block, 1), :], 0.0)
                a_ref[c * HIGH : (c + 1) * HIGH, lanes] = term.astype(BF16)

    def multiply(slot):
        acc_ref[...] += lax.dot_general(buffers[2 + slot][...], buffers[slot][...], NT, preferred_element_type=F32)

    def step(pair, carry):
        multiply(0)
        build(2 * pair + 1, 1)
        multiply(1)
        build(2 * pair + 2, 0)
        return carry

    acc_ref[...] = jnp.zeros(acc_ref.shape, F32)
    build(0, 0)
    lax.fori_loop(0, STEPS // 2 - 1, step, 0)
    multiply(0)
    build(STEPS - 1, 1)
    multiply(1)
    sums = acc_ref[...].T
    for c in range(count):
        at = 2 * c * HIGH
        out_ref[HIGH * c : HIGH * c + HIGH, :] = sums[at : at + HIGH] + sums[at + HIGH : at + 2 * HIGH]


def put_terms(terms_ref, c, values):
    large = values.astype(BF16).astype(F32)
    terms_ref[2 * c * NBLK : (2 * c + 1) * NBLK, :] = large
    terms_ref[(2 * c + 1) * NBLK : (2 * c + 2) * NBLK, :] = values - large


def put_sources(marked_ref, high_ref, low_ref):
    source = marked_ref[...]
    high = source >> 8
    high_ref[...] = high.astype(F32)
    low_ref[...] = (source - (high << 8)).astype(F32)


def source_normals_kernel(marked_ref, gain_ref, out_ref, terms_ref, high_ref, low_ref, *work):
    put_sources(marked_ref, high_ref, low_ref)
    gains = [gain_ref[NBLK * p : NBLK * p + NBLK, :] for p in range(5)]
    for at, (first, second) in enumerate(PAIR_LIST):
        put_terms(terms_ref, at, gains[first] * gains[second])
    source_sums(15, terms_ref, high_ref, low_ref, out_ref, *work)


def source_right_kernel(
    reply_ref, slot_ref, obs_ref, marked_ref, gain_ref, out_ref, terms_ref, high_ref, low_ref, *work
):
    put_sources(marked_ref, high_ref, low_ref)
    place = indicator(iota_f((WINDOWS, NBLK), 0) == slot_ref[0:1, :])
    rank = slot_ref[1:2, :]
    spread = exact_dot(reply_ref[...].T, place, NN)
    knots = None
    for s in range(CAP):
        piece = jnp.where(rank == float(s), spread[16 * s : 16 * s + 16, :], 0.0)
        knots = piece if knots is None else knots + piece
    u = obs_ref[0:128, :]
    att = [obs_ref[256 + 128 * q : 384 + 128 * q, :] for q in range(4)]
    v = 1.0 - u
    u2, v2 = u * u, v * v
    cubes = [v2 * v, u * v2, u2 * v, u2 * u]
    values = obs_ref[128:256, :]
    for j in range(4):
        spline = None
        for i in range(4):
            if SPLINE[j, i] != 0.0:
                piece = float(SPLINE[j, i]) * cubes[i]
                spline = piece if spline is None else spline + piece
        inner = None
        for q in range(4):
            piece = att[q] * knots[4 * j + q : 4 * j + q + 1, :]
            inner = piece if inner is None else inner + piece
        values = values - spline * inner
    values = values.T
    for p in range(5):
        put_terms(terms_ref, p, gain_ref[NBLK * p : NBLK * p + NBLK, :] * values)
    source_sums(5, terms_ref, high_ref, low_ref, out_ref.at[0], *work)
    for at in range(1, N_CCD):
        out_ref[at] = out_ref[0]


def factor_kernel(own_ref, one_ref, two_ref, three_ref, out_ref):
    entries = {}
    for at, pair in enumerate(PAIR_LIST):
        rows = slice(HIGH * at, HIGH * at + HIGH)
        total = (own_ref[rows, :] + two_ref[rows, :]) + (one_ref[rows, :] + three_ref[rows, :])
        entries[pair] = total + SOURCE_PRIOR if pair[0] == pair[1] else total
    lower = {}
    for column in range(5):
        pivot = entries[column, column]
        for before in range(column):
            pivot = pivot - lower[column, before] * lower[column, before]
        inverse = 1.0 / jnp.sqrt(pivot)
        lower[column, column] = inverse
        for row in range(column + 1, 5):
            running = entries[column, row]
            for before in range(column):
                running = running - lower[row, before] * lower[column, before]
            lower[row, column] = running * inverse
    for at, (first, second) in enumerate(PAIR_LIST):
        out_ref[HIGH * at : HIGH * at + HIGH, :] = lower[second, first]


def solve_kernel(factor_ref, parts_ref, out_ref):
    lower = {}
    for at, (first, second) in enumerate(PAIR_LIST):
        lower[second, first] = factor_ref[HIGH * at : HIGH * at + HIGH, :]
    values = []
    for row in range(5):
        rows = slice(HIGH * row, HIGH * row + HIGH)
        running = (parts_ref[0, rows, :] + parts_ref[1, rows, :]) + (parts_ref[2, rows, :] + parts_ref[3, rows, :])
        for before in range(row):
            running = running - lower[row, before] * values[before]
        values.append(running * lower[row, row])
    for row in reversed(range(5)):
        running = values[row]
        for later in range(row + 1, 5):
            running = running - lower[later, row] * values[later]
        values[row] = running * lower[row, row]
    for row in range(5):
        for high in range(HIGH):
            out_ref[row : row + 1, LOW * high : LOW * high + LOW] = values[row][high : high + 1, :]


def f32(*shape):
    return jax.ShapeDtypeStruct(shape, F32)


def kernel_call(body, name, outs, *args, scratch=(), flops=1_000_000, far=(), grant=32, passed=None):
    passed = passed or {}
    place = [pl.ANY if at in far else pltpu.MemorySpace.VMEM for at in range(len(args))]
    out_place = [pl.ANY if at in passed.values() else pltpu.MemorySpace.VMEM for at in range(len(jax.tree.leaves(outs)))]
    out_specs = [pl.BlockSpec(memory_space=at) for at in out_place]
    size = sum(math.prod(a.shape) * 4 for a in args)
    return pl.pallas_call(
        body,
        out_shape=outs,
        in_specs=[pl.BlockSpec(memory_space=at) for at in place],
        out_specs=tuple(out_specs) if isinstance(outs, tuple) else out_specs[0],
        input_output_aliases=passed,
        scratch_shapes=list(scratch),
        compiler_params=pltpu.CompilerParams(vmem_limit_bytes=grant * 1024 * 1024),
        cost_estimate=pl.CostEstimate(flops=flops, bytes_accessed=size, transcendentals=0),
        name=name,
    )(*args)


def segment_scratch(count):
    return (
        pltpu.VMEM((2 * count * NBLK, ROWS), F32),
        pltpu.VMEM((NBLK, ROWS), F32),
        pltpu.VMEM((NBLK, ROWS), F32),
        pltpu.VMEM((LOW, 2 * count * HIGH), F32),
        pltpu.VMEM((2 * count * HIGH, STEP_BLOCKS * ROWS), BF16),
        pltpu.VMEM((2 * count * HIGH, STEP_BLOCKS * ROWS), BF16),
        pltpu.VMEM((LOW, STEP_BLOCKS * ROWS), BF16),
        pltpu.VMEM((LOW, STEP_BLOCKS * ROWS), BF16),
    )


def from_others(values):
    return [
        lax.ppermute(values, "ccd", [(at, (at + shift) % N_CCD) for at in range(N_CCD)]) for shift in range(1, N_CCD)
    ]


def among_ccd(copies):
    return lax.all_to_all(copies, "ccd", split_axis=0, concat_axis=0, tiled=True)


def to_windows(values):
    return lax.all_to_all(values, ("src", "win"), split_axis=0, concat_axis=0, tiled=True)


def local(block_bin, block_rows, row_source, obs_resid, obs_phase, att_partial, src_partial):
    bins = block_bin.reshape(1, NBLK)
    rows = block_rows.reshape(1, NBLK)
    gains = jnp.transpose(src_partial, (1, 0, 2)).reshape(5 * NBLK, ROWS)
    send, obs, slots, marked = kernel_call(
        normals_kernel,
        "normals",
        (f32(SLOTS, 128), f32(6 * ROWS, NBLK), f32(8, NBLK), jax.ShapeDtypeStruct((NBLK, ROWS), jnp.int32)),
        bins,
        rows,
        obs_phase,
        att_partial.reshape(4 * NBLK, ROWS),
        obs_resid,
        row_source,
        scratch=(
            pltpu.VMEM((1, NBLK), jnp.int32),
            pltpu.VMEM((1, NBLK), jnp.int32),
            pltpu.VMEM((NBLK, ROWS), F32),
            pltpu.VMEM((4 * NBLK, ROWS), F32),
            pltpu.VMEM((NBLK, ROWS), F32),
            pltpu.VMEM((NBLK, ROWS), jnp.int32),
            pltpu.VMEM((NBLK, NBLK), F32),
            pltpu.SemaphoreType.DMA((6,)),
        ),
        far=range(6),
        grant=56,
    )
    got = to_windows(send.reshape(WINDOWS, CAP, 128)).reshape(SLOTS, 128)
    normal = kernel_call(
        source_normals_kernel,
        "source_normals",
        f32(15 * HIGH, LOW),
        marked,
        gains,
        scratch=segment_scratch(15),
        flops=2 * 480 * 256 * 16384,
    )
    moments = kernel_call(bins_kernel, "bins", f32(N_CCD, FEATS, KNOTS_W), got, normal, far=(1,))
    attitude, reply = kernel_call(
        attitude_kernel,
        "attitude",
        (f32(1, 4, KNOTS_W), f32(WINDOWS, 128)),
        among_ccd(moments),
        got,
        jnp.asarray(knot_matrix()),
    )
    knots = to_windows(reply)
    factors = kernel_call(factor_kernel, "factors", f32(15 * HIGH, LOW), normal, *from_others(normal))
    right = kernel_call(
        source_right_kernel,
        "source_right",
        f32(N_CCD, 5 * HIGH, LOW),
        knots,
        slots,
        obs,
        marked,
        gains,
        scratch=segment_scratch(5),
        flops=2 * 160 * 256 * 16384,
    )
    source_delta = kernel_call(solve_kernel, "solve", f32(5, SRC_DEV), factors, among_ccd(right))
    return attitude, source_delta


def solution(mesh):
    return jax.shard_map(
        local,
        mesh=mesh,
        in_specs=(
            P(("src", "win", "ccd")),
            P(("src", "win", "ccd")),
            P(("src", "win", "ccd"), None),
            P(("src", "win", "ccd"), None),
            P(("src", "win", "ccd"), None),
            P(("src", "win", "ccd"), None, None),
            P(("src", "win", "ccd"), None, None),
        ),
        out_specs=(P(("src", "win"), None, None), P(None, ("src", "win"))),
        check_vma=False,
    )
```

```python
import math

import jax
import jax.numpy as jnp
import ml_dtypes
import numpy as np
from jax import lax
from jax.experimental import pallas as pl
from jax.experimental.pallas import tpu as pltpu
from jax.sharding import PartitionSpec as P

KNOTS_W = 128
BINS_W = 125
NBLK = 128
ROWS = 128
WINDOWS = 64
CAP = 4
SLOTS = WINDOWS * CAP
SRC_DEV = 4096
ITERS = 8
N_CCD = 4
HIGH = 16
LOW = 256
STEP_BLOCKS = 16
STEPS = NBLK // STEP_BLOCKS

KNOT_PRIOR = 1.0
SOURCE_PRIOR = 1.0
PAIR_LIST = [(first, second) for first in range(5) for second in range(first, 5)]
ATT_PAIRS = [(first, second) for first in range(4) for second in range(first, 4)]
RHS_AT = 70
BIN_AT = 86
FEATS = 88

F32 = jnp.float32
BF16 = jnp.bfloat16
NT = (((1,), (1,)), ((), ()))
NN = (((1,), (0,)), ((), ()))

PIECES = np.array([[1, 0, 0, 0], [4, 12, 6, 1], [1, 6, 12, 4], [0, 0, 0, 1]], np.int64)
SPLINE = PIECES / 6.0


def knot_matrix():
    pair_at = {}
    for at, (first, second) in enumerate(ATT_PAIRS):
        pair_at[first, second] = pair_at[second, first] = at
    table = np.zeros((120, 4 * FEATS), np.float64)
    for d in range(-3, 4):
        for p in range(4):
            for q in range(4):
                row = ((d + 3) * 4 + p) * 4 + q
                for l in range(4):
                    j = l - d
                    if 0 <= j < 4:
                        for m, value in enumerate(np.convolve(PIECES[j], PIECES[l])):
                            table[row, l * FEATS + m * 10 + pair_at[q, p]] += value
    for q in range(4):
        for j in range(4):
            table[112 + q, j * FEATS + RHS_AT + 4 * j + q] = 36.0
            table[116 + q, j * FEATS + RHS_AT + 4 * j + q] = 36.0
    return table.astype(ml_dtypes.bfloat16)


def split_parts(values, count):
    parts = []
    for at in range(count):
        part = values.astype(BF16)
        parts.append(part)
        if at + 1 < count:
            values = values - part.astype(F32)
    return parts


def exact_dot(values, ones, dims, swap=False):
    total = None
    for part in split_parts(values, 3):
        pair = (ones, part) if swap else (part, ones)
        piece = lax.dot_general(*pair, dims, preferred_element_type=F32)
        total = piece if total is None else total + piece
    return total


def indicator(condition):
    return jnp.where(condition, 1.0, 0.0).astype(BF16)


def iota(shape, axis):
    return lax.broadcasted_iota(jnp.int32, shape, axis)


def iota_f(shape, axis):
    return iota(shape, axis).astype(F32)


def normals_kernel(*refs):
    given, (send_ref, obs_out, slot_ref, marked_out), here = refs[:6], refs[6:10], refs[10:16]
    pay_ref, obs_ref, marked_ref, done_ref = refs[16:]
    bin_ref, rows_ref, phase_ref, att_ref, resid_ref, source_ref = here
    copies = [pltpu.make_async_copy(given[at], here[at], done_ref.at[at]) for at in range(6)]
    for copy in copies:
        copy.start()
    square = (NBLK, NBLK)
    copies[0].wait()
    bins = bin_ref[...].astype(F32)
    window = jnp.floor((bins + 0.5) * (1.0 / BINS_W))
    local_bin = bins - BINS_W * window
    window_column = jnp.broadcast_to(window, square).T
    earlier = jnp.where(window_column == window, 1.0, 0.0) * jnp.where(iota(square, 0) < iota(square, 1), 1.0, 0.0)
    rank = jnp.sum(earlier, axis=0, keepdims=True)
    slot_ref[...] = jnp.concatenate([window, rank, jnp.zeros((6, NBLK), F32)], axis=0)
    place = indicator(iota_f((SLOTS, NBLK), 0) == CAP * window + rank)
    copies[1].wait()
    mask = iota(square, 0) < rows_ref[...]
    used = jnp.broadcast_to(rows_ref[...].astype(F32), square).T
    for copy in copies[2:]:
        copy.wait()
    marked_ref[...] = jnp.where(iota_f(square, 1) < used, source_ref[...], -LOW)
    u = phase_ref[...].T
    resid = jnp.where(mask, resid_ref[...].T, 0.0)
    att = [jnp.where(mask, att_ref[pl.ds(q, NBLK, stride=4), :].T, 0.0) for q in range(4)]
    obs_ref[0:128, :] = u
    obs_ref[128:256, :] = resid
    for q in range(4):
        obs_ref[256 + 128 * q : 384 + 128 * q, :] = att[q]
    results = [
        pltpu.make_async_copy(marked_ref, marked_out, done_ref.at[6]),
        pltpu.make_async_copy(obs_ref, obs_out, done_ref.at[7]),
    ]
    for copy in results:
        copy.start()
    v = 1.0 - u
    u2, v2 = u * u, v * v
    u3, v3 = u2 * u, v2 * v
    cubes = [v3, u * v2, u2 * v, u3]
    powers = [v3 * v3, u * v2 * v3, u2 * v2 * v2, u3 * v3, u2 * u2 * v2, u3 * u2 * v, u3 * u3]
    for at, (first, second) in enumerate(ATT_PAIRS):
        product = att[first] * att[second]
        for m in range(7):
            row = m * 10 + at
            pay_ref[row : row + 1, :] = jnp.sum(powers[m] * product, axis=0, keepdims=True)
    for q in range(4):
        product = att[q] * resid
        sums = [jnp.sum(cubes[i] * product, axis=0, keepdims=True) for i in range(4)]
        for j in range(4):
            total = None
            for i in range(4):
                if SPLINE[j, i] != 0.0:
                    piece = float(SPLINE[j, i]) * sums[i]
                    total = piece if total is None else total + piece
            row = RHS_AT + 4 * j + q
            pay_ref[row : row + 1, :] = total
    pay_ref[BIN_AT : BIN_AT + 1, :] = local_bin
    pay_ref[BIN_AT + 1 :, :] = jnp.zeros((NBLK - BIN_AT - 1, NBLK), F32)
    send_ref[...] = exact_dot(pay_ref[...], place, NT, swap=True)
    for copy in results:
        copy.wait()


def bins_kernel(got_ref, after_ref, out_ref):
    del after_ref
    got = got_ref[...].T
    place = indicator(iota_f((KNOTS_W, SLOTS), 0) == got[BIN_AT : BIN_AT + 1, :])
    moments = exact_dot(got[:FEATS], place, NT)
    for at in range(N_CCD):
        out_ref[at] = moments


def attitude_kernel(parts_ref, got_ref, table_ref, att_ref, reply_ref):
    total = ((parts_ref[0] + parts_ref[1]) + (parts_ref[2] + parts_ref[3])) * (1.0 / 36.0)
    moved = jnp.concatenate([total] + [pltpu.roll(total, l, 1) for l in range(1, 4)], axis=0)
    band = exact_dot(moved, table_ref[...], NN, swap=True)
    groups = [band[8 * at : 8 * at + 8] for at in range(14)]
    lower_half = iota((8, KNOTS_W), 0) < 4

    def doubled(values):
        return values + pltpu.roll(values, 4, 0)

    def norm(values):
        return jnp.sum(jnp.sum(values, axis=1, keepdims=True), axis=0, keepdims=True)

    def apply(vector):
        spread = [
            jnp.where(lower_half, vector[2 * at : 2 * at + 1, :], vector[2 * at + 1 : 2 * at + 2, :]) for at in range(2)
        ]
        pieces = []
        for d in range(-3, 4):
            piece = groups[2 * (d + 3)] * spread[0] + groups[2 * (d + 3) + 1] * spread[1]
            pieces.append(pltpu.roll(piece, -d % KNOTS_W, 1) if d else piece)
        outer = (pieces[0] + pieces[1]) + (pieces[2] + pieces[4])
        return KNOT_PRIOR * vector + doubled(outer + ((pieces[5] + pieces[6]) + pieces[3]))

    residual = band[112:120]
    direction = residual
    estimate = jnp.zeros_like(residual)
    for iteration in range(ITERS):
        applied = apply(direction)
        norm_now = norm(residual * residual)
        inverse = 1.0 / norm(direction * applied)
        across = norm(residual * applied)
        applied_norm = norm(applied * applied)
        step_size = norm_now * inverse
        estimate = estimate + step_size * direction
        residual = residual - step_size * applied
        if iteration + 1 < ITERS:
            ratio = 1.0 - 2.0 * (across * inverse) + step_size * (applied_norm * inverse)
            direction = residual + ratio * direction
    att_ref[0] = estimate[:4]
    moved = jnp.concatenate([estimate[:4]] + [pltpu.roll(estimate, KNOTS_W - j, 1)[:4] for j in range(1, 4)], axis=0)
    column = jnp.concatenate(
        [got_ref[pl.ds(s, WINDOWS, stride=CAP), :][:, BIN_AT : BIN_AT + 1] for s in range(CAP)], axis=0
    )
    place = indicator(iota_f((SLOTS, KNOTS_W), 1) == column)
    knots = exact_dot(moved, place, NT, swap=True)
    reply_ref[...] = jnp.zeros((WINDOWS, 128), F32)
    for s in range(CAP):
        reply_ref[:, 16 * s : 16 * s + 16] = knots[WINDOWS * s : WINDOWS * s + WINDOWS]


def source_sums(count, terms_ref, high_ref, low_ref, out_ref, acc_ref, *buffers):
    high_at = iota_f((HIGH, ROWS), 0)
    low_at = iota_f((LOW, ROWS), 0).astype(BF16)
    one, zero = jnp.ones((), BF16), jnp.zeros((), BF16)

    def build(at, slot):
        a_ref, b_ref = buffers[slot], buffers[2 + slot]
        for inner in range(STEP_BLOCKS):
            block = at * STEP_BLOCKS + inner
            lanes = slice(inner * ROWS, inner * ROWS + ROWS)
            here = high_at == high_ref[pl.ds(block, 1), :]
            low = jnp.broadcast_to(low_ref[pl.ds(block, 1), :], (HIGH, ROWS)).astype(BF16)
            low = jnp.concatenate([low] * (LOW // HIGH), axis=0)
            b_ref[:, lanes] = jnp.where(low_at == low, one, zero)
            for c in range(2 * count):
                term = jnp.where(here, terms_ref[pl.ds(c * NBLK + block, 1), :], 0.0)
                a_ref[c * HIGH : (c + 1) * HIGH, lanes] = term.astype(BF16)

    def multiply(slot):
        acc_ref[...] += lax.dot_general(buffers[2 + slot][...], buffers[slot][...], NT, preferred_element_type=F32)

    def step(pair, carry):
        multiply(0)
        build(2 * pair + 1, 1)
        multiply(1)
        build(2 * pair + 2, 0)
        return carry

    acc_ref[...] = jnp.zeros(acc_ref.shape, F32)
    build(0, 0)
    lax.fori_loop(0, STEPS // 2 - 1, step, 0)
    multiply(0)
    build(STEPS - 1, 1)
    multiply(1)
    sums = acc_ref[...].T
    for c in range(count):
        at = 2 * c * HIGH
        out_ref[HIGH * c : HIGH * c + HIGH, :] = sums[at : at + HIGH] + sums[at + HIGH : at + 2 * HIGH]


def put_terms(terms_ref, c, values):
    large = values.astype(BF16).astype(F32)
    terms_ref[2 * c * NBLK : (2 * c + 1) * NBLK, :] = large
    terms_ref[(2 * c + 1) * NBLK : (2 * c + 2) * NBLK, :] = values - large


def put_sources(marked_ref, high_ref, low_ref):
    source = marked_ref[...]
    high = source >> 8
    high_ref[...] = high.astype(F32)
    low_ref[...] = (source - (high << 8)).astype(F32)


def source_normals_kernel(marked_ref, gain_ref, out_ref, terms_ref, high_ref, low_ref, *work):
    put_sources(marked_ref, high_ref, low_ref)
    gains = [gain_ref[NBLK * p : NBLK * p + NBLK, :] for p in range(5)]
    for at, (first, second) in enumerate(PAIR_LIST):
        put_terms(terms_ref, at, gains[first] * gains[second])
    source_sums(15, terms_ref, high_ref, low_ref, out_ref, *work)


def source_right_kernel(
    reply_ref, slot_ref, obs_ref, marked_ref, gain_ref, out_ref, terms_ref, high_ref, low_ref, *work
):
    put_sources(marked_ref, high_ref, low_ref)
    place = indicator(iota_f((WINDOWS, NBLK), 0) == slot_ref[0:1, :])
    rank = slot_ref[1:2, :]
    spread = exact_dot(reply_ref[...].T, place, NN)
    knots = None
    for s in range(CAP):
        piece = jnp.where(rank == float(s), spread[16 * s : 16 * s + 16, :], 0.0)
        knots = piece if knots is None else knots + piece
    u = obs_ref[0:128, :]
    att = [obs_ref[256 + 128 * q : 384 + 128 * q, :] for q in range(4)]
    v = 1.0 - u
    u2, v2 = u * u, v * v
    cubes = [v2 * v, u * v2, u2 * v, u2 * u]
    values = obs_ref[128:256, :]
    for j in range(4):
        spline = None
        for i in range(4):
            if SPLINE[j, i] != 0.0:
                piece = float(SPLINE[j, i]) * cubes[i]
                spline = piece if spline is None else spline + piece
        inner = None
        for q in range(4):
            piece = att[q] * knots[4 * j + q : 4 * j + q + 1, :]
            inner = piece if inner is None else inner + piece
        values = values - spline * inner
    values = values.T
    for p in range(5):
        put_terms(terms_ref, p, gain_ref[NBLK * p : NBLK * p + NBLK, :] * values)
    source_sums(5, terms_ref, high_ref, low_ref, out_ref, *work)


def factor_kernel(own_ref, one_ref, two_ref, three_ref, out_ref):
    entries = {}
    for at, pair in enumerate(PAIR_LIST):
        rows = slice(HIGH * at, HIGH * at + HIGH)
        total = (own_ref[rows, :] + two_ref[rows, :]) + (one_ref[rows, :] + three_ref[rows, :])
        entries[pair] = total + SOURCE_PRIOR if pair[0] == pair[1] else total
    lower = {}
    for column in range(5):
        pivot = entries[column, column]
        for before in range(column):
            pivot = pivot - lower[column, before] * lower[column, before]
        inverse = 1.0 / jnp.sqrt(pivot)
        lower[column, column] = inverse
        for row in range(column + 1, 5):
            running = entries[column, row]
            for before in range(column):
                running = running - lower[row, before] * lower[column, before]
            lower[row, column] = running * inverse
    for at, (first, second) in enumerate(PAIR_LIST):
        out_ref[HIGH * at : HIGH * at + HIGH, :] = lower[second, first]


def solve_kernel(factor_ref, own_ref, one_ref, two_ref, three_ref, out_ref):
    lower = {}
    for at, (first, second) in enumerate(PAIR_LIST):
        lower[second, first] = factor_ref[HIGH * at : HIGH * at + HIGH, :]
    values = []
    for row in range(5):
        rows = slice(HIGH * row, HIGH * row + HIGH)
        running = (own_ref[rows, :] + two_ref[rows, :]) + (one_ref[rows, :] + three_ref[rows, :])
        for before in range(row):
            running = running - lower[row, before] * values[before]
        values.append(running * lower[row, row])
    for row in reversed(range(5)):
        running = values[row]
        for later in range(row + 1, 5):
            running = running - lower[later, row] * values[later]
        values[row] = running * lower[row, row]
    for row in range(5):
        for high in range(HIGH):
            out_ref[row : row + 1, LOW * high : LOW * high + LOW] = values[row][high : high + 1, :]


def f32(*shape):
    return jax.ShapeDtypeStruct(shape, F32)


def kernel_call(body, name, outs, *args, scratch=(), flops=1_000_000, far=(), far_out=(), grant=32):
    place = [pl.ANY if at in far else pltpu.MemorySpace.VMEM for at in range(len(args))]
    out_place = [pl.ANY if at in far_out else pltpu.MemorySpace.VMEM for at in range(len(jax.tree.leaves(outs)))]
    out_specs = [pl.BlockSpec(memory_space=at) for at in out_place]
    size = sum(math.prod(a.shape) * 4 for a in args)
    return pl.pallas_call(
        body,
        out_shape=outs,
        in_specs=[pl.BlockSpec(memory_space=at) for at in place],
        out_specs=tuple(out_specs) if isinstance(outs, tuple) else out_specs[0],
        scratch_shapes=list(scratch),
        compiler_params=pltpu.CompilerParams(vmem_limit_bytes=grant * 1024 * 1024),
        cost_estimate=pl.CostEstimate(flops=flops, bytes_accessed=size, transcendentals=0),
        name=name,
    )(*args)


def segment_scratch(count):
    return (
        pltpu.VMEM((2 * count * NBLK, ROWS), F32),
        pltpu.VMEM((NBLK, ROWS), F32),
        pltpu.VMEM((NBLK, ROWS), F32),
        pltpu.VMEM((LOW, 2 * count * HIGH), F32),
        pltpu.VMEM((2 * count * HIGH, STEP_BLOCKS * ROWS), BF16),
        pltpu.VMEM((2 * count * HIGH, STEP_BLOCKS * ROWS), BF16),
        pltpu.VMEM((LOW, STEP_BLOCKS * ROWS), BF16),
        pltpu.VMEM((LOW, STEP_BLOCKS * ROWS), BF16),
    )


def from_others(values):
    return [
        lax.ppermute(values, "ccd", [(at, (at + shift) % N_CCD) for at in range(N_CCD)]) for shift in range(1, N_CCD)
    ]


def among_ccd(copies):
    return lax.all_to_all(copies, "ccd", split_axis=0, concat_axis=0, tiled=True)


def to_windows(values):
    return lax.all_to_all(values, ("src", "win"), split_axis=0, concat_axis=0, tiled=True)


def local(block_bin, block_rows, row_source, obs_resid, obs_phase, att_partial, src_partial):
    bins = block_bin.reshape(1, NBLK)
    rows = block_rows.reshape(1, NBLK)
    gains = jnp.transpose(src_partial, (1, 0, 2)).reshape(5 * NBLK, ROWS)
    send, obs, slots, marked = kernel_call(
        normals_kernel,
        "normals",
        (f32(SLOTS, 128), f32(6 * ROWS, NBLK), f32(8, NBLK), jax.ShapeDtypeStruct((NBLK, ROWS), jnp.int32)),
        bins,
        rows,
        obs_phase,
        att_partial.reshape(4 * NBLK, ROWS),
        obs_resid,
        row_source,
        scratch=(
            pltpu.VMEM((1, NBLK), jnp.int32),
            pltpu.VMEM((1, NBLK), jnp.int32),
            pltpu.VMEM((NBLK, ROWS), F32),
            pltpu.VMEM((4 * NBLK, ROWS), F32),
            pltpu.VMEM((NBLK, ROWS), F32),
            pltpu.VMEM((NBLK, ROWS), jnp.int32),
            pltpu.VMEM((NBLK, NBLK), F32),
            pltpu.VMEM((6 * ROWS, NBLK), F32),
            pltpu.VMEM((NBLK, ROWS), jnp.int32),
            pltpu.SemaphoreType.DMA((8,)),
        ),
        far=range(6),
        far_out=(1, 3),
        grant=56,
    )
    got = to_windows(send.reshape(WINDOWS, CAP, 128)).reshape(SLOTS, 128)
    normal = kernel_call(
        source_normals_kernel,
        "source_normals",
        f32(15 * HIGH, LOW),
        marked,
        gains,
        scratch=segment_scratch(15),
        flops=2 * 480 * 256 * 16384,
    )
    moments = kernel_call(bins_kernel, "bins", f32(N_CCD, FEATS, KNOTS_W), got, normal, far=(1,))
    attitude, reply = kernel_call(
        attitude_kernel,
        "attitude",
        (f32(1, 4, KNOTS_W), f32(WINDOWS, 128)),
        among_ccd(moments),
        got,
        jnp.asarray(knot_matrix()),
    )
    knots = to_windows(reply)
    factors = kernel_call(factor_kernel, "factors", f32(15 * HIGH, LOW), normal, *from_others(normal))
    right = kernel_call(
        source_right_kernel,
        "source_right",
        f32(5 * HIGH, LOW),
        knots,
        slots,
        obs,
        marked,
        gains,
        scratch=segment_scratch(5),
        flops=2 * 160 * 256 * 16384,
    )
    source_delta = kernel_call(solve_kernel, "solve", f32(5, SRC_DEV), factors, right, *from_others(right))
    return attitude, source_delta


def solution(mesh):
    return jax.shard_map(
        local,
        mesh=mesh,
        in_specs=(
            P(("src", "win", "ccd")),
            P(("src", "win", "ccd")),
            P(("src", "win", "ccd"), None),
            P(("src", "win", "ccd"), None),
            P(("src", "win", "ccd"), None),
            P(("src", "win", "ccd"), None, None),
            P(("src", "win", "ccd"), None, None),
        ),
        out_specs=(P(("src", "win"), None, None), P(None, ("src", "win"))),
        check_vma=False,
    )
```

```python
import math

import jax
import jax.numpy as jnp
import ml_dtypes
import numpy as np
from jax import lax
from jax.experimental import pallas as pl
from jax.experimental.pallas import tpu as pltpu
from jax.sharding import PartitionSpec as P

KNOTS_W = 128
BINS_W = 125
NBLK = 128
ROWS = 128
WINDOWS = 64
CAP = 4
SLOTS = WINDOWS * CAP
SRC_DEV = 4096
ITERS = 8
N_CCD = 4
HIGH = 16
LOW = 256
DOT_BLOCKS = 8

KNOT_PRIOR = 1.0
SOURCE_PRIOR = 1.0
PAIR_LIST = [(first, second) for first in range(5) for second in range(first, 5)]
ATT_PAIRS = [(first, second) for first in range(4) for second in range(first, 4)]
RHS_AT = 70
BIN_AT = 86
FEATS = 88

F32 = jnp.float32
BF16 = jnp.bfloat16
NT = (((1,), (1,)), ((), ()))
NN = (((1,), (0,)), ((), ()))

PIECES = np.array([[1, 0, 0, 0], [4, 12, 6, 1], [1, 6, 12, 4], [0, 0, 0, 1]], np.int64)
SPLINE = PIECES / 6.0


def knot_matrix():
    pair_at = {}
    for at, (first, second) in enumerate(ATT_PAIRS):
        pair_at[first, second] = pair_at[second, first] = at
    table = np.zeros((120, 4 * FEATS), np.float64)
    for d in range(-3, 4):
        for p in range(4):
            for q in range(4):
                row = ((d + 3) * 4 + p) * 4 + q
                for l in range(4):
                    j = l - d
                    if 0 <= j < 4:
                        for m, value in enumerate(np.convolve(PIECES[j], PIECES[l])):
                            table[row, l * FEATS + m * 10 + pair_at[q, p]] += value
    for q in range(4):
        for j in range(4):
            table[112 + q, j * FEATS + RHS_AT + 4 * j + q] = 36.0
            table[116 + q, j * FEATS + RHS_AT + 4 * j + q] = 36.0
    return table.astype(ml_dtypes.bfloat16)


def split_parts(values, count):
    parts = []
    for at in range(count):
        part = values.astype(BF16)
        parts.append(part)
        if at + 1 < count:
            values = values - part.astype(F32)
    return parts


def exact_dot(values, ones, dims, swap=False):
    total = None
    for part in split_parts(values, 3):
        pair = (ones, part) if swap else (part, ones)
        piece = lax.dot_general(*pair, dims, preferred_element_type=F32)
        total = piece if total is None else total + piece
    return total


def indicator(condition):
    return jnp.where(condition, 1.0, 0.0).astype(BF16)


def iota(shape, axis):
    return lax.broadcasted_iota(jnp.int32, shape, axis)


def iota_f(shape, axis):
    return iota(shape, axis).astype(F32)


def normals_kernel(*refs):
    given, (send_ref, obs_ref, slot_ref, marked_ref), here = refs[:6], refs[6:10], refs[10:16]
    pay_ref, done_ref = refs[16:]
    bin_ref, rows_ref, phase_ref, att_ref, resid_ref, source_ref = here
    copies = [pltpu.make_async_copy(given[at], here[at], done_ref.at[at]) for at in range(6)]
    for copy in copies:
        copy.start()
    square = (NBLK, NBLK)
    copies[0].wait()
    bins = bin_ref[...].astype(F32)
    window = jnp.floor((bins + 0.5) * (1.0 / BINS_W))
    local_bin = bins - BINS_W * window
    window_column = jnp.broadcast_to(window, square).T
    earlier = jnp.where(window_column == window, 1.0, 0.0) * jnp.where(iota(square, 0) < iota(square, 1), 1.0, 0.0)
    rank = jnp.sum(earlier, axis=0, keepdims=True)
    slot_ref[...] = jnp.concatenate([window, rank, jnp.zeros((6, NBLK), F32)], axis=0)
    place = indicator(iota_f((SLOTS, NBLK), 0) == CAP * window + rank)
    copies[1].wait()
    mask = iota(square, 0) < rows_ref[...]
    used = jnp.broadcast_to(rows_ref[...].astype(F32), square).T
    for copy in copies[2:]:
        copy.wait()
    marked_ref[...] = jnp.where(iota_f(square, 1) < used, source_ref[...], -LOW)
    u = phase_ref[...].T
    resid = jnp.where(mask, resid_ref[...].T, 0.0)
    att = [jnp.where(mask, att_ref[pl.ds(q, NBLK, stride=4), :].T, 0.0) for q in range(4)]
    obs_ref[0:128, :] = u
    obs_ref[128:256, :] = resid
    for q in range(4):
        obs_ref[256 + 128 * q : 384 + 128 * q, :] = att[q]
    v = 1.0 - u
    u2, v2 = u * u, v * v
    u3, v3 = u2 * u, v2 * v
    cubes = [v3, u * v2, u2 * v, u3]
    powers = [v3 * v3, u * v2 * v3, u2 * v2 * v2, u3 * v3, u2 * u2 * v2, u3 * u2 * v, u3 * u3]
    for at, (first, second) in enumerate(ATT_PAIRS):
        product = att[first] * att[second]
        for m in range(7):
            row = m * 10 + at
            pay_ref[row : row + 1, :] = jnp.sum(powers[m] * product, axis=0, keepdims=True)
    for q in range(4):
        product = att[q] * resid
        sums = [jnp.sum(cubes[i] * product, axis=0, keepdims=True) for i in range(4)]
        for j in range(4):
            total = None
            for i in range(4):
                if SPLINE[j, i] != 0.0:
                    piece = float(SPLINE[j, i]) * sums[i]
                    total = piece if total is None else total + piece
            row = RHS_AT + 4 * j + q
            pay_ref[row : row + 1, :] = total
    pay_ref[BIN_AT : BIN_AT + 1, :] = local_bin
    pay_ref[BIN_AT + 1 :, :] = jnp.zeros((NBLK - BIN_AT - 1, NBLK), F32)
    send_ref[...] = exact_dot(pay_ref[...], place, NT, swap=True)


def bins_kernel(got_ref, after_ref, out_ref):
    del after_ref
    got = got_ref[...].T
    place = indicator(iota_f((KNOTS_W, SLOTS), 0) == got[BIN_AT : BIN_AT + 1, :])
    out_ref[...] = exact_dot(got[:FEATS], place, NT)


def attitude_kernel(own_ref, one_ref, two_ref, three_ref, got_ref, table_ref, att_ref, reply_ref):
    total = ((own_ref[...] + two_ref[...]) + (one_ref[...] + three_ref[...])) * (1.0 / 36.0)
    moved = jnp.concatenate([total] + [pltpu.roll(total, l, 1) for l in range(1, 4)], axis=0)
    band = exact_dot(moved, table_ref[...], NN, swap=True)
    groups = [band[8 * at : 8 * at + 8] for at in range(14)]
    lower_half = iota((8, KNOTS_W), 0) < 4

    def doubled(values):
        return values + pltpu.roll(values, 4, 0)

    def norm(values):
        return jnp.sum(jnp.sum(values, axis=1, keepdims=True), axis=0, keepdims=True)

    def apply(vector):
        spread = [
            jnp.where(lower_half, vector[2 * at : 2 * at + 1, :], vector[2 * at + 1 : 2 * at + 2, :]) for at in range(2)
        ]
        pieces = []
        for d in range(-3, 4):
            piece = groups[2 * (d + 3)] * spread[0] + groups[2 * (d + 3) + 1] * spread[1]
            pieces.append(pltpu.roll(piece, -d % KNOTS_W, 1) if d else piece)
        outer = (pieces[0] + pieces[1]) + (pieces[2] + pieces[4])
        return KNOT_PRIOR * vector + doubled(outer + ((pieces[5] + pieces[6]) + pieces[3]))

    residual = band[112:120]
    direction = residual
    estimate = jnp.zeros_like(residual)
    for iteration in range(ITERS):
        applied = apply(direction)
        norm_now = norm(residual * residual)
        inverse = 1.0 / norm(direction * applied)
        across = norm(residual * applied)
        applied_norm = norm(applied * applied)
        step_size = norm_now * inverse
        estimate = estimate + step_size * direction
        residual = residual - step_size * applied
        if iteration + 1 < ITERS:
            ratio = 1.0 - 2.0 * (across * inverse) + step_size * (applied_norm * inverse)
            direction = residual + ratio * direction
    att_ref[0] = estimate[:4]
    moved = jnp.concatenate([estimate[:4]] + [pltpu.roll(estimate, KNOTS_W - j, 1)[:4] for j in range(1, 4)], axis=0)
    column = jnp.concatenate(
        [got_ref[pl.ds(s, WINDOWS, stride=CAP), :][:, BIN_AT : BIN_AT + 1] for s in range(CAP)], axis=0
    )
    place = indicator(iota_f((SLOTS, KNOTS_W), 1) == column)
    knots = exact_dot(moved, place, NT, swap=True)
    reply_ref[...] = jnp.zeros((WINDOWS, 128), F32)
    for s in range(CAP):
        reply_ref[:, 16 * s : 16 * s + 16] = knots[WINDOWS * s : WINDOWS * s + WINDOWS]


def source_sums(count, chunk, terms_ref, high_ref, low_ref, out_ref, acc_ref):
    high_at = iota_f((HIGH, ROWS), 0)
    low_at = iota_f((LOW, ROWS), 0).astype(BF16)
    one, zero = jnp.ones((), BF16), jnp.zeros((), BF16)

    def factors(block):
        here = high_at == high_ref[pl.ds(block, 1), :]
        low = jnp.broadcast_to(low_ref[pl.ds(block, 1), :], (HIGH, ROWS)).astype(BF16)
        low = jnp.concatenate([low] * (LOW // HIGH), axis=0)
        terms = [
            jnp.where(here, terms_ref[pl.ds(c * NBLK + block, 1), :], 0.0).astype(BF16) for c in range(2 * count)
        ]
        return jnp.concatenate(terms, axis=0), jnp.where(low_at == low, one, zero)

    def step(at, carry):
        for first in range(0, chunk, DOT_BLOCKS):
            pairs = [factors(at * chunk + first + inner) for inner in range(DOT_BLOCKS)]
            terms = jnp.concatenate([pair[0] for pair in pairs], axis=1)
            ones = jnp.concatenate([pair[1] for pair in pairs], axis=1)
            acc_ref[...] += lax.dot_general(ones, terms, NT, preferred_element_type=F32)
        return carry

    acc_ref[...] = jnp.zeros(acc_ref.shape, F32)
    lax.fori_loop(0, NBLK // chunk, step, 0)
    sums = acc_ref[...].T
    for c in range(count):
        at = 2 * c * HIGH
        out_ref[HIGH * c : HIGH * c + HIGH, :] = sums[at : at + HIGH] + sums[at + HIGH : at + 2 * HIGH]


def put_terms(terms_ref, c, values):
    large = values.astype(BF16).astype(F32)
    terms_ref[2 * c * NBLK : (2 * c + 1) * NBLK, :] = large
    terms_ref[(2 * c + 1) * NBLK : (2 * c + 2) * NBLK, :] = values - large


def put_sources(marked_ref, high_ref, low_ref):
    source = marked_ref[...]
    high = source >> 8
    high_ref[...] = high.astype(F32)
    low_ref[...] = (source - (high << 8)).astype(F32)


def source_normals_kernel(marked_ref, gain_ref, out_ref, terms_ref, high_ref, low_ref, *work):
    put_sources(marked_ref, high_ref, low_ref)
    gains = [gain_ref[NBLK * p : NBLK * p + NBLK, :] for p in range(5)]
    for at, (first, second) in enumerate(PAIR_LIST):
        put_terms(terms_ref, at, gains[first] * gains[second])
    source_sums(15, 32, terms_ref, high_ref, low_ref, out_ref, *work)


def source_right_kernel(
    reply_ref, slot_ref, obs_ref, marked_ref, gain_ref, out_ref, terms_ref, high_ref, low_ref, *work
):
    put_sources(marked_ref, high_ref, low_ref)
    place = indicator(iota_f((WINDOWS, NBLK), 0) == slot_ref[0:1, :])
    rank = slot_ref[1:2, :]
    spread = exact_dot(reply_ref[...].T, place, NN)
    knots = None
    for s in range(CAP):
        piece = jnp.where(rank == float(s), spread[16 * s : 16 * s + 16, :], 0.0)
        knots = piece if knots is None else knots + piece
    u = obs_ref[0:128, :]
    att = [obs_ref[256 + 128 * q : 384 + 128 * q, :] for q in range(4)]
    v = 1.0 - u
    u2, v2 = u * u, v * v
    cubes = [v2 * v, u * v2, u2 * v, u2 * u]
    values = obs_ref[128:256, :]
    for j in range(4):
        spline = None
        for i in range(4):
            if SPLINE[j, i] != 0.0:
                piece = float(SPLINE[j, i]) * cubes[i]
                spline = piece if spline is None else spline + piece
        inner = None
        for q in range(4):
            piece = att[q] * knots[4 * j + q : 4 * j + q + 1, :]
            inner = piece if inner is None else inner + piece
        values = values - spline * inner
    values = values.T
    for p in range(5):
        put_terms(terms_ref, p, gain_ref[NBLK * p : NBLK * p + NBLK, :] * values)
    source_sums(5, 64, terms_ref, high_ref, low_ref, out_ref, *work)


def factor_kernel(own_ref, one_ref, two_ref, three_ref, out_ref):
    entries = {}
    for at, pair in enumerate(PAIR_LIST):
        rows = slice(HIGH * at, HIGH * at + HIGH)
        total = (own_ref[rows, :] + two_ref[rows, :]) + (one_ref[rows, :] + three_ref[rows, :])
        entries[pair] = total + SOURCE_PRIOR if pair[0] == pair[1] else total
    lower = {}
    for column in range(5):
        pivot = entries[column, column]
        for before in range(column):
            pivot = pivot - lower[column, before] * lower[column, before]
        inverse = 1.0 / jnp.sqrt(pivot)
        lower[column, column] = inverse
        for row in range(column + 1, 5):
            running = entries[column, row]
            for before in range(column):
                running = running - lower[row, before] * lower[column, before]
            lower[row, column] = running * inverse
    for at, (first, second) in enumerate(PAIR_LIST):
        out_ref[HIGH * at : HIGH * at + HIGH, :] = lower[second, first]


def solve_kernel(factor_ref, own_ref, one_ref, two_ref, three_ref, out_ref):
    lower = {}
    for at, (first, second) in enumerate(PAIR_LIST):
        lower[second, first] = factor_ref[HIGH * at : HIGH * at + HIGH, :]
    values = []
    for row in range(5):
        rows = slice(HIGH * row, HIGH * row + HIGH)
        running = (own_ref[rows, :] + two_ref[rows, :]) + (one_ref[rows, :] + three_ref[rows, :])
        for before in range(row):
            running = running - lower[row, before] * values[before]
        values.append(running * lower[row, row])
    for row in reversed(range(5)):
        running = values[row]
        for later in range(row + 1, 5):
            running = running - lower[later, row] * values[later]
        values[row] = running * lower[row, row]
    for row in range(5):
        for high in range(HIGH):
            out_ref[row : row + 1, LOW * high : LOW * high + LOW] = values[row][high : high + 1, :]


def f32(*shape):
    return jax.ShapeDtypeStruct(shape, F32)


def kernel_call(body, name, outs, *args, scratch=(), flops=1_000_000, far=(), grant=32, passed=None):
    passed = passed or {}
    place = [pl.ANY if at in far else pltpu.MemorySpace.VMEM for at in range(len(args))]
    out_place = [pl.ANY if at in passed.values() else pltpu.MemorySpace.VMEM for at in range(len(jax.tree.leaves(outs)))]
    out_specs = [pl.BlockSpec(memory_space=at) for at in out_place]
    size = sum(math.prod(a.shape) * 4 for a in args)
    return pl.pallas_call(
        body,
        out_shape=outs,
        in_specs=[pl.BlockSpec(memory_space=at) for at in place],
        out_specs=tuple(out_specs) if isinstance(outs, tuple) else out_specs[0],
        input_output_aliases=passed,
        scratch_shapes=list(scratch),
        compiler_params=pltpu.CompilerParams(vmem_limit_bytes=grant * 1024 * 1024),
        cost_estimate=pl.CostEstimate(flops=flops, bytes_accessed=size, transcendentals=0),
        name=name,
    )(*args)


def segment_scratch(count):
    return (
        pltpu.VMEM((2 * count * NBLK, ROWS), F32),
        pltpu.VMEM((NBLK, ROWS), F32),
        pltpu.VMEM((NBLK, ROWS), F32),
        pltpu.VMEM((LOW, 2 * count * HIGH), F32),
    )


def from_others(values):
    return [
        lax.ppermute(values, "ccd", [(at, (at + shift) % N_CCD) for at in range(N_CCD)]) for shift in range(1, N_CCD)
    ]


def to_windows(values):
    return lax.all_to_all(values, ("src", "win"), split_axis=0, concat_axis=0, tiled=True)


def local(block_bin, block_rows, row_source, obs_resid, obs_phase, att_partial, src_partial):
    bins = block_bin.reshape(1, NBLK)
    rows = block_rows.reshape(1, NBLK)
    gains = jnp.transpose(src_partial, (1, 0, 2)).reshape(5 * NBLK, ROWS)
    send, obs, slots, marked = kernel_call(
        normals_kernel,
        "normals",
        (f32(SLOTS, 128), f32(6 * ROWS, NBLK), f32(8, NBLK), jax.ShapeDtypeStruct((NBLK, ROWS), jnp.int32)),
        bins,
        rows,
        obs_phase,
        att_partial.reshape(4 * NBLK, ROWS),
        obs_resid,
        row_source,
        scratch=(
            pltpu.VMEM((1, NBLK), jnp.int32),
            pltpu.VMEM((1, NBLK), jnp.int32),
            pltpu.VMEM((NBLK, ROWS), F32),
            pltpu.VMEM((4 * NBLK, ROWS), F32),
            pltpu.VMEM((NBLK, ROWS), F32),
            pltpu.VMEM((NBLK, ROWS), jnp.int32),
            pltpu.VMEM((NBLK, NBLK), F32),
            pltpu.SemaphoreType.DMA((6,)),
        ),
        far=range(6),
        grant=56,
    )
    got = to_windows(send.reshape(WINDOWS, CAP, 128)).reshape(SLOTS, 128)
    normal = kernel_call(
        source_normals_kernel,
        "source_normals",
        f32(15 * HIGH, LOW),
        marked,
        gains,
        scratch=segment_scratch(15),
        flops=2 * 480 * 256 * 16384,
    )
    moments = kernel_call(bins_kernel, "bins", f32(FEATS, KNOTS_W), got, normal, far=(1,))
    attitude, reply = kernel_call(
        attitude_kernel,
        "attitude",
        (f32(1, 4, KNOTS_W), f32(WINDOWS, 128)),
        moments,
        *from_others(moments),
        got,
        jnp.asarray(knot_matrix()),
    )
    knots = to_windows(reply)
    factors = kernel_call(factor_kernel, "factors", f32(15 * HIGH, LOW), normal, *from_others(normal))
    right = kernel_call(
        source_right_kernel,
        "source_right",
        f32(5 * HIGH, LOW),
        knots,
        slots,
        obs,
        marked,
        gains,
        scratch=segment_scratch(5),
        flops=2 * 160 * 256 * 16384,
    )
    source_delta = kernel_call(solve_kernel, "solve", f32(5, SRC_DEV), factors, right, *from_others(right))
    return attitude, source_delta


def solution(mesh):
    return jax.shard_map(
        local,
        mesh=mesh,
        in_specs=(
            P(("src", "win", "ccd")),
            P(("src", "win", "ccd")),
            P(("src", "win", "ccd"), None),
            P(("src", "win", "ccd"), None),
            P(("src", "win", "ccd"), None),
            P(("src", "win", "ccd"), None, None),
            P(("src", "win", "ccd"), None, None),
        ),
        out_specs=(P(("src", "win"), None, None), P(None, ("src", "win"))),
        check_vma=False,
    )
```

```python
import math

import jax
import jax.numpy as jnp
import ml_dtypes
import numpy as np
from jax import lax
from jax.experimental import pallas as pl
from jax.experimental.pallas import tpu as pltpu
from jax.sharding import PartitionSpec as P

KNOTS_W = 128
BINS_W = 125
NBLK = 128
ROWS = 128
WINDOWS = 64
CAP = 4
SLOTS = WINDOWS * CAP
SRC_DEV = 4096
ITERS = 8
N_CCD = 4
HIGH = 16
LOW = 256
DOT_BLOCKS = 8

KNOT_PRIOR = 1.0
SOURCE_PRIOR = 1.0
PAIR_LIST = [(first, second) for first in range(5) for second in range(first, 5)]
ATT_PAIRS = [(first, second) for first in range(4) for second in range(first, 4)]
RHS_AT = 70
BIN_AT = 86
FEATS = 88

F32 = jnp.float32
BF16 = jnp.bfloat16
NT = (((1,), (1,)), ((), ()))
NN = (((1,), (0,)), ((), ()))

PIECES = np.array([[1, 0, 0, 0], [4, 12, 6, 1], [1, 6, 12, 4], [0, 0, 0, 1]], np.int64)
SPLINE = PIECES / 6.0


def knot_matrix():
    pair_at = {}
    for at, (first, second) in enumerate(ATT_PAIRS):
        pair_at[first, second] = pair_at[second, first] = at
    table = np.zeros((120, 4 * FEATS), np.float64)
    for d in range(-3, 4):
        for p in range(4):
            for q in range(4):
                row = ((d + 3) * 4 + p) * 4 + q
                for l in range(4):
                    j = l - d
                    if 0 <= j < 4:
                        for m, value in enumerate(np.convolve(PIECES[j], PIECES[l])):
                            table[row, l * FEATS + m * 10 + pair_at[q, p]] += value
    for q in range(4):
        for j in range(4):
            table[112 + q, j * FEATS + RHS_AT + 4 * j + q] = 36.0
            table[116 + q, j * FEATS + RHS_AT + 4 * j + q] = 36.0
    return table.astype(ml_dtypes.bfloat16)


def split_parts(values, count):
    parts = []
    for at in range(count):
        part = values.astype(BF16)
        parts.append(part)
        if at + 1 < count:
            values = values - part.astype(F32)
    return parts


def exact_dot(values, ones, dims, swap=False):
    total = None
    for part in split_parts(values, 3):
        pair = (ones, part) if swap else (part, ones)
        piece = lax.dot_general(*pair, dims, preferred_element_type=F32)
        total = piece if total is None else total + piece
    return total


def indicator(condition):
    return jnp.where(condition, 1.0, 0.0).astype(BF16)


def iota(shape, axis):
    return lax.broadcasted_iota(jnp.int32, shape, axis)


def iota_f(shape, axis):
    return iota(shape, axis).astype(F32)


def normals_kernel(*refs):
    given, (send_ref, obs_ref, slot_ref, marked_ref), here = refs[:6], refs[6:10], refs[10:16]
    pay_ref, done_ref = refs[16:]
    bin_ref, rows_ref, phase_ref, att_ref, resid_ref, source_ref = here
    copies = [pltpu.make_async_copy(given[at], here[at], done_ref.at[at]) for at in range(6)]
    for copy in copies:
        copy.start()
    square = (NBLK, NBLK)
    copies[0].wait()
    bins = bin_ref[...].astype(F32)
    window = jnp.floor((bins + 0.5) * (1.0 / BINS_W))
    local_bin = bins - BINS_W * window
    window_column = jnp.broadcast_to(window, square).T
    earlier = jnp.where(window_column == window, 1.0, 0.0) * jnp.where(iota(square, 0) < iota(square, 1), 1.0, 0.0)
    rank = jnp.sum(earlier, axis=0, keepdims=True)
    slot_ref[...] = jnp.concatenate([window, rank, jnp.zeros((6, NBLK), F32)], axis=0)
    place = indicator(iota_f((SLOTS, NBLK), 0) == CAP * window + rank)
    copies[1].wait()
    mask = iota(square, 0) < rows_ref[...]
    used = jnp.broadcast_to(rows_ref[...].astype(F32), square).T
    for copy in copies[2:]:
        copy.wait()
    marked_ref[...] = jnp.where(iota_f(square, 1) < used, source_ref[...], -LOW)
    u = phase_ref[...].T
    resid = jnp.where(mask, resid_ref[...].T, 0.0)
    att = [jnp.where(mask, att_ref[pl.ds(q, NBLK, stride=4), :].T, 0.0) for q in range(4)]
    obs_ref[0:128, :] = u
    obs_ref[128:256, :] = resid
    for q in range(4):
        obs_ref[256 + 128 * q : 384 + 128 * q, :] = att[q]
    v = 1.0 - u
    u2, v2 = u * u, v * v
    u3, v3 = u2 * u, v2 * v
    cubes = [v3, u * v2, u2 * v, u3]
    powers = [v3 * v3, u * v2 * v3, u2 * v2 * v2, u3 * v3, u2 * u2 * v2, u3 * u2 * v, u3 * u3]
    for at, (first, second) in enumerate(ATT_PAIRS):
        product = att[first] * att[second]
        for m in range(7):
            row = m * 10 + at
            pay_ref[row : row + 1, :] = jnp.sum(powers[m] * product, axis=0, keepdims=True)
    for q in range(4):
        product = att[q] * resid
        sums = [jnp.sum(cubes[i] * product, axis=0, keepdims=True) for i in range(4)]
        for j in range(4):
            total = None
            for i in range(4):
                if SPLINE[j, i] != 0.0:
                    piece = float(SPLINE[j, i]) * sums[i]
                    total = piece if total is None else total + piece
            row = RHS_AT + 4 * j + q
            pay_ref[row : row + 1, :] = total
    pay_ref[BIN_AT : BIN_AT + 1, :] = local_bin
    pay_ref[BIN_AT + 1 :, :] = jnp.zeros((NBLK - BIN_AT - 1, NBLK), F32)
    send_ref[...] = exact_dot(pay_ref[...], place, NT, swap=True)


def bins_kernel(got_ref, after_ref, out_ref):
    del after_ref
    got = got_ref[...].T
    place = indicator(iota_f((KNOTS_W, SLOTS), 0) == got[BIN_AT : BIN_AT + 1, :])
    moments = exact_dot(got[:FEATS], place, NT)
    for at in range(N_CCD):
        out_ref[at] = moments


def attitude_kernel(parts_ref, got_ref, table_ref, normal_ref, att_ref, reply_ref, passed_ref):
    del normal_ref, passed_ref
    total = ((parts_ref[0] + parts_ref[1]) + (parts_ref[2] + parts_ref[3])) * (1.0 / 36.0)
    moved = jnp.concatenate([total] + [pltpu.roll(total, l, 1) for l in range(1, 4)], axis=0)
    band = exact_dot(moved, table_ref[...], NN, swap=True)
    groups = [band[8 * at : 8 * at + 8] for at in range(14)]
    lower_half = iota((8, KNOTS_W), 0) < 4

    def doubled(values):
        return values + pltpu.roll(values, 4, 0)

    def norm(values):
        return jnp.sum(jnp.sum(values, axis=1, keepdims=True), axis=0, keepdims=True)

    def apply(vector):
        spread = [
            jnp.where(lower_half, vector[2 * at : 2 * at + 1, :], vector[2 * at + 1 : 2 * at + 2, :]) for at in range(2)
        ]
        pieces = []
        for d in range(-3, 4):
            piece = groups[2 * (d + 3)] * spread[0] + groups[2 * (d + 3) + 1] * spread[1]
            pieces.append(pltpu.roll(piece, -d % KNOTS_W, 1) if d else piece)
        outer = (pieces[0] + pieces[1]) + (pieces[2] + pieces[4])
        return KNOT_PRIOR * vector + doubled(outer + ((pieces[5] + pieces[6]) + pieces[3]))

    residual = band[112:120]
    direction = residual
    estimate = jnp.zeros_like(residual)
    for iteration in range(ITERS):
        applied = apply(direction)
        norm_now = norm(residual * residual)
        inverse = 1.0 / norm(direction * applied)
        across = norm(residual * applied)
        applied_norm = norm(applied * applied)
        step_size = norm_now * inverse
        estimate = estimate + step_size * direction
        residual = residual - step_size * applied
        if iteration + 1 < ITERS:
            ratio = 1.0 - 2.0 * (across * inverse) + step_size * (applied_norm * inverse)
            direction = residual + ratio * direction
    att_ref[0] = estimate[:4]
    moved = jnp.concatenate([estimate[:4]] + [pltpu.roll(estimate, KNOTS_W - j, 1)[:4] for j in range(1, 4)], axis=0)
    column = jnp.concatenate(
        [got_ref[pl.ds(s, WINDOWS, stride=CAP), :][:, BIN_AT : BIN_AT + 1] for s in range(CAP)], axis=0
    )
    place = indicator(iota_f((SLOTS, KNOTS_W), 1) == column)
    knots = exact_dot(moved, place, NT, swap=True)
    reply_ref[...] = jnp.zeros((WINDOWS, 128), F32)
    for s in range(CAP):
        reply_ref[:, 16 * s : 16 * s + 16] = knots[WINDOWS * s : WINDOWS * s + WINDOWS]


def source_sums(count, chunk, terms_ref, high_ref, low_ref, out_ref, acc_ref):
    high_at = iota_f((HIGH, ROWS), 0)
    low_at = iota_f((LOW, ROWS), 0).astype(BF16)
    one, zero = jnp.ones((), BF16), jnp.zeros((), BF16)

    def factors(block):
        here = high_at == high_ref[pl.ds(block, 1), :]
        low = jnp.broadcast_to(low_ref[pl.ds(block, 1), :], (HIGH, ROWS)).astype(BF16)
        low = jnp.concatenate([low] * (LOW // HIGH), axis=0)
        terms = [
            jnp.where(here, terms_ref[pl.ds(c * NBLK + block, 1), :], 0.0).astype(BF16) for c in range(2 * count)
        ]
        return jnp.concatenate(terms, axis=0), jnp.where(low_at == low, one, zero)

    def step(at, carry):
        for first in range(0, chunk, DOT_BLOCKS):
            pairs = [factors(at * chunk + first + inner) for inner in range(DOT_BLOCKS)]
            terms = jnp.concatenate([pair[0] for pair in pairs], axis=1)
            ones = jnp.concatenate([pair[1] for pair in pairs], axis=1)
            acc_ref[...] += lax.dot_general(ones, terms, NT, preferred_element_type=F32)
        return carry

    acc_ref[...] = jnp.zeros(acc_ref.shape, F32)
    lax.fori_loop(0, NBLK // chunk, step, 0)
    sums = acc_ref[...].T
    for c in range(count):
        at = 2 * c * HIGH
        out_ref[HIGH * c : HIGH * c + HIGH, :] = sums[at : at + HIGH] + sums[at + HIGH : at + 2 * HIGH]


def put_terms(terms_ref, c, values):
    large = values.astype(BF16).astype(F32)
    terms_ref[2 * c * NBLK : (2 * c + 1) * NBLK, :] = large
    terms_ref[(2 * c + 1) * NBLK : (2 * c + 2) * NBLK, :] = values - large


def put_sources(marked_ref, high_ref, low_ref):
    source = marked_ref[...]
    high = source >> 8
    high_ref[...] = high.astype(F32)
    low_ref[...] = (source - (high << 8)).astype(F32)


def source_normals_kernel(marked_ref, gain_ref, out_ref, terms_ref, high_ref, low_ref, *work):
    put_sources(marked_ref, high_ref, low_ref)
    gains = [gain_ref[NBLK * p : NBLK * p + NBLK, :] for p in range(5)]
    for at, (first, second) in enumerate(PAIR_LIST):
        put_terms(terms_ref, at, gains[first] * gains[second])
    source_sums(15, 32, terms_ref, high_ref, low_ref, out_ref, *work)


def source_right_kernel(
    reply_ref, slot_ref, obs_ref, marked_ref, gain_ref, out_ref, terms_ref, high_ref, low_ref, *work
):
    put_sources(marked_ref, high_ref, low_ref)
    place = indicator(iota_f((WINDOWS, NBLK), 0) == slot_ref[0:1, :])
    rank = slot_ref[1:2, :]
    spread = exact_dot(reply_ref[...].T, place, NN)
    knots = None
    for s in range(CAP):
        piece = jnp.where(rank == float(s), spread[16 * s : 16 * s + 16, :], 0.0)
        knots = piece if knots is None else knots + piece
    u = obs_ref[0:128, :]
    att = [obs_ref[256 + 128 * q : 384 + 128 * q, :] for q in range(4)]
    v = 1.0 - u
    u2, v2 = u * u, v * v
    cubes = [v2 * v, u * v2, u2 * v, u2 * u]
    values = obs_ref[128:256, :]
    for j in range(4):
        spline = None
        for i in range(4):
            if SPLINE[j, i] != 0.0:
                piece = float(SPLINE[j, i]) * cubes[i]
                spline = piece if spline is None else spline + piece
        inner = None
        for q in range(4):
            piece = att[q] * knots[4 * j + q : 4 * j + q + 1, :]
            inner = piece if inner is None else inner + piece
        values = values - spline * inner
    values = values.T
    for p in range(5):
        put_terms(terms_ref, p, gain_ref[NBLK * p : NBLK * p + NBLK, :] * values)
    source_sums(5, NBLK, terms_ref, high_ref, low_ref, out_ref, *work)


def factor_kernel(own_ref, one_ref, two_ref, three_ref, out_ref):
    entries = {}
    for at, pair in enumerate(PAIR_LIST):
        rows = slice(HIGH * at, HIGH * at + HIGH)
        total = (own_ref[rows, :] + two_ref[rows, :]) + (one_ref[rows, :] + three_ref[rows, :])
        entries[pair] = total + SOURCE_PRIOR if pair[0] == pair[1] else total
    lower = {}
    for column in range(5):
        pivot = entries[column, column]
        for before in range(column):
            pivot = pivot - lower[column, before] * lower[column, before]
        inverse = 1.0 / jnp.sqrt(pivot)
        lower[column, column] = inverse
        for row in range(column + 1, 5):
            running = entries[column, row]
            for before in range(column):
                running = running - lower[row, before] * lower[column, before]
            lower[row, column] = running * inverse
    for at, (first, second) in enumerate(PAIR_LIST):
        out_ref[HIGH * at : HIGH * at + HIGH, :] = lower[second, first]


def solve_kernel(factor_ref, own_ref, one_ref, two_ref, three_ref, out_ref):
    lower = {}
    for at, (first, second) in enumerate(PAIR_LIST):
        lower[second, first] = factor_ref[HIGH * at : HIGH * at + HIGH, :]
    values = []
    for row in range(5):
        rows = slice(HIGH * row, HIGH * row + HIGH)
        running = (own_ref[rows, :] + two_ref[rows, :]) + (one_ref[rows, :] + three_ref[rows, :])
        for before in range(row):
            running = running - lower[row, before] * values[before]
        values.append(running * lower[row, row])
    for row in reversed(range(5)):
        running = values[row]
        for later in range(row + 1, 5):
            running = running - lower[later, row] * values[later]
        values[row] = running * lower[row, row]
    for row in range(5):
        for high in range(HIGH):
            out_ref[row : row + 1, LOW * high : LOW * high + LOW] = values[row][high : high + 1, :]


def f32(*shape):
    return jax.ShapeDtypeStruct(shape, F32)


def kernel_call(body, name, outs, *args, scratch=(), flops=1_000_000, far=(), grant=32, passed=None):
    passed = passed or {}
    place = [pl.ANY if at in far else pltpu.MemorySpace.VMEM for at in range(len(args))]
    out_place = [pl.ANY if at in passed.values() else pltpu.MemorySpace.VMEM for at in range(len(jax.tree.leaves(outs)))]
    out_specs = [pl.BlockSpec(memory_space=at) for at in out_place]
    size = sum(math.prod(a.shape) * 4 for a in args)
    return pl.pallas_call(
        body,
        out_shape=outs,
        in_specs=[pl.BlockSpec(memory_space=at) for at in place],
        out_specs=tuple(out_specs) if isinstance(outs, tuple) else out_specs[0],
        input_output_aliases=passed,
        scratch_shapes=list(scratch),
        compiler_params=pltpu.CompilerParams(vmem_limit_bytes=grant * 1024 * 1024),
        cost_estimate=pl.CostEstimate(flops=flops, bytes_accessed=size, transcendentals=0),
        name=name,
    )(*args)


def segment_scratch(count):
    return (
        pltpu.VMEM((2 * count * NBLK, ROWS), F32),
        pltpu.VMEM((NBLK, ROWS), F32),
        pltpu.VMEM((NBLK, ROWS), F32),
        pltpu.VMEM((LOW, 2 * count * HIGH), F32),
    )


def from_others(values):
    return [
        lax.ppermute(values, "ccd", [(at, (at + shift) % N_CCD) for at in range(N_CCD)]) for shift in range(1, N_CCD)
    ]


def among_ccd(copies):
    return lax.all_to_all(copies, "ccd", split_axis=0, concat_axis=0, tiled=True)


def to_windows(values):
    return lax.all_to_all(values, ("src", "win"), split_axis=0, concat_axis=0, tiled=True)


def local(block_bin, block_rows, row_source, obs_resid, obs_phase, att_partial, src_partial):
    bins = block_bin.reshape(1, NBLK)
    rows = block_rows.reshape(1, NBLK)
    gains = jnp.transpose(src_partial, (1, 0, 2)).reshape(5 * NBLK, ROWS)
    send, obs, slots, marked = kernel_call(
        normals_kernel,
        "normals",
        (f32(SLOTS, 128), f32(6 * ROWS, NBLK), f32(8, NBLK), jax.ShapeDtypeStruct((NBLK, ROWS), jnp.int32)),
        bins,
        rows,
        obs_phase,
        att_partial.reshape(4 * NBLK, ROWS),
        obs_resid,
        row_source,
        scratch=(
            pltpu.VMEM((1, NBLK), jnp.int32),
            pltpu.VMEM((1, NBLK), jnp.int32),
            pltpu.VMEM((NBLK, ROWS), F32),
            pltpu.VMEM((4 * NBLK, ROWS), F32),
            pltpu.VMEM((NBLK, ROWS), F32),
            pltpu.VMEM((NBLK, ROWS), jnp.int32),
            pltpu.VMEM((NBLK, NBLK), F32),
            pltpu.SemaphoreType.DMA((6,)),
        ),
        far=range(6),
        grant=56,
    )
    got = to_windows(send.reshape(WINDOWS, CAP, 128)).reshape(SLOTS, 128)
    normal = kernel_call(
        source_normals_kernel,
        "source_normals",
        f32(15 * HIGH, LOW),
        marked,
        gains,
        scratch=segment_scratch(15),
        flops=2 * 480 * 256 * 16384,
    )
    moments = kernel_call(bins_kernel, "bins", f32(N_CCD, FEATS, KNOTS_W), got, normal, far=(1,))
    attitude, reply, normal = kernel_call(
        attitude_kernel,
        "attitude",
        (f32(1, 4, KNOTS_W), f32(WINDOWS, 128), f32(15 * HIGH, LOW)),
        among_ccd(moments),
        got,
        jnp.asarray(knot_matrix()),
        normal,
        far=(3,),
        passed={3: 2},
    )
    knots = to_windows(reply)
    factors = kernel_call(factor_kernel, "factors", f32(15 * HIGH, LOW), normal, *from_others(normal))
    right = kernel_call(
        source_right_kernel,
        "source_right",
        f32(5 * HIGH, LOW),
        knots,
        slots,
        obs,
        marked,
        gains,
        scratch=segment_scratch(5),
        flops=2 * 160 * 256 * 16384,
    )
    source_delta = kernel_call(solve_kernel, "solve", f32(5, SRC_DEV), factors, right, *from_others(right))
    return attitude, source_delta


def solution(mesh):
    return jax.shard_map(
        local,
        mesh=mesh,
        in_specs=(
            P(("src", "win", "ccd")),
            P(("src", "win", "ccd")),
            P(("src", "win", "ccd"), None),
            P(("src", "win", "ccd"), None),
            P(("src", "win", "ccd"), None),
            P(("src", "win", "ccd"), None, None),
            P(("src", "win", "ccd"), None, None),
        ),
        out_specs=(P(("src", "win"), None, None), P(None, ("src", "win"))),
        check_vma=False,
    )
```

```python
import math

import jax
import jax.numpy as jnp
import ml_dtypes
import numpy as np
from jax import lax
from jax.experimental import pallas as pl
from jax.experimental.pallas import tpu as pltpu
from jax.sharding import PartitionSpec as P

KNOTS_W = 128
BINS_W = 125
NBLK = 128
ROWS = 128
WINDOWS = 64
CAP = 4
SLOTS = WINDOWS * CAP
SRC_DEV = 4096
ITERS = 8
N_CCD = 4
HIGH = 16
LOW = 256
DOT_BLOCKS = 8

KNOT_PRIOR = 1.0
SOURCE_PRIOR = 1.0
PAIR_LIST = [(first, second) for first in range(5) for second in range(first, 5)]
ATT_PAIRS = [(first, second) for first in range(4) for second in range(first, 4)]
RHS_AT = 70
BIN_AT = 86
FEATS = 88

F32 = jnp.float32
BF16 = jnp.bfloat16
NT = (((1,), (1,)), ((), ()))
NN = (((1,), (0,)), ((), ()))

PIECES = np.array([[1, 0, 0, 0], [4, 12, 6, 1], [1, 6, 12, 4], [0, 0, 0, 1]], np.int64)
SPLINE = PIECES / 6.0


def knot_matrix():
    pair_at = {}
    for at, (first, second) in enumerate(ATT_PAIRS):
        pair_at[first, second] = pair_at[second, first] = at
    table = np.zeros((120, 4 * FEATS), np.float64)
    for d in range(-3, 4):
        for p in range(4):
            for q in range(4):
                row = ((d + 3) * 4 + p) * 4 + q
                for l in range(4):
                    j = l - d
                    if 0 <= j < 4:
                        for m, value in enumerate(np.convolve(PIECES[j], PIECES[l])):
                            table[row, l * FEATS + m * 10 + pair_at[q, p]] += value
    for q in range(4):
        for j in range(4):
            table[112 + q, j * FEATS + RHS_AT + 4 * j + q] = 36.0
            table[116 + q, j * FEATS + RHS_AT + 4 * j + q] = 36.0
    return table.astype(ml_dtypes.bfloat16)


def split_parts(values, count):
    parts = []
    for at in range(count):
        part = values.astype(BF16)
        parts.append(part)
        if at + 1 < count:
            values = values - part.astype(F32)
    return parts


def exact_dot(values, ones, dims, swap=False):
    total = None
    for part in split_parts(values, 3):
        pair = (ones, part) if swap else (part, ones)
        piece = lax.dot_general(*pair, dims, preferred_element_type=F32)
        total = piece if total is None else total + piece
    return total


def indicator(condition):
    return jnp.where(condition, 1.0, 0.0).astype(BF16)


def iota(shape, axis):
    return lax.broadcasted_iota(jnp.int32, shape, axis)


def iota_f(shape, axis):
    return iota(shape, axis).astype(F32)


def normals_kernel(*refs):
    given, (send_ref, obs_ref, slot_ref, marked_ref), here = refs[:6], refs[6:10], refs[10:16]
    pay_ref, done_ref = refs[16:]
    bin_ref, rows_ref, phase_ref, att_ref, resid_ref, source_ref = here
    copies = [pltpu.make_async_copy(given[at], here[at], done_ref.at[at]) for at in range(6)]
    for copy in copies:
        copy.start()
    square = (NBLK, NBLK)
    copies[0].wait()
    bins = bin_ref[...].astype(F32)
    window = jnp.floor((bins + 0.5) * (1.0 / BINS_W))
    local_bin = bins - BINS_W * window
    window_column = jnp.broadcast_to(window, square).T
    earlier = jnp.where(window_column == window, 1.0, 0.0) * jnp.where(iota(square, 0) < iota(square, 1), 1.0, 0.0)
    rank = jnp.sum(earlier, axis=0, keepdims=True)
    slot_ref[...] = jnp.concatenate([window, rank, jnp.zeros((6, NBLK), F32)], axis=0)
    place = indicator(iota_f((SLOTS, NBLK), 0) == CAP * window + rank)
    copies[1].wait()
    mask = iota(square, 0) < rows_ref[...]
    used = jnp.broadcast_to(rows_ref[...].astype(F32), square).T
    for copy in copies[2:]:
        copy.wait()
    marked_ref[...] = jnp.where(iota_f(square, 1) < used, source_ref[...], -LOW)
    u = phase_ref[...].T
    resid = jnp.where(mask, resid_ref[...].T, 0.0)
    att = [jnp.where(mask, att_ref[pl.ds(q, NBLK, stride=4), :].T, 0.0) for q in range(4)]
    obs_ref[0:128, :] = u
    obs_ref[128:256, :] = resid
    for q in range(4):
        obs_ref[256 + 128 * q : 384 + 128 * q, :] = att[q]
    v = 1.0 - u
    u2, v2 = u * u, v * v
    u3, v3 = u2 * u, v2 * v
    cubes = [v3, u * v2, u2 * v, u3]
    powers = [v3 * v3, u * v2 * v3, u2 * v2 * v2, u3 * v3, u2 * u2 * v2, u3 * u2 * v, u3 * u3]
    for at, (first, second) in enumerate(ATT_PAIRS):
        product = att[first] * att[second]
        for m in range(7):
            row = m * 10 + at
            pay_ref[row : row + 1, :] = jnp.sum(powers[m] * product, axis=0, keepdims=True)
    for q in range(4):
        product = att[q] * resid
        sums = [jnp.sum(cubes[i] * product, axis=0, keepdims=True) for i in range(4)]
        for j in range(4):
            total = None
            for i in range(4):
                if SPLINE[j, i] != 0.0:
                    piece = float(SPLINE[j, i]) * sums[i]
                    total = piece if total is None else total + piece
            row = RHS_AT + 4 * j + q
            pay_ref[row : row + 1, :] = total
    pay_ref[BIN_AT : BIN_AT + 1, :] = local_bin
    pay_ref[BIN_AT + 1 :, :] = jnp.zeros((NBLK - BIN_AT - 1, NBLK), F32)
    send_ref[...] = exact_dot(pay_ref[...], place, NT, swap=True)


def bins_kernel(got_ref, after_ref, out_ref):
    del after_ref
    got = got_ref[...].T
    place = indicator(iota_f((KNOTS_W, SLOTS), 0) == got[BIN_AT : BIN_AT + 1, :])
    out_ref[...] = exact_dot(got[:FEATS], place, NT)


def attitude_kernel(own_ref, one_ref, two_ref, three_ref, got_ref, table_ref, after_ref, att_ref, reply_ref):
    del after_ref
    total = ((own_ref[...] + two_ref[...]) + (one_ref[...] + three_ref[...])) * (1.0 / 36.0)
    moved = jnp.concatenate([total] + [pltpu.roll(total, l, 1) for l in range(1, 4)], axis=0)
    band = exact_dot(moved, table_ref[...], NN, swap=True)
    groups = [band[8 * at : 8 * at + 8] for at in range(14)]
    lower_half = iota((8, KNOTS_W), 0) < 4

    def doubled(values):
        return values + pltpu.roll(values, 4, 0)

    def norm(values):
        return jnp.sum(jnp.sum(values, axis=1, keepdims=True), axis=0, keepdims=True)

    def apply(vector):
        spread = [
            jnp.where(lower_half, vector[2 * at : 2 * at + 1, :], vector[2 * at + 1 : 2 * at + 2, :]) for at in range(2)
        ]
        pieces = []
        for d in range(-3, 4):
            piece = groups[2 * (d + 3)] * spread[0] + groups[2 * (d + 3) + 1] * spread[1]
            pieces.append(pltpu.roll(piece, -d % KNOTS_W, 1) if d else piece)
        outer = (pieces[0] + pieces[1]) + (pieces[2] + pieces[4])
        return KNOT_PRIOR * vector + doubled(outer + ((pieces[5] + pieces[6]) + pieces[3]))

    residual = band[112:120]
    direction = residual
    estimate = jnp.zeros_like(residual)
    for iteration in range(ITERS):
        applied = apply(direction)
        norm_now = norm(residual * residual)
        inverse = 1.0 / norm(direction * applied)
        across = norm(residual * applied)
        applied_norm = norm(applied * applied)
        step_size = norm_now * inverse
        estimate = estimate + step_size * direction
        residual = residual - step_size * applied
        if iteration + 1 < ITERS:
            ratio = 1.0 - 2.0 * (across * inverse) + step_size * (applied_norm * inverse)
            direction = residual + ratio * direction
    att_ref[0] = estimate[:4]
    moved = jnp.concatenate([estimate[:4]] + [pltpu.roll(estimate, KNOTS_W - j, 1)[:4] for j in range(1, 4)], axis=0)
    column = jnp.concatenate(
        [got_ref[pl.ds(s, WINDOWS, stride=CAP), :][:, BIN_AT : BIN_AT + 1] for s in range(CAP)], axis=0
    )
    place = indicator(iota_f((SLOTS, KNOTS_W), 1) == column)
    knots = exact_dot(moved, place, NT, swap=True)
    reply_ref[...] = jnp.zeros((WINDOWS, 128), F32)
    for s in range(CAP):
        reply_ref[:, 16 * s : 16 * s + 16] = knots[WINDOWS * s : WINDOWS * s + WINDOWS]


def source_sums(count, chunk, terms_ref, high_ref, low_ref, out_ref, acc_ref):
    high_at = iota_f((HIGH, ROWS), 0)
    low_at = iota_f((LOW, ROWS), 0).astype(BF16)
    one, zero = jnp.ones((), BF16), jnp.zeros((), BF16)

    def factors(block):
        here = high_at == high_ref[pl.ds(block, 1), :]
        low = jnp.broadcast_to(low_ref[pl.ds(block, 1), :], (HIGH, ROWS)).astype(BF16)
        low = jnp.concatenate([low] * (LOW // HIGH), axis=0)
        terms = [
            jnp.where(here, terms_ref[pl.ds(c * NBLK + block, 1), :], 0.0).astype(BF16) for c in range(2 * count)
        ]
        return jnp.concatenate(terms, axis=0), jnp.where(low_at == low, one, zero)

    def step(at, carry):
        for first in range(0, chunk, DOT_BLOCKS):
            pairs = [factors(at * chunk + first + inner) for inner in range(DOT_BLOCKS)]
            terms = jnp.concatenate([pair[0] for pair in pairs], axis=1)
            ones = jnp.concatenate([pair[1] for pair in pairs], axis=1)
            acc_ref[...] += lax.dot_general(ones, terms, NT, preferred_element_type=F32)
        return carry

    acc_ref[...] = jnp.zeros(acc_ref.shape, F32)
    lax.fori_loop(0, NBLK // chunk, step, 0)
    sums = acc_ref[...].T
    for c in range(count):
        at = 2 * c * HIGH
        out_ref[HIGH * c : HIGH * c + HIGH, :] = sums[at : at + HIGH] + sums[at + HIGH : at + 2 * HIGH]


def put_terms(terms_ref, c, values):
    large = values.astype(BF16).astype(F32)
    terms_ref[2 * c * NBLK : (2 * c + 1) * NBLK, :] = large
    terms_ref[(2 * c + 1) * NBLK : (2 * c + 2) * NBLK, :] = values - large


def put_sources(marked_ref, high_ref, low_ref):
    source = marked_ref[...]
    high = source >> 8
    high_ref[...] = high.astype(F32)
    low_ref[...] = (source - (high << 8)).astype(F32)


def source_normals_kernel(marked_ref, gain_ref, out_ref, terms_ref, high_ref, low_ref, *work):
    put_sources(marked_ref, high_ref, low_ref)
    gains = [gain_ref[NBLK * p : NBLK * p + NBLK, :] for p in range(5)]
    for at, (first, second) in enumerate(PAIR_LIST):
        put_terms(terms_ref, at, gains[first] * gains[second])
    source_sums(15, 32, terms_ref, high_ref, low_ref, out_ref, *work)


def source_right_kernel(
    reply_ref, slot_ref, obs_ref, marked_ref, gain_ref, out_ref, terms_ref, high_ref, low_ref, *work
):
    put_sources(marked_ref, high_ref, low_ref)
    place = indicator(iota_f((WINDOWS, NBLK), 0) == slot_ref[0:1, :])
    rank = slot_ref[1:2, :]
    spread = exact_dot(reply_ref[...].T, place, NN)
    knots = None
    for s in range(CAP):
        piece = jnp.where(rank == float(s), spread[16 * s : 16 * s + 16, :], 0.0)
        knots = piece if knots is None else knots + piece
    u = obs_ref[0:128, :]
    att = [obs_ref[256 + 128 * q : 384 + 128 * q, :] for q in range(4)]
    v = 1.0 - u
    u2, v2 = u * u, v * v
    cubes = [v2 * v, u * v2, u2 * v, u2 * u]
    values = obs_ref[128:256, :]
    for j in range(4):
        spline = None
        for i in range(4):
            if SPLINE[j, i] != 0.0:
                piece = float(SPLINE[j, i]) * cubes[i]
                spline = piece if spline is None else spline + piece
        inner = None
        for q in range(4):
            piece = att[q] * knots[4 * j + q : 4 * j + q + 1, :]
            inner = piece if inner is None else inner + piece
        values = values - spline * inner
    values = values.T
    for p in range(5):
        put_terms(terms_ref, p, gain_ref[NBLK * p : NBLK * p + NBLK, :] * values)
    source_sums(5, NBLK, terms_ref, high_ref, low_ref, out_ref, *work)


def pair_kernel(own_ref, other_ref, out_ref):
    out_ref[...] = own_ref[...] + other_ref[...]


def factor_kernel(own_ref, other_ref, after_ref, out_ref):
    del after_ref
    entries = {}
    for at, pair in enumerate(PAIR_LIST):
        rows = slice(HIGH * at, HIGH * at + HIGH)
        total = own_ref[rows, :] + other_ref[rows, :]
        entries[pair] = total + SOURCE_PRIOR if pair[0] == pair[1] else total
    lower = {}
    for column in range(5):
        pivot = entries[column, column]
        for before in range(column):
            pivot = pivot - lower[column, before] * lower[column, before]
        inverse = 1.0 / jnp.sqrt(pivot)
        lower[column, column] = inverse
        for row in range(column + 1, 5):
            running = entries[column, row]
            for before in range(column):
                running = running - lower[row, before] * lower[column, before]
            lower[row, column] = running * inverse
    for at, (first, second) in enumerate(PAIR_LIST):
        out_ref[HIGH * at : HIGH * at + HIGH, :] = lower[second, first]


def solve_kernel(factor_ref, own_ref, one_ref, two_ref, three_ref, out_ref):
    lower = {}
    for at, (first, second) in enumerate(PAIR_LIST):
        lower[second, first] = factor_ref[HIGH * at : HIGH * at + HIGH, :]
    values = []
    for row in range(5):
        rows = slice(HIGH * row, HIGH * row + HIGH)
        running = (own_ref[rows, :] + two_ref[rows, :]) + (one_ref[rows, :] + three_ref[rows, :])
        for before in range(row):
            running = running - lower[row, before] * values[before]
        values.append(running * lower[row, row])
    for row in reversed(range(5)):
        running = values[row]
        for later in range(row + 1, 5):
            running = running - lower[later, row] * values[later]
        values[row] = running * lower[row, row]
    for row in range(5):
        for high in range(HIGH):
            out_ref[row : row + 1, LOW * high : LOW * high + LOW] = values[row][high : high + 1, :]


def f32(*shape):
    return jax.ShapeDtypeStruct(shape, F32)


def kernel_call(body, name, outs, *args, scratch=(), flops=1_000_000, far=(), grant=32, passed=None):
    passed = passed or {}
    place = [pl.ANY if at in far else pltpu.MemorySpace.VMEM for at in range(len(args))]
    out_place = [pl.ANY if at in passed.values() else pltpu.MemorySpace.VMEM for at in range(len(jax.tree.leaves(outs)))]
    out_specs = [pl.BlockSpec(memory_space=at) for at in out_place]
    size = sum(math.prod(a.shape) * 4 for a in args)
    return pl.pallas_call(
        body,
        out_shape=outs,
        in_specs=[pl.BlockSpec(memory_space=at) for at in place],
        out_specs=tuple(out_specs) if isinstance(outs, tuple) else out_specs[0],
        input_output_aliases=passed,
        scratch_shapes=list(scratch),
        compiler_params=pltpu.CompilerParams(vmem_limit_bytes=grant * 1024 * 1024),
        cost_estimate=pl.CostEstimate(flops=flops, bytes_accessed=size, transcendentals=0),
        name=name,
    )(*args)


def segment_scratch(count):
    return (
        pltpu.VMEM((2 * count * NBLK, ROWS), F32),
        pltpu.VMEM((NBLK, ROWS), F32),
        pltpu.VMEM((NBLK, ROWS), F32),
        pltpu.VMEM((LOW, 2 * count * HIGH), F32),
    )


def swapped(values, partner):
    return lax.ppermute(values, "ccd", list(enumerate(partner)))


def from_others(values):
    return [
        lax.ppermute(values, "ccd", [(at, (at + shift) % N_CCD) for at in range(N_CCD)]) for shift in range(1, N_CCD)
    ]


def to_windows(values):
    return lax.all_to_all(values, ("src", "win"), split_axis=0, concat_axis=0, tiled=True)


def local(block_bin, block_rows, row_source, obs_resid, obs_phase, att_partial, src_partial):
    bins = block_bin.reshape(1, NBLK)
    rows = block_rows.reshape(1, NBLK)
    gains = jnp.transpose(src_partial, (1, 0, 2)).reshape(5 * NBLK, ROWS)
    send, obs, slots, marked = kernel_call(
        normals_kernel,
        "normals",
        (f32(SLOTS, 128), f32(6 * ROWS, NBLK), f32(8, NBLK), jax.ShapeDtypeStruct((NBLK, ROWS), jnp.int32)),
        bins,
        rows,
        obs_phase,
        att_partial.reshape(4 * NBLK, ROWS),
        obs_resid,
        row_source,
        scratch=(
            pltpu.VMEM((1, NBLK), jnp.int32),
            pltpu.VMEM((1, NBLK), jnp.int32),
            pltpu.VMEM((NBLK, ROWS), F32),
            pltpu.VMEM((4 * NBLK, ROWS), F32),
            pltpu.VMEM((NBLK, ROWS), F32),
            pltpu.VMEM((NBLK, ROWS), jnp.int32),
            pltpu.VMEM((NBLK, NBLK), F32),
            pltpu.SemaphoreType.DMA((6,)),
        ),
        far=range(6),
        grant=56,
    )
    got = to_windows(send.reshape(WINDOWS, CAP, 128)).reshape(SLOTS, 128)
    normal = kernel_call(
        source_normals_kernel,
        "source_normals",
        f32(15 * HIGH, LOW),
        marked,
        gains,
        scratch=segment_scratch(15),
        flops=2 * 480 * 256 * 16384,
    )
    moments = kernel_call(bins_kernel, "bins", f32(FEATS, KNOTS_W), got, normal, far=(1,))
    normal = kernel_call(pair_kernel, "pairs", f32(15 * HIGH, LOW), normal, swapped(normal, (1, 0, 3, 2)))
    other = swapped(normal, (3, 2, 1, 0))
    attitude, reply = kernel_call(
        attitude_kernel,
        "attitude",
        (f32(1, 4, KNOTS_W), f32(WINDOWS, 128)),
        moments,
        *from_others(moments),
        got,
        jnp.asarray(knot_matrix()),
        normal,
        far=(6,),
    )
    knots = to_windows(reply)
    right = kernel_call(
        source_right_kernel,
        "source_right",
        f32(5 * HIGH, LOW),
        knots,
        slots,
        obs,
        marked,
        gains,
        scratch=segment_scratch(5),
        flops=2 * 160 * 256 * 16384,
    )
    factors = kernel_call(factor_kernel, "factors", f32(15 * HIGH, LOW), normal, other, right, far=(2,))
    source_delta = kernel_call(solve_kernel, "solve", f32(5, SRC_DEV), factors, right, *from_others(right))
    return attitude, source_delta


def solution(mesh):
    return jax.shard_map(
        local,
        mesh=mesh,
        in_specs=(
            P(("src", "win", "ccd")),
            P(("src", "win", "ccd")),
            P(("src", "win", "ccd"), None),
            P(("src", "win", "ccd"), None),
            P(("src", "win", "ccd"), None),
            P(("src", "win", "ccd"), None, None),
            P(("src", "win", "ccd"), None, None),
        ),
        out_specs=(P(("src", "win"), None, None), P(None, ("src", "win"))),
        check_vma=False,
    )
```

```python
import math

import jax
import jax.numpy as jnp
import ml_dtypes
import numpy as np
from jax import lax
from jax.experimental import pallas as pl
from jax.experimental.pallas import tpu as pltpu
from jax.sharding import PartitionSpec as P

KNOTS_W = 128
BINS_W = 125
NBLK = 128
ROWS = 128
WINDOWS = 64
CAP = 4
SLOTS = WINDOWS * CAP
SRC_DEV = 4096
ITERS = 8
N_CCD = 4
HIGH = 16
LOW = 256
DOT_BLOCKS = 8

KNOT_PRIOR = 1.0
SOURCE_PRIOR = 1.0
PAIR_LIST = [(first, second) for first in range(5) for second in range(first, 5)]
ATT_PAIRS = [(first, second) for first in range(4) for second in range(first, 4)]
RHS_AT = 70
BIN_AT = 86
FEATS = 88

F32 = jnp.float32
BF16 = jnp.bfloat16
NT = (((1,), (1,)), ((), ()))
NN = (((1,), (0,)), ((), ()))

PIECES = np.array([[1, 0, 0, 0], [4, 12, 6, 1], [1, 6, 12, 4], [0, 0, 0, 1]], np.int64)
SPLINE = PIECES / 6.0


def knot_matrix():
    pair_at = {}
    for at, (first, second) in enumerate(ATT_PAIRS):
        pair_at[first, second] = pair_at[second, first] = at
    table = np.zeros((120, 4 * FEATS), np.float64)
    for d in range(-3, 4):
        for p in range(4):
            for q in range(4):
                row = ((d + 3) * 4 + p) * 4 + q
                for l in range(4):
                    j = l - d
                    if 0 <= j < 4:
                        for m, value in enumerate(np.convolve(PIECES[j], PIECES[l])):
                            table[row, l * FEATS + m * 10 + pair_at[q, p]] += value
    for q in range(4):
        for j in range(4):
            table[112 + q, j * FEATS + RHS_AT + 4 * j + q] = 36.0
            table[116 + q, j * FEATS + RHS_AT + 4 * j + q] = 36.0
    return table.astype(ml_dtypes.bfloat16)


def split_parts(values, count):
    parts = []
    for at in range(count):
        part = values.astype(BF16)
        parts.append(part)
        if at + 1 < count:
            values = values - part.astype(F32)
    return parts


def exact_dot(values, ones, dims, swap=False):
    total = None
    for part in split_parts(values, 3):
        pair = (ones, part) if swap else (part, ones)
        piece = lax.dot_general(*pair, dims, preferred_element_type=F32)
        total = piece if total is None else total + piece
    return total


def indicator(condition):
    return jnp.where(condition, 1.0, 0.0).astype(BF16)


def iota(shape, axis):
    return lax.broadcasted_iota(jnp.int32, shape, axis)


def iota_f(shape, axis):
    return iota(shape, axis).astype(F32)


def normals_kernel(*refs):
    given, (send_ref, obs_ref, slot_ref, marked_ref), here = refs[:6], refs[6:10], refs[10:16]
    pay_ref, done_ref = refs[16:]
    bin_ref, rows_ref, phase_ref, att_ref, resid_ref, source_ref = here
    copies = [pltpu.make_async_copy(given[at], here[at], done_ref.at[at]) for at in range(6)]
    for copy in copies:
        copy.start()
    square = (NBLK, NBLK)
    copies[0].wait()
    bins = bin_ref[...].astype(F32)
    window = jnp.floor((bins + 0.5) * (1.0 / BINS_W))
    local_bin = bins - BINS_W * window
    window_column = jnp.broadcast_to(window, square).T
    earlier = jnp.where(window_column == window, 1.0, 0.0) * jnp.where(iota(square, 0) < iota(square, 1), 1.0, 0.0)
    rank = jnp.sum(earlier, axis=0, keepdims=True)
    slot_ref[...] = jnp.concatenate([window, rank, jnp.zeros((6, NBLK), F32)], axis=0)
    place = indicator(iota_f((SLOTS, NBLK), 0) == CAP * window + rank)
    copies[1].wait()
    mask = iota(square, 0) < rows_ref[...]
    used = jnp.broadcast_to(rows_ref[...].astype(F32), square).T
    for copy in copies[2:]:
        copy.wait()
    marked_ref[...] = jnp.where(iota_f(square, 1) < used, source_ref[...], -LOW)
    u = phase_ref[...].T
    resid = jnp.where(mask, resid_ref[...].T, 0.0)
    att = [jnp.where(mask, att_ref[pl.ds(q, NBLK, stride=4), :].T, 0.0) for q in range(4)]
    obs_ref[0:128, :] = u
    obs_ref[128:256, :] = resid
    for q in range(4):
        obs_ref[256 + 128 * q : 384 + 128 * q, :] = att[q]
    v = 1.0 - u
    u2, v2 = u * u, v * v
    u3, v3 = u2 * u, v2 * v
    cubes = [v3, u * v2, u2 * v, u3]
    powers = [v3 * v3, u * v2 * v3, u2 * v2 * v2, u3 * v3, u2 * u2 * v2, u3 * u2 * v, u3 * u3]
    for at, (first, second) in enumerate(ATT_PAIRS):
        product = att[first] * att[second]
        for m in range(7):
            row = m * 10 + at
            pay_ref[row : row + 1, :] = jnp.sum(powers[m] * product, axis=0, keepdims=True)
    for q in range(4):
        product = att[q] * resid
        sums = [jnp.sum(cubes[i] * product, axis=0, keepdims=True) for i in range(4)]
        for j in range(4):
            total = None
            for i in range(4):
                if SPLINE[j, i] != 0.0:
                    piece = float(SPLINE[j, i]) * sums[i]
                    total = piece if total is None else total + piece
            row = RHS_AT + 4 * j + q
            pay_ref[row : row + 1, :] = total
    pay_ref[BIN_AT : BIN_AT + 1, :] = local_bin
    pay_ref[BIN_AT + 1 :, :] = jnp.zeros((NBLK - BIN_AT - 1, NBLK), F32)
    send_ref[...] = exact_dot(pay_ref[...], place, NT, swap=True)


def bins_kernel(got_ref, after_ref, out_ref):
    del after_ref
    got = got_ref[...].T
    place = indicator(iota_f((KNOTS_W, SLOTS), 0) == got[BIN_AT : BIN_AT + 1, :])
    out_ref[...] = exact_dot(got[:FEATS], place, NT)


def attitude_kernel(
    own_ref, one_ref, two_ref, three_ref, got_ref, table_ref, normal_ref, other_ref, att_ref, reply_ref, pair_ref
):
    pair_ref[...] = normal_ref[...] + other_ref[...]
    total = ((own_ref[...] + two_ref[...]) + (one_ref[...] + three_ref[...])) * (1.0 / 36.0)
    moved = jnp.concatenate([total] + [pltpu.roll(total, l, 1) for l in range(1, 4)], axis=0)
    band = exact_dot(moved, table_ref[...], NN, swap=True)
    groups = [band[8 * at : 8 * at + 8] for at in range(14)]
    lower_half = iota((8, KNOTS_W), 0) < 4

    def doubled(values):
        return values + pltpu.roll(values, 4, 0)

    def norm(values):
        return jnp.sum(jnp.sum(values, axis=1, keepdims=True), axis=0, keepdims=True)

    def apply(vector):
        spread = [
            jnp.where(lower_half, vector[2 * at : 2 * at + 1, :], vector[2 * at + 1 : 2 * at + 2, :]) for at in range(2)
        ]
        pieces = []
        for d in range(-3, 4):
            piece = groups[2 * (d + 3)] * spread[0] + groups[2 * (d + 3) + 1] * spread[1]
            pieces.append(pltpu.roll(piece, -d % KNOTS_W, 1) if d else piece)
        outer = (pieces[0] + pieces[1]) + (pieces[2] + pieces[4])
        return KNOT_PRIOR * vector + doubled(outer + ((pieces[5] + pieces[6]) + pieces[3]))

    residual = band[112:120]
    direction = residual
    estimate = jnp.zeros_like(residual)
    for iteration in range(ITERS):
        applied = apply(direction)
        norm_now = norm(residual * residual)
        inverse = 1.0 / norm(direction * applied)
        across = norm(residual * applied)
        applied_norm = norm(applied * applied)
        step_size = norm_now * inverse
        estimate = estimate + step_size * direction
        residual = residual - step_size * applied
        if iteration + 1 < ITERS:
            ratio = 1.0 - 2.0 * (across * inverse) + step_size * (applied_norm * inverse)
            direction = residual + ratio * direction
    att_ref[0] = estimate[:4]
    moved = jnp.concatenate([estimate[:4]] + [pltpu.roll(estimate, KNOTS_W - j, 1)[:4] for j in range(1, 4)], axis=0)
    column = jnp.concatenate(
        [got_ref[pl.ds(s, WINDOWS, stride=CAP), :][:, BIN_AT : BIN_AT + 1] for s in range(CAP)], axis=0
    )
    place = indicator(iota_f((SLOTS, KNOTS_W), 1) == column)
    knots = exact_dot(moved, place, NT, swap=True)
    reply_ref[...] = jnp.zeros((WINDOWS, 128), F32)
    for s in range(CAP):
        reply_ref[:, 16 * s : 16 * s + 16] = knots[WINDOWS * s : WINDOWS * s + WINDOWS]


def source_sums(count, chunk, terms_ref, high_ref, low_ref, out_ref, acc_ref):
    high_at = iota_f((HIGH, ROWS), 0)
    low_at = iota_f((LOW, ROWS), 0).astype(BF16)
    one, zero = jnp.ones((), BF16), jnp.zeros((), BF16)

    def factors(block):
        here = high_at == high_ref[pl.ds(block, 1), :]
        low = jnp.broadcast_to(low_ref[pl.ds(block, 1), :], (HIGH, ROWS)).astype(BF16)
        low = jnp.concatenate([low] * (LOW // HIGH), axis=0)
        terms = [
            jnp.where(here, terms_ref[pl.ds(c * NBLK + block, 1), :], 0.0).astype(BF16) for c in range(2 * count)
        ]
        return jnp.concatenate(terms, axis=0), jnp.where(low_at == low, one, zero)

    def step(at, carry):
        for first in range(0, chunk, DOT_BLOCKS):
            pairs = [factors(at * chunk + first + inner) for inner in range(DOT_BLOCKS)]
            terms = jnp.concatenate([pair[0] for pair in pairs], axis=1)
            ones = jnp.concatenate([pair[1] for pair in pairs], axis=1)
            acc_ref[...] += lax.dot_general(ones, terms, NT, preferred_element_type=F32)
        return carry

    acc_ref[...] = jnp.zeros(acc_ref.shape, F32)
    lax.fori_loop(0, NBLK // chunk, step, 0)
    sums = acc_ref[...].T
    for c in range(count):
        at = 2 * c * HIGH
        out_ref[HIGH * c : HIGH * c + HIGH, :] = sums[at : at + HIGH] + sums[at + HIGH : at + 2 * HIGH]


def put_terms(terms_ref, c, values):
    large = values.astype(BF16).astype(F32)
    terms_ref[2 * c * NBLK : (2 * c + 1) * NBLK, :] = large
    terms_ref[(2 * c + 1) * NBLK : (2 * c + 2) * NBLK, :] = values - large


def put_sources(marked_ref, high_ref, low_ref):
    source = marked_ref[...]
    high = source >> 8
    high_ref[...] = high.astype(F32)
    low_ref[...] = (source - (high << 8)).astype(F32)


def source_normals_kernel(marked_ref, gain_ref, out_ref, terms_ref, high_ref, low_ref, *work):
    put_sources(marked_ref, high_ref, low_ref)
    gains = [gain_ref[NBLK * p : NBLK * p + NBLK, :] for p in range(5)]
    for at, (first, second) in enumerate(PAIR_LIST):
        put_terms(terms_ref, at, gains[first] * gains[second])
    source_sums(15, 64, terms_ref, high_ref, low_ref, out_ref, *work)


def source_right_kernel(
    reply_ref, slot_ref, obs_ref, marked_ref, gain_ref, after_ref, out_ref, terms_ref, high_ref, low_ref, *work
):
    put_sources(marked_ref, high_ref, low_ref)
    place = indicator(iota_f((WINDOWS, NBLK), 0) == slot_ref[0:1, :])
    rank = slot_ref[1:2, :]
    spread = exact_dot(reply_ref[...].T, place, NN)
    knots = None
    for s in range(CAP):
        piece = jnp.where(rank == float(s), spread[16 * s : 16 * s + 16, :], 0.0)
        knots = piece if knots is None else knots + piece
    u = obs_ref[0:128, :]
    att = [obs_ref[256 + 128 * q : 384 + 128 * q, :] for q in range(4)]
    v = 1.0 - u
    u2, v2 = u * u, v * v
    cubes = [v2 * v, u * v2, u2 * v, u2 * u]
    values = obs_ref[128:256, :]
    for j in range(4):
        spline = None
        for i in range(4):
            if SPLINE[j, i] != 0.0:
                piece = float(SPLINE[j, i]) * cubes[i]
                spline = piece if spline is None else spline + piece
        inner = None
        for q in range(4):
            piece = att[q] * knots[4 * j + q : 4 * j + q + 1, :]
            inner = piece if inner is None else inner + piece
        values = values - spline * inner
    values = values.T
    for p in range(5):
        put_terms(terms_ref, p, gain_ref[NBLK * p : NBLK * p + NBLK, :] * values)
    source_sums(5, NBLK, terms_ref, high_ref, low_ref, out_ref, *work)


def factor_kernel(own_ref, other_ref, after_ref, out_ref):
    del after_ref
    entries = {}
    for at, pair in enumerate(PAIR_LIST):
        rows = slice(HIGH * at, HIGH * at + HIGH)
        total = own_ref[rows, :] + other_ref[rows, :]
        entries[pair] = total + SOURCE_PRIOR if pair[0] == pair[1] else total
    lower = {}
    for column in range(5):
        pivot = entries[column, column]
        for before in range(column):
            pivot = pivot - lower[column, before] * lower[column, before]
        inverse = 1.0 / jnp.sqrt(pivot)
        lower[column, column] = inverse
        for row in range(column + 1, 5):
            running = entries[column, row]
            for before in range(column):
                running = running - lower[row, before] * lower[column, before]
            lower[row, column] = running * inverse
    for at, (first, second) in enumerate(PAIR_LIST):
        out_ref[HIGH * at : HIGH * at + HIGH, :] = lower[second, first]


def solve_kernel(factor_ref, own_ref, one_ref, two_ref, three_ref, out_ref):
    lower = {}
    for at, (first, second) in enumerate(PAIR_LIST):
        lower[second, first] = factor_ref[HIGH * at : HIGH * at + HIGH, :]
    values = []
    for row in range(5):
        rows = slice(HIGH * row, HIGH * row + HIGH)
        running = (own_ref[rows, :] + two_ref[rows, :]) + (one_ref[rows, :] + three_ref[rows, :])
        for before in range(row):
            running = running - lower[row, before] * values[before]
        values.append(running * lower[row, row])
    for row in reversed(range(5)):
        running = values[row]
        for later in range(row + 1, 5):
            running = running - lower[later, row] * values[later]
        values[row] = running * lower[row, row]
    for row in range(5):
        for high in range(HIGH):
            out_ref[row : row + 1, LOW * high : LOW * high + LOW] = values[row][high : high + 1, :]


def f32(*shape):
    return jax.ShapeDtypeStruct(shape, F32)


def kernel_call(body, name, outs, *args, scratch=(), flops=1_000_000, far=(), grant=32, passed=None):
    passed = passed or {}
    place = [pl.ANY if at in far else pltpu.MemorySpace.VMEM for at in range(len(args))]
    out_place = [pl.ANY if at in passed.values() else pltpu.MemorySpace.VMEM for at in range(len(jax.tree.leaves(outs)))]
    out_specs = [pl.BlockSpec(memory_space=at) for at in out_place]
    size = sum(math.prod(a.shape) * 4 for a in args)
    return pl.pallas_call(
        body,
        out_shape=outs,
        in_specs=[pl.BlockSpec(memory_space=at) for at in place],
        out_specs=tuple(out_specs) if isinstance(outs, tuple) else out_specs[0],
        input_output_aliases=passed,
        scratch_shapes=list(scratch),
        compiler_params=pltpu.CompilerParams(vmem_limit_bytes=grant * 1024 * 1024),
        cost_estimate=pl.CostEstimate(flops=flops, bytes_accessed=size, transcendentals=0),
        name=name,
    )(*args)


def segment_scratch(count):
    return (
        pltpu.VMEM((2 * count * NBLK, ROWS), F32),
        pltpu.VMEM((NBLK, ROWS), F32),
        pltpu.VMEM((NBLK, ROWS), F32),
        pltpu.VMEM((LOW, 2 * count * HIGH), F32),
    )


def swapped(values, partner):
    return lax.ppermute(values, "ccd", list(enumerate(partner)))


def from_others(values):
    return [
        lax.ppermute(values, "ccd", [(at, (at + shift) % N_CCD) for at in range(N_CCD)]) for shift in range(1, N_CCD)
    ]


def to_windows(values):
    return lax.all_to_all(values, ("src", "win"), split_axis=0, concat_axis=0, tiled=True)


def local(block_bin, block_rows, row_source, obs_resid, obs_phase, att_partial, src_partial):
    bins = block_bin.reshape(1, NBLK)
    rows = block_rows.reshape(1, NBLK)
    gains = jnp.transpose(src_partial, (1, 0, 2)).reshape(5 * NBLK, ROWS)
    send, obs, slots, marked = kernel_call(
        normals_kernel,
        "normals",
        (f32(SLOTS, 128), f32(6 * ROWS, NBLK), f32(8, NBLK), jax.ShapeDtypeStruct((NBLK, ROWS), jnp.int32)),
        bins,
        rows,
        obs_phase,
        att_partial.reshape(4 * NBLK, ROWS),
        obs_resid,
        row_source,
        scratch=(
            pltpu.VMEM((1, NBLK), jnp.int32),
            pltpu.VMEM((1, NBLK), jnp.int32),
            pltpu.VMEM((NBLK, ROWS), F32),
            pltpu.VMEM((4 * NBLK, ROWS), F32),
            pltpu.VMEM((NBLK, ROWS), F32),
            pltpu.VMEM((NBLK, ROWS), jnp.int32),
            pltpu.VMEM((NBLK, NBLK), F32),
            pltpu.SemaphoreType.DMA((6,)),
        ),
        far=range(6),
        grant=56,
    )
    got = to_windows(send.reshape(WINDOWS, CAP, 128)).reshape(SLOTS, 128)
    normal = kernel_call(
        source_normals_kernel,
        "source_normals",
        f32(15 * HIGH, LOW),
        marked,
        gains,
        scratch=segment_scratch(15),
        flops=2 * 480 * 256 * 16384,
    )
    moments = kernel_call(bins_kernel, "bins", f32(FEATS, KNOTS_W), got, normal, far=(1,))
    attitude, reply, normal = kernel_call(
        attitude_kernel,
        "attitude",
        (f32(1, 4, KNOTS_W), f32(WINDOWS, 128), f32(15 * HIGH, LOW)),
        moments,
        *from_others(moments),
        got,
        jnp.asarray(knot_matrix()),
        normal,
        swapped(normal, (1, 0, 3, 2)),
    )
    other = swapped(normal, (3, 2, 1, 0))
    knots = to_windows(reply)
    right = kernel_call(
        source_right_kernel,
        "source_right",
        f32(5 * HIGH, LOW),
        knots,
        slots,
        obs,
        marked,
        gains,
        other,
        far=(5,),
        scratch=segment_scratch(5),
        flops=2 * 160 * 256 * 16384,
    )
    factors = kernel_call(factor_kernel, "factors", f32(15 * HIGH, LOW), normal, other, right, far=(2,))
    source_delta = kernel_call(solve_kernel, "solve", f32(5, SRC_DEV), factors, right, *from_others(right))
    return attitude, source_delta


def solution(mesh):
    return jax.shard_map(
        local,
        mesh=mesh,
        in_specs=(
            P(("src", "win", "ccd")),
            P(("src", "win", "ccd")),
            P(("src", "win", "ccd"), None),
            P(("src", "win", "ccd"), None),
            P(("src", "win", "ccd"), None),
            P(("src", "win", "ccd"), None, None),
            P(("src", "win", "ccd"), None, None),
        ),
        out_specs=(P(("src", "win"), None, None), P(None, ("src", "win"))),
        check_vma=False,
    )
```

```python
import math

import jax
import jax.numpy as jnp
import ml_dtypes
import numpy as np
from jax import lax
from jax.experimental import pallas as pl
from jax.experimental.pallas import tpu as pltpu
from jax.sharding import PartitionSpec as P

KNOTS_W = 128
BINS_W = 125
NBLK = 128
ROWS = 128
WINDOWS = 64
CAP = 4
SLOTS = WINDOWS * CAP
SRC_DEV = 4096
ITERS = 8
N_CCD = 4
HIGH = 16
LOW = 256
DOT_BLOCKS = 8

KNOT_PRIOR = 1.0
SOURCE_PRIOR = 1.0
PAIR_LIST = [(first, second) for first in range(5) for second in range(first, 5)]
ATT_PAIRS = [(first, second) for first in range(4) for second in range(first, 4)]
RHS_AT = 70
BIN_AT = 86
FEATS = 88

F32 = jnp.float32
BF16 = jnp.bfloat16
NT = (((1,), (1,)), ((), ()))
NN = (((1,), (0,)), ((), ()))

PIECES = np.array([[1, 0, 0, 0], [4, 12, 6, 1], [1, 6, 12, 4], [0, 0, 0, 1]], np.int64)
SPLINE = PIECES / 6.0


def knot_matrix():
    pair_at = {}
    for at, (first, second) in enumerate(ATT_PAIRS):
        pair_at[first, second] = pair_at[second, first] = at
    table = np.zeros((120, 4 * FEATS), np.float64)
    for d in range(-3, 4):
        for p in range(4):
            for q in range(4):
                row = ((d + 3) * 4 + p) * 4 + q
                for l in range(4):
                    j = l - d
                    if 0 <= j < 4:
                        for m, value in enumerate(np.convolve(PIECES[j], PIECES[l])):
                            table[row, l * FEATS + m * 10 + pair_at[q, p]] += value
    for q in range(4):
        for j in range(4):
            table[112 + q, j * FEATS + RHS_AT + 4 * j + q] = 36.0
            table[116 + q, j * FEATS + RHS_AT + 4 * j + q] = 36.0
    return table.astype(ml_dtypes.bfloat16)


def split_parts(values, count):
    parts = []
    for at in range(count):
        part = values.astype(BF16)
        parts.append(part)
        if at + 1 < count:
            values = values - part.astype(F32)
    return parts


def exact_dot(values, ones, dims, swap=False):
    total = None
    for part in split_parts(values, 3):
        pair = (ones, part) if swap else (part, ones)
        piece = lax.dot_general(*pair, dims, preferred_element_type=F32)
        total = piece if total is None else total + piece
    return total


def indicator(condition):
    return jnp.where(condition, 1.0, 0.0).astype(BF16)


def iota(shape, axis):
    return lax.broadcasted_iota(jnp.int32, shape, axis)


def iota_f(shape, axis):
    return iota(shape, axis).astype(F32)


def normals_kernel(*refs):
    given, (send_ref, obs_ref, slot_ref, marked_ref), here = refs[:6], refs[6:10], refs[10:16]
    pay_ref, done_ref = refs[16:]
    bin_ref, rows_ref, phase_ref, att_ref, resid_ref, source_ref = here
    copies = [pltpu.make_async_copy(given[at], here[at], done_ref.at[at]) for at in range(6)]
    for copy in copies:
        copy.start()
    square = (NBLK, NBLK)
    copies[0].wait()
    bins = bin_ref[...].astype(F32)
    window = jnp.floor((bins + 0.5) * (1.0 / BINS_W))
    local_bin = bins - BINS_W * window
    window_column = jnp.broadcast_to(window, square).T
    earlier = jnp.where(window_column == window, 1.0, 0.0) * jnp.where(iota(square, 0) < iota(square, 1), 1.0, 0.0)
    rank = jnp.sum(earlier, axis=0, keepdims=True)
    slot_ref[...] = jnp.concatenate([window, rank, jnp.zeros((6, NBLK), F32)], axis=0)
    place = indicator(iota_f((SLOTS, NBLK), 0) == CAP * window + rank)
    copies[1].wait()
    mask = iota(square, 0) < rows_ref[...]
    used = jnp.broadcast_to(rows_ref[...].astype(F32), square).T
    for copy in copies[2:]:
        copy.wait()
    marked_ref[...] = jnp.where(iota_f(square, 1) < used, source_ref[...], -LOW)
    u = phase_ref[...].T
    resid = jnp.where(mask, resid_ref[...].T, 0.0)
    att = [jnp.where(mask, att_ref[pl.ds(q, NBLK, stride=4), :].T, 0.0) for q in range(4)]
    obs_ref[0:128, :] = u
    obs_ref[128:256, :] = resid
    for q in range(4):
        obs_ref[256 + 128 * q : 384 + 128 * q, :] = att[q]
    v = 1.0 - u
    u2, v2 = u * u, v * v
    u3, v3 = u2 * u, v2 * v
    cubes = [v3, u * v2, u2 * v, u3]
    powers = [v3 * v3, u * v2 * v3, u2 * v2 * v2, u3 * v3, u2 * u2 * v2, u3 * u2 * v, u3 * u3]
    for at, (first, second) in enumerate(ATT_PAIRS):
        product = att[first] * att[second]
        for m in range(7):
            row = m * 10 + at
            pay_ref[row : row + 1, :] = jnp.sum(powers[m] * product, axis=0, keepdims=True)
    for q in range(4):
        product = att[q] * resid
        sums = [jnp.sum(cubes[i] * product, axis=0, keepdims=True) for i in range(4)]
        for j in range(4):
            total = None
            for i in range(4):
                if SPLINE[j, i] != 0.0:
                    piece = float(SPLINE[j, i]) * sums[i]
                    total = piece if total is None else total + piece
            row = RHS_AT + 4 * j + q
            pay_ref[row : row + 1, :] = total
    pay_ref[BIN_AT : BIN_AT + 1, :] = local_bin
    pay_ref[BIN_AT + 1 :, :] = jnp.zeros((NBLK - BIN_AT - 1, NBLK), F32)
    send_ref[...] = exact_dot(pay_ref[...], place, NT, swap=True)


def bins_kernel(got_ref, after_ref, out_ref):
    del after_ref
    got = got_ref[...].T
    place = indicator(iota_f((KNOTS_W, SLOTS), 0) == got[BIN_AT : BIN_AT + 1, :])
    out_ref[...] = exact_dot(got[:FEATS], place, NT)


def attitude_kernel(
    own_ref, one_ref, two_ref, three_ref, got_ref, table_ref, normal_ref, other_ref, att_ref, reply_ref, pair_ref
):
    pair_ref[...] = normal_ref[...] + other_ref[...]
    total = ((own_ref[...] + two_ref[...]) + (one_ref[...] + three_ref[...])) * (1.0 / 36.0)
    moved = jnp.concatenate([total] + [pltpu.roll(total, l, 1) for l in range(1, 4)], axis=0)
    band = exact_dot(moved, table_ref[...], NN, swap=True)
    groups = [band[8 * at : 8 * at + 8] for at in range(14)]
    lower_half = iota((8, KNOTS_W), 0) < 4

    def doubled(values):
        return values + pltpu.roll(values, 4, 0)

    def norm(values):
        return jnp.sum(jnp.sum(values, axis=1, keepdims=True), axis=0, keepdims=True)

    def apply(vector):
        spread = [
            jnp.where(lower_half, vector[2 * at : 2 * at + 1, :], vector[2 * at + 1 : 2 * at + 2, :]) for at in range(2)
        ]
        pieces = []
        for d in range(-3, 4):
            piece = groups[2 * (d + 3)] * spread[0] + groups[2 * (d + 3) + 1] * spread[1]
            pieces.append(pltpu.roll(piece, -d % KNOTS_W, 1) if d else piece)
        outer = (pieces[0] + pieces[1]) + (pieces[2] + pieces[4])
        return KNOT_PRIOR * vector + doubled(outer + ((pieces[5] + pieces[6]) + pieces[3]))

    residual = band[112:120]
    direction = residual
    estimate = jnp.zeros_like(residual)
    for iteration in range(ITERS):
        applied = apply(direction)
        norm_now = norm(residual * residual)
        inverse = 1.0 / norm(direction * applied)
        across = norm(residual * applied)
        applied_norm = norm(applied * applied)
        step_size = norm_now * inverse
        estimate = estimate + step_size * direction
        residual = residual - step_size * applied
        if iteration + 1 < ITERS:
            ratio = 1.0 - 2.0 * (across * inverse) + step_size * (applied_norm * inverse)
            direction = residual + ratio * direction
    att_ref[0] = estimate[:4]
    moved = jnp.concatenate([estimate[:4]] + [pltpu.roll(estimate, KNOTS_W - j, 1)[:4] for j in range(1, 4)], axis=0)
    column = jnp.concatenate(
        [got_ref[pl.ds(s, WINDOWS, stride=CAP), :][:, BIN_AT : BIN_AT + 1] for s in range(CAP)], axis=0
    )
    place = indicator(iota_f((SLOTS, KNOTS_W), 1) == column)
    knots = exact_dot(moved, place, NT, swap=True)
    reply_ref[...] = jnp.zeros((WINDOWS, 128), F32)
    for s in range(CAP):
        reply_ref[:, 16 * s : 16 * s + 16] = knots[WINDOWS * s : WINDOWS * s + WINDOWS]


def source_sums(count, chunk, terms_ref, high_ref, low_ref, out_ref, acc_ref):
    high_at = iota_f((HIGH, ROWS), 0)
    low_at = iota_f((LOW, ROWS), 0).astype(BF16)
    one, zero = jnp.ones((), BF16), jnp.zeros((), BF16)

    def factors(block):
        here = high_at == high_ref[pl.ds(block, 1), :]
        low = jnp.broadcast_to(low_ref[pl.ds(block, 1), :], (HIGH, ROWS)).astype(BF16)
        low = jnp.concatenate([low] * (LOW // HIGH), axis=0)
        terms = [
            jnp.where(here, terms_ref[pl.ds(c * NBLK + block, 1), :], 0.0).astype(BF16) for c in range(2 * count)
        ]
        return jnp.concatenate(terms, axis=0), jnp.where(low_at == low, one, zero)

    def step(at, carry):
        for first in range(0, chunk, DOT_BLOCKS):
            pairs = [factors(at * chunk + first + inner) for inner in range(DOT_BLOCKS)]
            terms = jnp.concatenate([pair[0] for pair in pairs], axis=1)
            ones = jnp.concatenate([pair[1] for pair in pairs], axis=1)
            acc_ref[...] += lax.dot_general(ones, terms, NT, preferred_element_type=F32)
        return carry

    acc_ref[...] = jnp.zeros(acc_ref.shape, F32)
    lax.fori_loop(0, NBLK // chunk, step, 0)
    sums = acc_ref[...].T
    for c in range(count):
        at = 2 * c * HIGH
        out_ref[HIGH * c : HIGH * c + HIGH, :] = sums[at : at + HIGH] + sums[at + HIGH : at + 2 * HIGH]


def put_terms(terms_ref, c, values):
    large = values.astype(BF16).astype(F32)
    terms_ref[2 * c * NBLK : (2 * c + 1) * NBLK, :] = large
    terms_ref[(2 * c + 1) * NBLK : (2 * c + 2) * NBLK, :] = values - large


def put_sources(marked_ref, high_ref, low_ref):
    source = marked_ref[...]
    high = source >> 8
    high_ref[...] = high.astype(F32)
    low_ref[...] = (source - (high << 8)).astype(F32)


def source_normals_kernel(marked_ref, gain_ref, out_ref, terms_ref, high_ref, low_ref, *work):
    put_sources(marked_ref, high_ref, low_ref)
    gains = [gain_ref[NBLK * p : NBLK * p + NBLK, :] for p in range(5)]
    for at, (first, second) in enumerate(PAIR_LIST):
        put_terms(terms_ref, at, gains[first] * gains[second])
    source_sums(15, 64, terms_ref, high_ref, low_ref, out_ref, *work)


def source_right_kernel(
    reply_ref, slot_ref, obs_ref, marked_ref, gain_ref, out_ref, terms_ref, high_ref, low_ref, *work
):
    put_sources(marked_ref, high_ref, low_ref)
    place = indicator(iota_f((WINDOWS, NBLK), 0) == slot_ref[0:1, :])
    rank = slot_ref[1:2, :]
    spread = exact_dot(reply_ref[...].T, place, NN)
    knots = None
    for s in range(CAP):
        piece = jnp.where(rank == float(s), spread[16 * s : 16 * s + 16, :], 0.0)
        knots = piece if knots is None else knots + piece
    u = obs_ref[0:128, :]
    att = [obs_ref[256 + 128 * q : 384 + 128 * q, :] for q in range(4)]
    v = 1.0 - u
    u2, v2 = u * u, v * v
    cubes = [v2 * v, u * v2, u2 * v, u2 * u]
    values = obs_ref[128:256, :]
    for j in range(4):
        spline = None
        for i in range(4):
            if SPLINE[j, i] != 0.0:
                piece = float(SPLINE[j, i]) * cubes[i]
                spline = piece if spline is None else spline + piece
        inner = None
        for q in range(4):
            piece = att[q] * knots[4 * j + q : 4 * j + q + 1, :]
            inner = piece if inner is None else inner + piece
        values = values - spline * inner
    values = values.T
    for p in range(5):
        put_terms(terms_ref, p, gain_ref[NBLK * p : NBLK * p + NBLK, :] * values)
    source_sums(5, NBLK, terms_ref, high_ref, low_ref, out_ref, *work)


def factor_kernel(own_ref, other_ref, after_ref, out_ref):
    del after_ref
    entries = {}
    for at, pair in enumerate(PAIR_LIST):
        rows = slice(HIGH * at, HIGH * at + HIGH)
        total = own_ref[rows, :] + other_ref[rows, :]
        entries[pair] = total + SOURCE_PRIOR if pair[0] == pair[1] else total
    lower = {}
    for column in range(5):
        pivot = entries[column, column]
        for before in range(column):
            pivot = pivot - lower[column, before] * lower[column, before]
        inverse = 1.0 / jnp.sqrt(pivot)
        lower[column, column] = inverse
        for row in range(column + 1, 5):
            running = entries[column, row]
            for before in range(column):
                running = running - lower[row, before] * lower[column, before]
            lower[row, column] = running * inverse
    for at, (first, second) in enumerate(PAIR_LIST):
        out_ref[HIGH * at : HIGH * at + HIGH, :] = lower[second, first]


def solve_kernel(factor_ref, own_ref, one_ref, two_ref, three_ref, out_ref):
    lower = {}
    for at, (first, second) in enumerate(PAIR_LIST):
        lower[second, first] = factor_ref[HIGH * at : HIGH * at + HIGH, :]
    values = []
    for row in range(5):
        rows = slice(HIGH * row, HIGH * row + HIGH)
        running = (own_ref[rows, :] + two_ref[rows, :]) + (one_ref[rows, :] + three_ref[rows, :])
        for before in range(row):
            running = running - lower[row, before] * values[before]
        values.append(running * lower[row, row])
    for row in reversed(range(5)):
        running = values[row]
        for later in range(row + 1, 5):
            running = running - lower[later, row] * values[later]
        values[row] = running * lower[row, row]
    for row in range(5):
        for high in range(HIGH):
            out_ref[row : row + 1, LOW * high : LOW * high + LOW] = values[row][high : high + 1, :]


def f32(*shape):
    return jax.ShapeDtypeStruct(shape, F32)


def kernel_call(body, name, outs, *args, scratch=(), flops=1_000_000, far=(), grant=32, passed=None):
    passed = passed or {}
    place = [pl.ANY if at in far else pltpu.MemorySpace.VMEM for at in range(len(args))]
    out_place = [pl.ANY if at in passed.values() else pltpu.MemorySpace.VMEM for at in range(len(jax.tree.leaves(outs)))]
    out_specs = [pl.BlockSpec(memory_space=at) for at in out_place]
    size = sum(math.prod(a.shape) * 4 for a in args)
    return pl.pallas_call(
        body,
        out_shape=outs,
        in_specs=[pl.BlockSpec(memory_space=at) for at in place],
        out_specs=tuple(out_specs) if isinstance(outs, tuple) else out_specs[0],
        input_output_aliases=passed,
        scratch_shapes=list(scratch),
        compiler_params=pltpu.CompilerParams(vmem_limit_bytes=grant * 1024 * 1024),
        cost_estimate=pl.CostEstimate(flops=flops, bytes_accessed=size, transcendentals=0),
        name=name,
    )(*args)


def segment_scratch(count):
    return (
        pltpu.VMEM((2 * count * NBLK, ROWS), F32),
        pltpu.VMEM((NBLK, ROWS), F32),
        pltpu.VMEM((NBLK, ROWS), F32),
        pltpu.VMEM((LOW, 2 * count * HIGH), F32),
    )


def swapped(values, partner):
    return lax.ppermute(values, "ccd", list(enumerate(partner)))


def from_others(values):
    return [
        lax.ppermute(values, "ccd", [(at, (at + shift) % N_CCD) for at in range(N_CCD)]) for shift in range(1, N_CCD)
    ]


def to_windows(values):
    return lax.all_to_all(values, ("src", "win"), split_axis=0, concat_axis=0, tiled=True)


def local(block_bin, block_rows, row_source, obs_resid, obs_phase, att_partial, src_partial):
    bins = block_bin.reshape(1, NBLK)
    rows = block_rows.reshape(1, NBLK)
    gains = jnp.transpose(src_partial, (1, 0, 2)).reshape(5 * NBLK, ROWS)
    send, obs, slots, marked = kernel_call(
        normals_kernel,
        "normals",
        (f32(SLOTS, 128), f32(6 * ROWS, NBLK), f32(8, NBLK), jax.ShapeDtypeStruct((NBLK, ROWS), jnp.int32)),
        bins,
        rows,
        obs_phase,
        att_partial.reshape(4 * NBLK, ROWS),
        obs_resid,
        row_source,
        scratch=(
            pltpu.VMEM((1, NBLK), jnp.int32),
            pltpu.VMEM((1, NBLK), jnp.int32),
            pltpu.VMEM((NBLK, ROWS), F32),
            pltpu.VMEM((4 * NBLK, ROWS), F32),
            pltpu.VMEM((NBLK, ROWS), F32),
            pltpu.VMEM((NBLK, ROWS), jnp.int32),
            pltpu.VMEM((NBLK, NBLK), F32),
            pltpu.SemaphoreType.DMA((6,)),
        ),
        far=range(6),
        grant=56,
    )
    got = to_windows(send.reshape(WINDOWS, CAP, 128)).reshape(SLOTS, 128)
    normal = kernel_call(
        source_normals_kernel,
        "source_normals",
        f32(15 * HIGH, LOW),
        marked,
        gains,
        scratch=segment_scratch(15),
        flops=2 * 480 * 256 * 16384,
    )
    moments = kernel_call(bins_kernel, "bins", f32(FEATS, KNOTS_W), got, normal, far=(1,))
    attitude, reply, normal = kernel_call(
        attitude_kernel,
        "attitude",
        (f32(1, 4, KNOTS_W), f32(WINDOWS, 128), f32(15 * HIGH, LOW)),
        moments,
        *from_others(moments),
        got,
        jnp.asarray(knot_matrix()),
        normal,
        swapped(normal, (1, 0, 3, 2)),
    )
    other = swapped(normal, (3, 2, 1, 0))
    knots = to_windows(reply)
    right = kernel_call(
        source_right_kernel,
        "source_right",
        f32(5 * HIGH, LOW),
        knots,
        slots,
        obs,
        marked,
        gains,
        scratch=segment_scratch(5),
        flops=2 * 160 * 256 * 16384,
    )
    factors = kernel_call(factor_kernel, "factors", f32(15 * HIGH, LOW), normal, other, right, far=(2,))
    source_delta = kernel_call(solve_kernel, "solve", f32(5, SRC_DEV), factors, right, *from_others(right))
    return attitude, source_delta


def solution(mesh):
    return jax.shard_map(
        local,
        mesh=mesh,
        in_specs=(
            P(("src", "win", "ccd")),
            P(("src", "win", "ccd")),
            P(("src", "win", "ccd"), None),
            P(("src", "win", "ccd"), None),
            P(("src", "win", "ccd"), None),
            P(("src", "win", "ccd"), None, None),
            P(("src", "win", "ccd"), None, None),
        ),
        out_specs=(P(("src", "win"), None, None), P(None, ("src", "win"))),
        check_vma=False,
    )
```

```python
import math

import jax
import jax.numpy as jnp
import ml_dtypes
import numpy as np
from jax import lax
from jax.experimental import pallas as pl
from jax.experimental.pallas import tpu as pltpu
from jax.sharding import PartitionSpec as P

KNOTS_W = 128
BINS_W = 125
NBLK = 128
ROWS = 128
WINDOWS = 64
CAP = 4
SLOTS = WINDOWS * CAP
SRC_DEV = 4096
ITERS = 8
N_CCD = 4
HIGH = 16
LOW = 256
DOT_BLOCKS = 16

KNOT_PRIOR = 1.0
SOURCE_PRIOR = 1.0
PAIR_LIST = [(first, second) for first in range(5) for second in range(first, 5)]
ATT_PAIRS = [(first, second) for first in range(4) for second in range(first, 4)]
RHS_AT = 70
BIN_AT = 86
FEATS = 88

F32 = jnp.float32
BF16 = jnp.bfloat16
NT = (((1,), (1,)), ((), ()))
NN = (((1,), (0,)), ((), ()))

PIECES = np.array([[1, 0, 0, 0], [4, 12, 6, 1], [1, 6, 12, 4], [0, 0, 0, 1]], np.int64)
SPLINE = PIECES / 6.0


def knot_matrix():
    pair_at = {}
    for at, (first, second) in enumerate(ATT_PAIRS):
        pair_at[first, second] = pair_at[second, first] = at
    table = np.zeros((120, 4 * FEATS), np.float64)
    for d in range(-3, 4):
        for p in range(4):
            for q in range(4):
                row = ((d + 3) * 4 + p) * 4 + q
                for l in range(4):
                    j = l - d
                    if 0 <= j < 4:
                        for m, value in enumerate(np.convolve(PIECES[j], PIECES[l])):
                            table[row, l * FEATS + m * 10 + pair_at[q, p]] += value
    for q in range(4):
        for j in range(4):
            table[112 + q, j * FEATS + RHS_AT + 4 * j + q] = 36.0
            table[116 + q, j * FEATS + RHS_AT + 4 * j + q] = 36.0
    return table.astype(ml_dtypes.bfloat16)


def split_parts(values, count):
    parts = []
    for at in range(count):
        part = values.astype(BF16)
        parts.append(part)
        if at + 1 < count:
            values = values - part.astype(F32)
    return parts


def exact_dot(values, ones, dims, swap=False):
    total = None
    for part in split_parts(values, 3):
        pair = (ones, part) if swap else (part, ones)
        piece = lax.dot_general(*pair, dims, preferred_element_type=F32)
        total = piece if total is None else total + piece
    return total


def indicator(condition):
    return jnp.where(condition, 1.0, 0.0).astype(BF16)


def iota(shape, axis):
    return lax.broadcasted_iota(jnp.int32, shape, axis)


def iota_f(shape, axis):
    return iota(shape, axis).astype(F32)


def normals_kernel(*refs):
    given, (send_ref, obs_ref, slot_ref, marked_ref), here = refs[:6], refs[6:10], refs[10:16]
    pay_ref, done_ref = refs[16:]
    bin_ref, rows_ref, phase_ref, att_ref, resid_ref, source_ref = here
    copies = [pltpu.make_async_copy(given[at], here[at], done_ref.at[at]) for at in range(6)]
    for copy in copies:
        copy.start()
    square = (NBLK, NBLK)
    copies[0].wait()
    bins = bin_ref[...].astype(F32)
    window = jnp.floor((bins + 0.5) * (1.0 / BINS_W))
    local_bin = bins - BINS_W * window
    window_column = jnp.broadcast_to(window, square).T
    earlier = jnp.where(window_column == window, 1.0, 0.0) * jnp.where(iota(square, 0) < iota(square, 1), 1.0, 0.0)
    rank = jnp.sum(earlier, axis=0, keepdims=True)
    slot_ref[...] = jnp.concatenate([window, rank, jnp.zeros((6, NBLK), F32)], axis=0)
    place = indicator(iota_f((SLOTS, NBLK), 0) == CAP * window + rank)
    copies[1].wait()
    mask = iota(square, 0) < rows_ref[...]
    used = jnp.broadcast_to(rows_ref[...].astype(F32), square).T
    for copy in copies[2:]:
        copy.wait()
    marked_ref[...] = jnp.where(iota_f(square, 1) < used, source_ref[...], -LOW)
    u = phase_ref[...].T
    resid = jnp.where(mask, resid_ref[...].T, 0.0)
    att = [jnp.where(mask, att_ref[pl.ds(q, NBLK, stride=4), :].T, 0.0) for q in range(4)]
    obs_ref[0:128, :] = u
    obs_ref[128:256, :] = resid
    for q in range(4):
        obs_ref[256 + 128 * q : 384 + 128 * q, :] = att[q]
    v = 1.0 - u
    u2, v2 = u * u, v * v
    u3, v3 = u2 * u, v2 * v
    cubes = [v3, u * v2, u2 * v, u3]
    powers = [v3 * v3, u * v2 * v3, u2 * v2 * v2, u3 * v3, u2 * u2 * v2, u3 * u2 * v, u3 * u3]
    for at, (first, second) in enumerate(ATT_PAIRS):
        product = att[first] * att[second]
        for m in range(7):
            row = m * 10 + at
            pay_ref[row : row + 1, :] = jnp.sum(powers[m] * product, axis=0, keepdims=True)
    for q in range(4):
        product = att[q] * resid
        sums = [jnp.sum(cubes[i] * product, axis=0, keepdims=True) for i in range(4)]
        for j in range(4):
            total = None
            for i in range(4):
                if SPLINE[j, i] != 0.0:
                    piece = float(SPLINE[j, i]) * sums[i]
                    total = piece if total is None else total + piece
            row = RHS_AT + 4 * j + q
            pay_ref[row : row + 1, :] = total
    pay_ref[BIN_AT : BIN_AT + 1, :] = local_bin
    pay_ref[BIN_AT + 1 :, :] = jnp.zeros((NBLK - BIN_AT - 1, NBLK), F32)
    send_ref[...] = exact_dot(pay_ref[...], place, NT, swap=True)


def bins_kernel(got_ref, after_ref, out_ref):
    del after_ref
    got = got_ref[...].T
    place = indicator(iota_f((KNOTS_W, SLOTS), 0) == got[BIN_AT : BIN_AT + 1, :])
    out_ref[...] = exact_dot(got[:FEATS], place, NT)


def attitude_kernel(
    own_ref, one_ref, two_ref, three_ref, got_ref, table_ref, normal_ref, other_ref, att_ref, reply_ref, pair_ref
):
    pair_ref[...] = normal_ref[...] + other_ref[...]
    total = ((own_ref[...] + two_ref[...]) + (one_ref[...] + three_ref[...])) * (1.0 / 36.0)
    moved = jnp.concatenate([total] + [pltpu.roll(total, l, 1) for l in range(1, 4)], axis=0)
    band = exact_dot(moved, table_ref[...], NN, swap=True)
    groups = [band[8 * at : 8 * at + 8] for at in range(14)]
    lower_half = iota((8, KNOTS_W), 0) < 4

    def doubled(values):
        return values + pltpu.roll(values, 4, 0)

    def norm(values):
        return jnp.sum(jnp.sum(values, axis=1, keepdims=True), axis=0, keepdims=True)

    def apply(vector):
        spread = [
            jnp.where(lower_half, vector[2 * at : 2 * at + 1, :], vector[2 * at + 1 : 2 * at + 2, :]) for at in range(2)
        ]
        pieces = []
        for d in range(-3, 4):
            piece = groups[2 * (d + 3)] * spread[0] + groups[2 * (d + 3) + 1] * spread[1]
            pieces.append(pltpu.roll(piece, -d % KNOTS_W, 1) if d else piece)
        outer = (pieces[0] + pieces[1]) + (pieces[2] + pieces[4])
        return KNOT_PRIOR * vector + doubled(outer + ((pieces[5] + pieces[6]) + pieces[3]))

    residual = band[112:120]
    direction = residual
    estimate = jnp.zeros_like(residual)
    for iteration in range(ITERS):
        applied = apply(direction)
        norm_now = norm(residual * residual)
        inverse = 1.0 / norm(direction * applied)
        across = norm(residual * applied)
        applied_norm = norm(applied * applied)
        step_size = norm_now * inverse
        estimate = estimate + step_size * direction
        residual = residual - step_size * applied
        if iteration + 1 < ITERS:
            ratio = 1.0 - 2.0 * (across * inverse) + step_size * (applied_norm * inverse)
            direction = residual + ratio * direction
    att_ref[0] = estimate[:4]
    moved = jnp.concatenate([estimate[:4]] + [pltpu.roll(estimate, KNOTS_W - j, 1)[:4] for j in range(1, 4)], axis=0)
    column = jnp.concatenate(
        [got_ref[pl.ds(s, WINDOWS, stride=CAP), :][:, BIN_AT : BIN_AT + 1] for s in range(CAP)], axis=0
    )
    place = indicator(iota_f((SLOTS, KNOTS_W), 1) == column)
    knots = exact_dot(moved, place, NT, swap=True)
    reply_ref[...] = jnp.zeros((WINDOWS, 128), F32)
    for s in range(CAP):
        reply_ref[:, 16 * s : 16 * s + 16] = knots[WINDOWS * s : WINDOWS * s + WINDOWS]


def source_sums(count, chunk, terms_ref, high_ref, low_ref, out_ref, acc_ref):
    high_at = iota_f((HIGH, ROWS), 0)
    low_at = iota_f((LOW, ROWS), 0).astype(BF16)
    one, zero = jnp.ones((), BF16), jnp.zeros((), BF16)

    def factors(block):
        here = high_at == high_ref[pl.ds(block, 1), :]
        low = jnp.broadcast_to(low_ref[pl.ds(block, 1), :], (HIGH, ROWS)).astype(BF16)
        low = jnp.concatenate([low] * (LOW // HIGH), axis=0)
        terms = [
            jnp.where(here, terms_ref[pl.ds(c * NBLK + block, 1), :], 0.0).astype(BF16) for c in range(2 * count)
        ]
        return jnp.concatenate(terms, axis=0), jnp.where(low_at == low, one, zero)

    def step(at, carry):
        for first in range(0, chunk, DOT_BLOCKS):
            pairs = [factors(at * chunk + first + inner) for inner in range(DOT_BLOCKS)]
            terms = jnp.concatenate([pair[0] for pair in pairs], axis=1)
            ones = jnp.concatenate([pair[1] for pair in pairs], axis=1)
            acc_ref[...] += lax.dot_general(ones, terms, NT, preferred_element_type=F32)
        return carry

    acc_ref[...] = jnp.zeros(acc_ref.shape, F32)
    lax.fori_loop(0, NBLK // chunk, step, 0)
    sums = acc_ref[...].T
    for c in range(count):
        at = 2 * c * HIGH
        out_ref[HIGH * c : HIGH * c + HIGH, :] = sums[at : at + HIGH] + sums[at + HIGH : at + 2 * HIGH]


def put_terms(terms_ref, c, values):
    large = values.astype(BF16).astype(F32)
    terms_ref[2 * c * NBLK : (2 * c + 1) * NBLK, :] = large
    terms_ref[(2 * c + 1) * NBLK : (2 * c + 2) * NBLK, :] = values - large


def put_sources(marked_ref, high_ref, low_ref):
    source = marked_ref[...]
    high = source >> 8
    high_ref[...] = high.astype(F32)
    low_ref[...] = (source - (high << 8)).astype(F32)


def source_normals_kernel(marked_ref, gain_ref, out_ref, terms_ref, high_ref, low_ref, *work):
    put_sources(marked_ref, high_ref, low_ref)
    gains = [gain_ref[NBLK * p : NBLK * p + NBLK, :] for p in range(5)]
    for at, (first, second) in enumerate(PAIR_LIST):
        put_terms(terms_ref, at, gains[first] * gains[second])
    source_sums(15, NBLK, terms_ref, high_ref, low_ref, out_ref, *work)


def source_right_kernel(
    reply_ref, slot_ref, obs_ref, marked_ref, gain_ref, out_ref, terms_ref, high_ref, low_ref, *work
):
    put_sources(marked_ref, high_ref, low_ref)
    place = indicator(iota_f((WINDOWS, NBLK), 0) == slot_ref[0:1, :])
    rank = slot_ref[1:2, :]
    spread = exact_dot(reply_ref[...].T, place, NN)
    knots = None
    for s in range(CAP):
        piece = jnp.where(rank == float(s), spread[16 * s : 16 * s + 16, :], 0.0)
        knots = piece if knots is None else knots + piece
    u = obs_ref[0:128, :]
    att = [obs_ref[256 + 128 * q : 384 + 128 * q, :] for q in range(4)]
    v = 1.0 - u
    u2, v2 = u * u, v * v
    cubes = [v2 * v, u * v2, u2 * v, u2 * u]
    values = obs_ref[128:256, :]
    for j in range(4):
        spline = None
        for i in range(4):
            if SPLINE[j, i] != 0.0:
                piece = float(SPLINE[j, i]) * cubes[i]
                spline = piece if spline is None else spline + piece
        inner = None
        for q in range(4):
            piece = att[q] * knots[4 * j + q : 4 * j + q + 1, :]
            inner = piece if inner is None else inner + piece
        values = values - spline * inner
    values = values.T
    for p in range(5):
        put_terms(terms_ref, p, gain_ref[NBLK * p : NBLK * p + NBLK, :] * values)
    source_sums(5, NBLK, terms_ref, high_ref, low_ref, out_ref, *work)


def factor_kernel(own_ref, other_ref, after_ref, out_ref):
    del after_ref
    entries = {}
    for at, pair in enumerate(PAIR_LIST):
        rows = slice(HIGH * at, HIGH * at + HIGH)
        total = own_ref[rows, :] + other_ref[rows, :]
        entries[pair] = total + SOURCE_PRIOR if pair[0] == pair[1] else total
    lower = {}
    for column in range(5):
        pivot = entries[column, column]
        for before in range(column):
            pivot = pivot - lower[column, before] * lower[column, before]
        inverse = 1.0 / jnp.sqrt(pivot)
        lower[column, column] = inverse
        for row in range(column + 1, 5):
            running = entries[column, row]
            for before in range(column):
                running = running - lower[row, before] * lower[column, before]
            lower[row, column] = running * inverse
    for at, (first, second) in enumerate(PAIR_LIST):
        out_ref[HIGH * at : HIGH * at + HIGH, :] = lower[second, first]


def solve_kernel(factor_ref, own_ref, one_ref, two_ref, three_ref, out_ref):
    lower = {}
    for at, (first, second) in enumerate(PAIR_LIST):
        lower[second, first] = factor_ref[HIGH * at : HIGH * at + HIGH, :]
    values = []
    for row in range(5):
        rows = slice(HIGH * row, HIGH * row + HIGH)
        running = (own_ref[rows, :] + two_ref[rows, :]) + (one_ref[rows, :] + three_ref[rows, :])
        for before in range(row):
            running = running - lower[row, before] * values[before]
        values.append(running * lower[row, row])
    for row in reversed(range(5)):
        running = values[row]
        for later in range(row + 1, 5):
            running = running - lower[later, row] * values[later]
        values[row] = running * lower[row, row]
    for row in range(5):
        for high in range(HIGH):
            out_ref[row : row + 1, LOW * high : LOW * high + LOW] = values[row][high : high + 1, :]


def f32(*shape):
    return jax.ShapeDtypeStruct(shape, F32)


def kernel_call(body, name, outs, *args, scratch=(), flops=1_000_000, far=(), grant=32, passed=None):
    passed = passed or {}
    place = [pl.ANY if at in far else pltpu.MemorySpace.VMEM for at in range(len(args))]
    out_place = [pl.ANY if at in passed.values() else pltpu.MemorySpace.VMEM for at in range(len(jax.tree.leaves(outs)))]
    out_specs = [pl.BlockSpec(memory_space=at) for at in out_place]
    size = sum(math.prod(a.shape) * 4 for a in args)
    return pl.pallas_call(
        body,
        out_shape=outs,
        in_specs=[pl.BlockSpec(memory_space=at) for at in place],
        out_specs=tuple(out_specs) if isinstance(outs, tuple) else out_specs[0],
        input_output_aliases=passed,
        scratch_shapes=list(scratch),
        compiler_params=pltpu.CompilerParams(vmem_limit_bytes=grant * 1024 * 1024),
        cost_estimate=pl.CostEstimate(flops=flops, bytes_accessed=size, transcendentals=0),
        name=name,
    )(*args)


def segment_scratch(count):
    return (
        pltpu.VMEM((2 * count * NBLK, ROWS), F32),
        pltpu.VMEM((NBLK, ROWS), F32),
        pltpu.VMEM((NBLK, ROWS), F32),
        pltpu.VMEM((LOW, 2 * count * HIGH), F32),
    )


def swapped(values, partner):
    return lax.ppermute(values, "ccd", list(enumerate(partner)))


def from_others(values):
    return [
        lax.ppermute(values, "ccd", [(at, (at + shift) % N_CCD) for at in range(N_CCD)]) for shift in range(1, N_CCD)
    ]


def to_windows(values):
    return lax.all_to_all(values, ("src", "win"), split_axis=0, concat_axis=0, tiled=True)


def local(block_bin, block_rows, row_source, obs_resid, obs_phase, att_partial, src_partial):
    bins = block_bin.reshape(1, NBLK)
    rows = block_rows.reshape(1, NBLK)
    gains = jnp.transpose(src_partial, (1, 0, 2)).reshape(5 * NBLK, ROWS)
    send, obs, slots, marked = kernel_call(
        normals_kernel,
        "normals",
        (f32(SLOTS, 128), f32(6 * ROWS, NBLK), f32(8, NBLK), jax.ShapeDtypeStruct((NBLK, ROWS), jnp.int32)),
        bins,
        rows,
        obs_phase,
        att_partial.reshape(4 * NBLK, ROWS),
        obs_resid,
        row_source,
        scratch=(
            pltpu.VMEM((1, NBLK), jnp.int32),
            pltpu.VMEM((1, NBLK), jnp.int32),
            pltpu.VMEM((NBLK, ROWS), F32),
            pltpu.VMEM((4 * NBLK, ROWS), F32),
            pltpu.VMEM((NBLK, ROWS), F32),
            pltpu.VMEM((NBLK, ROWS), jnp.int32),
            pltpu.VMEM((NBLK, NBLK), F32),
            pltpu.SemaphoreType.DMA((6,)),
        ),
        far=range(6),
        grant=56,
    )
    got = to_windows(send.reshape(WINDOWS, CAP, 128)).reshape(SLOTS, 128)
    normal = kernel_call(
        source_normals_kernel,
        "source_normals",
        f32(15 * HIGH, LOW),
        marked,
        gains,
        scratch=segment_scratch(15),
        flops=2 * 480 * 256 * 16384,
    )
    moments = kernel_call(bins_kernel, "bins", f32(FEATS, KNOTS_W), got, normal, far=(1,))
    attitude, reply, normal = kernel_call(
        attitude_kernel,
        "attitude",
        (f32(1, 4, KNOTS_W), f32(WINDOWS, 128), f32(15 * HIGH, LOW)),
        moments,
        *from_others(moments),
        got,
        jnp.asarray(knot_matrix()),
        normal,
        swapped(normal, (1, 0, 3, 2)),
    )
    other = swapped(normal, (3, 2, 1, 0))
    knots = to_windows(reply)
    right = kernel_call(
        source_right_kernel,
        "source_right",
        f32(5 * HIGH, LOW),
        knots,
        slots,
        obs,
        marked,
        gains,
        scratch=segment_scratch(5),
        flops=2 * 160 * 256 * 16384,
    )
    factors = kernel_call(factor_kernel, "factors", f32(15 * HIGH, LOW), normal, other, right, far=(2,))
    source_delta = kernel_call(solve_kernel, "solve", f32(5, SRC_DEV), factors, right, *from_others(right))
    return attitude, source_delta


def solution(mesh):
    return jax.shard_map(
        local,
        mesh=mesh,
        in_specs=(
            P(("src", "win", "ccd")),
            P(("src", "win", "ccd")),
            P(("src", "win", "ccd"), None),
            P(("src", "win", "ccd"), None),
            P(("src", "win", "ccd"), None),
            P(("src", "win", "ccd"), None, None),
            P(("src", "win", "ccd"), None, None),
        ),
        out_specs=(P(("src", "win"), None, None), P(None, ("src", "win"))),
        check_vma=False,
    )
```
